128 devices in a mesh: blk: 16 (over y, z), sub: 8 (over x, core).
Axes of the slice: x: 4, y: 4, z: 4, core: 2. Of those that a mesh axis runs over, the one named last changes fastest.
Arguments:
- fields: float32 [4, 216, 32768], P(None, None, ('blk', 'sub')), may hold values from -6 to 6
- metric: float32 [32768], P(('blk', 'sub')), may hold values from 1 to 3
- neighbours: int32 [6, 32768], P(None, ('blk', 'sub')), may hold values from -2 to 32767, as said below
- mortar_sends: int32 [3, 65536], P(None, ('blk', 'sub')), may hold values from -1 to 127, as said below
- mortar_pairs: int32 [2, 32768], P(None, ('blk', 'sub')), may hold values from -1 to 511, as said below
Outputs:
- advanced: float32 [4, 216, 32768], P(None, None, ('blk', 'sub'))
The draws below stay inside these ranges and needn't reach their ends.
Inputs may be any that keep to these rules, and one draw needn't show every extreme that they name: `neighbours`: element numbers run device by device, 256 to a device, devices blk-major. A neighbour across faces 0 and 1 lies on the same device or on the device before or after it along sub, across faces 2 and 3 on the same device or along blk, across faces 4 and 5 on the same device; an element named across face f names the first one back across face f xor 1. On each device and for each of faces 0 to 3, the elements whose neighbour lies on another device number 32, or zero where no device lies that way. Exactly 64 elements of each device have -2 on face 5 and 64 on face 4; -2 appears on no other face. `mortar_sends`: row 0 names one of the device's 2 * 64 interface faces, or -1 for an empty slot; rows 1 and 2 are 0 on empty slots and satisfy 0 <= lo < hi <= 16 on live ones. Device d's slots for owner o are the 4 columns from 2 * 256 d + 2 * 2 o on. Every interface face is named in exactly two live slots, whose intervals split [0, 16] in two. `mortar_pairs`: column 256 o + j is mortar slot j of owner o; both rows are -1 for an empty mortar slot. Every live send slot is named by exactly one mortar; the rotor entry names a slot carrying a rotor face, the stator entry one carrying a stator face, with intervals of equal length. Some owner has all 256 mortar slots live. The two slots of a mortar are partners; the live send slots of one device whose partners lie on one device (possibly itself) number at most 4, and some pair of devices has exactly 4.
All inputs are finite; a program needn't handle non-finite values.
Results may differ from the reference program's by a relative error of at most 0.00005.
Values sent between devices are 32-bit elements; how exact they have to be, the bound alone decides.
No kernel may reach another device: no remote copies, remote signals or barrier semaphores. Data moves between devices by JAX's collectives and lax.ppermute only.
A program may use at most 128 MiB of HBM per device.

```python
import math
import jax
import jax.numpy as jnp
import numpy as np
from jax import lax

P_SIZE = 6
NP = 216
EA = 8
EC = 4
SUB = 16
ET = 32768
N_BLK = 16
N_SUB = 8


def mortar_tables(key):
    devices = N_BLK * N_SUB
    cycle = EA * EA
    capacity = 4 * cycle
    tile = capacity // devices
    total = 2 * cycle * devices
    stream = jnp.arange(total, dtype=jnp.int32)
    holder = stream % devices
    row_step = stream // devices
    rotor_face = row_step // 2
    half_bit = row_step % 2
    ordering_shift = jax.random.permutation(jax.random.fold_in(key, 1), devices).astype(jnp.int32)
    face_ids_all = jnp.arange(cycle, dtype=jnp.int32)
    face_shift = (ordering_shift[face_ids_all % devices] - ordering_shift[0]) % devices
    stator_holder = ((holder + face_shift[rotor_face]) % devices).astype(jnp.int32)
    stator_face = (rotor_face + half_bit) % cycle
    slide = jax.random.randint(jax.random.fold_in(key, 2), (devices,), 1, SUB, dtype=jnp.int32)
    theta = slide[stator_holder]
    rotor_lo = jnp.where(half_bit == 0, 0, SUB - theta)
    rotor_hi = jnp.where(half_bit == 0, SUB - theta, SUB)
    stator_lo = jnp.where(half_bit == 0, theta, 0)
    stator_hi = jnp.where(half_bit == 0, SUB, theta)
    pattern = jnp.array([capacity, capacity // 2, capacity // 4, capacity // 4], jnp.int32)
    loads = pattern[jnp.arange(devices, dtype=jnp.int32) % 4]
    starts = jnp.cumsum(loads) - loads
    owner_order = jax.random.permutation(jax.random.fold_in(key, 3), devices).astype(jnp.int32)
    position = (jnp.searchsorted(starts, stream, side='right') - 1).astype(jnp.int32)
    owner = owner_order[position]
    owner_slot = stream - starts[position]
    source = jnp.concatenate([holder, stator_holder])
    target = jnp.concatenate([owner, owner])
    face_ids = jnp.concatenate([rotor_face, cycle + stator_face])
    lows = jnp.concatenate([rotor_lo, stator_lo])
    highs = jnp.concatenate([rotor_hi, stator_hi])
    sequence = jnp.concatenate([2 * stream, 2 * stream + 1])
    pair_key = source * devices + target
    order_key = pair_key * (2 * total) + sequence
    ordering = jnp.argsort(order_key)
    sorted_pairs = pair_key[ordering]
    first_seen = jnp.searchsorted(sorted_pairs, sorted_pairs, side='left').astype(jnp.int32)
    within = jnp.zeros((2 * total,), jnp.int32).at[ordering].set(jnp.arange(2 * total, dtype=jnp.int32) - first_seen)
    send_column = source * (2 * capacity) + target * (2 * tile) + within
    sends = jnp.zeros((3, devices * 2 * capacity), jnp.int32).at[0].set(-1)
    sends = sends.at[0, send_column].set(face_ids)
    sends = sends.at[1, send_column].set(lows)
    sends = sends.at[2, send_column].set(highs)
    received = source * (2 * tile) + within
    owner_column = owner * capacity + owner_slot
    pairs = jnp.full((2, devices * capacity), -1, jnp.int32)
    pairs = pairs.at[0, owner_column].set(received[:total])
    pairs = pairs.at[1, owner_column].set(received[total:])
    return (sends, pairs)


def draw_mortar_sends(key, part):
    tables = mortar_tables(key)
    return tables[0]


def draw_mortar_pairs(key, part):
    tables = mortar_tables(key)
    return tables[1]


def draw_neighbours(key, part):
    key = jax.random.fold_in(key, 11)
    devices = N_BLK * N_SUB
    per_device = EA * EA * EC
    orders = jax.vmap(lambda item: jax.random.permutation(item, per_device))(jax.random.split(key, devices)).astype(jnp.int32)
    places = jax.vmap(lambda ordering: jnp.zeros((per_device,), jnp.int32).at[ordering].set(jnp.arange(per_device, dtype=jnp.int32)))(orders)
    device = jnp.repeat(jnp.arange(devices, dtype=jnp.int32), per_device)
    cell = orders.reshape(-1)
    pos_a = cell // (EA * EC)
    pos_b = cell // EC % EA
    pos_c = cell % EC
    blk_pos = device // N_SUB
    sub_pos = device % N_SUB

    def locate(where_device, at_a, at_b, at_c):
        where_device = jnp.clip(where_device, 0, devices - 1)
        cell_index = (jnp.clip(at_a, 0, EA - 1) * EA + jnp.clip(at_b, 0, EA - 1)) * EC + jnp.clip(at_c, 0, EC - 1)
        return where_device * per_device + places[where_device, cell_index]
    face_zero = jnp.where(pos_a > 0, locate(device, pos_a - 1, pos_b, pos_c), jnp.where(sub_pos > 0, locate(device - 1, EA - 1 + 0 * pos_a, pos_b, pos_c), -1))
    face_one = jnp.where(pos_a < EA - 1, locate(device, pos_a + 1, pos_b, pos_c), jnp.where(sub_pos < N_SUB - 1, locate(device + 1, 0 * pos_a, pos_b, pos_c), -1))
    face_two = jnp.where(pos_b > 0, locate(device, pos_a, pos_b - 1, pos_c), jnp.where(blk_pos > 0, locate(device - N_SUB, pos_a, EA - 1 + 0 * pos_b, pos_c), -1))
    face_three = jnp.where(pos_b < EA - 1, locate(device, pos_a, pos_b + 1, pos_c), jnp.where(blk_pos < N_BLK - 1, locate(device + N_SUB, pos_a, 0 * pos_b, pos_c), -1))
    face_four = jnp.where(pos_c == EC // 2, -2, jnp.where(pos_c == 0, -1, locate(device, pos_a, pos_b, pos_c - 1)))
    face_five = jnp.where(pos_c == EC // 2 - 1, -2, jnp.where(pos_c == EC - 1, -1, locate(device, pos_a, pos_b, pos_c + 1)))
    return jnp.stack([face_zero, face_one, face_two, face_three, face_four, face_five]).astype(jnp.int32)


def block_scale(key, shape, pieces, low, high):
    loudness, own = 1.0, jax.random.fold_in(key, 6)
    for axis_at, blocks in pieces:
        heights = jnp.exp(jax.random.uniform(jax.random.fold_in(own, axis_at), (blocks,), jnp.float32, low / len(pieces), high / len(pieces)))
        loudness = loudness * jnp.repeat(heights, shape[axis_at] // blocks).reshape([-1 if axis == axis_at else 1 for axis in range(len(shape))])
    return loudness


def bell_draw(stream_key, shape, spread, limit, pieces=(), kind=jnp.bfloat16):
    result = spread * jax.random.normal(stream_key, shape, jnp.float32)
    if pieces:
        result = result * block_scale(stream_key, shape, pieces, -0.22, 0.18)
    return jnp.clip(result, -limit, limit).astype(kind)


def setup_inputs(seed: int = 0) -> dict:
    seeds = jax.random.split(jax.random.key(seed), 6)
    fields = bell_draw(seeds[0], (4, NP, ET), 1.0, 6.0, ((2, 128),), jnp.float32)
    metric = jnp.clip(jnp.exp(math.log(3.0) - 1.0986123 * jax.random.uniform(seeds[1], (ET,), jnp.float32) ** block_scale(seeds[1], (ET,), ((0, 128),), -0.2, 0.2)), 1.0, 3.0)
    neighbours = draw_neighbours(jax.random.fold_in(seeds[5], 71), 0)
    mortar_sends = draw_mortar_sends(jax.random.fold_in(seeds[5], 71), 0)
    mortar_pairs = draw_mortar_pairs(jax.random.fold_in(seeds[5], 71), 0)
    return {"fields": fields, "metric": metric, "neighbours": neighbours, "mortar_sends": mortar_sends, "mortar_pairs": mortar_pairs}


DT_STEP = 0.01


def legendre_columns(points, npts):
    legendre = np.zeros((npts, npts))
    legendre[:, 0] = 1.0
    legendre[:, 1] = points
    for k in range(2, npts):
        legendre[:, k] = ((2 * k - 1) * points * legendre[:, k - 1] - (k - 1) * legendre[:, k - 2]) / k
    return legendre


def basis_tables(npts):
    order = npts - 1
    points = -np.cos(np.pi * np.arange(npts) / order)
    for iteration in range(60):
        legendre = legendre_columns(points, npts)
        points = points - (points * legendre[:, order] - legendre[:, order - 1]) / (npts * legendre[:, order])
    legendre = legendre_columns(points, npts)
    weights = 2.0 / (order * npts * legendre[:, order] ** 2)
    separation = points[:, None] - points[None, :] + np.eye(npts)
    derivative = (legendre[:, order][:, None] / legendre[:, order][None, :]) / separation
    derivative = derivative * (1.0 - np.eye(npts))
    derivative[0, 0] = -order * npts / 4.0
    derivative[order, order] = order * npts / 4.0
    return points, weights, derivative


def volume_operators(npts):
    points, weights, derivative = basis_tables(npts)
    single = np.eye(npts)
    square = np.eye(npts * npts)
    along_a = np.kron(derivative, square)
    along_b = np.kron(single, np.kron(derivative, single))
    along_c = np.kron(square, derivative)
    stacked = np.concatenate([along_a, along_b, along_c], axis=0)
    joined = np.concatenate([along_a, along_b, along_c], axis=1)
    return stacked, joined


def face_trace(field_cube, face_index):
    spot = 0 if face_index % 2 == 0 else field_cube.shape[1] - 1
    return lax.index_in_dim(field_cube, spot, 1 + face_index // 2, keepdims=False)


def place_face(surface, values, face_index):
    spot = 0 if face_index % 2 == 0 else surface.shape[1] - 1
    selector = [slice(None)] * 5
    selector[1 + face_index // 2] = spot
    return surface.at[tuple(selector)].add(values)


def normal_flux(trace, face_index):
    along = face_index // 2
    orient = 1.0 if face_index % 2 == 1 else -1.0
    blank = jnp.zeros_like(trace[0])
    parts = [blank, blank, blank, blank]
    parts[0] = orient * trace[1 + along]
    parts[1 + along] = orient * trace[0]
    return jnp.stack(parts)


def face_term(inside, outside, face_index):
    return 0.5 * (normal_flux(inside, face_index) - normal_flux(outside, face_index)) - 0.5 * (inside - outside)


def lagrange_rows(points, targets):
    rows_out = []
    for i in range(len(points)):
        product = jnp.ones_like(targets)
        for j in range(len(points)):
            if j != i:
                product = product * (targets - float(points[j])) / float(points[i] - points[j])
        rows_out.append(product)
    return jnp.stack(rows_out)


def mortar_points(points, lower, upper):
    unit = (jnp.asarray(points, jnp.float32)[:, None] + 1.0) * 0.5
    spots = lower[None, :] + (upper - lower)[None, :] * unit
    return spots * (2.0 / SUB) - 1.0


def to_mortar(flat, lower, upper, points):
    npts = len(points)
    slots = flat.shape[1]
    grid = flat.reshape(4, npts, npts, slots)
    basis = lagrange_rows(points, mortar_points(points, lower, upper))
    moved = jnp.einsum("ims,civs->cmvs", basis, grid, precision=lax.Precision.HIGHEST)
    return moved.reshape(4 * npts * npts, slots)


def from_mortar(flat, lower, upper, points, weights):
    npts = len(points)
    slots = flat.shape[1]
    grid = flat.reshape(4, npts, npts, slots)
    basis = lagrange_rows(points, mortar_points(points, lower, upper))
    scale = jnp.asarray(weights, jnp.float32)[:, None] * ((upper - lower) / SUB)[None, :]
    moved = jnp.einsum("ims,cmvs->civs", basis * scale[None], grid, precision=lax.Precision.HIGHEST)
    moved = moved / jnp.asarray(weights, jnp.float32)[None, :, None, None]
    return moved.reshape(4 * npts * npts, slots)


def mortar_flux(rotor_vals, stator_vals):
    cols = rotor_vals.shape[1]
    rotor_grid = rotor_vals.reshape(4, -1, cols)
    stator_grid = stator_vals.reshape(4, -1, cols)
    half_jump = 0.5 * (normal_flux(rotor_grid, 5) - normal_flux(stator_grid, 5))
    half_gap = 0.5 * (rotor_grid - stator_grid)
    return (half_jump - half_gap).reshape(-1, cols), (half_jump + half_gap).reshape(-1, cols)


def reference(fields, metric, neighbours, mortar_sends, mortar_pairs):
    points, weights, derivative = basis_tables(P_SIZE)
    stacked_np, joined_np = volume_operators(P_SIZE)
    stacked = jnp.asarray(stacked_np, jnp.float32)
    joined = jnp.asarray(joined_np, jnp.float32)
    lift_scale = 1.0 / float(weights[0])
    devices = N_BLK * N_SUB
    elem_count = EA * EA * EC
    total_elems = devices * elem_count
    node_count = P_SIZE ** 3
    row_count = 4 * P_SIZE * P_SIZE
    cycle = EA * EA
    capacity = 4 * cycle
    tile_pair = 2 * capacity // devices
    slot_total = devices * 2 * capacity
    local_ids = jnp.arange(elem_count, dtype=jnp.int32)
    offsets = (jnp.arange(devices, dtype=jnp.int32) * elem_count)[:, None]

    def cycle_members(flags):
        ordering = jnp.where(flags.reshape(devices, elem_count), local_ids[None, :], elem_count + local_ids[None, :])
        chosen = jnp.argsort(ordering, axis=1)[:, :cycle].astype(jnp.int32)
        return (chosen + offsets).reshape(-1)

    rotor_elems = cycle_members(neighbours[5] == -2)
    stator_elems = cycle_members(neighbours[4] == -2)
    slot_device = jnp.arange(slot_total, dtype=jnp.int32) // (2 * capacity)
    send_face = mortar_sends[0]
    send_live = (send_face >= 0).astype(jnp.float32)
    global_face = (slot_device * (2 * cycle) + jnp.maximum(send_face, 0)).astype(jnp.int32)
    send_lo = mortar_sends[1].astype(jnp.float32)
    send_hi = mortar_sends[2].astype(jnp.float32)
    owner_ids = jnp.arange(devices * capacity, dtype=jnp.int32) // capacity

    def global_slot(entry):
        entry = jnp.maximum(entry, 0)
        return ((entry // tile_pair) * (2 * capacity) + owner_ids * tile_pair + entry % tile_pair).astype(jnp.int32)

    pair_live = mortar_pairs[0] >= 0
    rotor_slot = global_slot(mortar_pairs[0])
    stator_slot = global_slot(mortar_pairs[1])
    rotor_put = jnp.where(pair_live, rotor_slot, slot_total)
    stator_put = jnp.where(pair_live, stator_slot, slot_total)
    face_segment = jnp.where(send_face >= 0, global_face, devices * 2 * cycle)

    def interface_terms(face_low, face_high):
        rotor_tr = jnp.take(face_high, rotor_elems, axis=1).reshape(row_count, devices, cycle)
        stator_tr = jnp.take(face_low, stator_elems, axis=1).reshape(row_count, devices, cycle)
        both = jnp.concatenate([rotor_tr, stator_tr], axis=2).reshape(row_count, devices * 2 * cycle)
        sent = jnp.take(both, global_face, axis=1) * send_live[None, :]
        mortar_vals = to_mortar(sent, send_lo, send_hi, points)
        rotor_flux, stator_flux = mortar_flux(jnp.take(mortar_vals, rotor_slot, axis=1), jnp.take(mortar_vals, stator_slot, axis=1))
        gathered = jnp.zeros((row_count, slot_total), jnp.float32)
        gathered = gathered.at[:, rotor_put].set(rotor_flux, mode="drop")
        gathered = gathered.at[:, stator_put].set(stator_flux, mode="drop")
        returned = from_mortar(gathered, send_lo, send_hi, points, weights)
        per_face = jax.ops.segment_sum(returned.T, face_segment, num_segments=devices * 2 * cycle + 1)[:-1].T
        per_face = per_face.reshape(row_count, devices, 2, cycle)
        return per_face[:, :, 0].reshape(row_count, -1), per_face[:, :, 1].reshape(row_count, -1)

    def time_rates(current):
        field_cube = current.reshape(4, P_SIZE, P_SIZE, P_SIZE, total_elems)
        traces = [face_trace(field_cube, f).reshape(row_count, total_elems) for f in range(6)]
        rotor_part, stator_part = interface_terms(traces[4], traces[5])
        gradient = jnp.dot(stacked, current[0], precision=lax.Precision.HIGHEST).reshape(3, node_count, total_elems)
        divergence = jnp.dot(joined, current[1:].reshape(3 * node_count, total_elems), precision=lax.Precision.HIGHEST)
        surface = jnp.zeros((4, P_SIZE, P_SIZE, P_SIZE, total_elems), jnp.float32)
        for face_index in range(6):
            target = neighbours[face_index]
            outside = jnp.take(traces[face_index ^ 1], jnp.maximum(target, 0), axis=1) * (target >= 0).astype(jnp.float32)[None, :]
            term = face_term(traces[face_index].reshape(4, P_SIZE, P_SIZE, total_elems), outside.reshape(4, P_SIZE, P_SIZE, total_elems), face_index)
            if face_index >= 4:
                term = jnp.where(target == -2, 0.0, term)
            surface = place_face(surface, term, face_index)
        surface = surface.at[:, :, :, P_SIZE - 1, rotor_elems].add(rotor_part.reshape(4, P_SIZE, P_SIZE, -1))
        surface = surface.at[:, :, :, 0, stator_elems].add(stator_part.reshape(4, P_SIZE, P_SIZE, -1))
        volume = jnp.concatenate([divergence[None], gradient], axis=0)
        return metric * (lift_scale * surface.reshape(4, node_count, total_elems) - volume)

    first_section = fields + DT_STEP * time_rates(fields)
    second_section = 0.75 * fields + 0.25 * (first_section + DT_STEP * time_rates(first_section))
    return fields / 3.0 + (2.0 / 3.0) * (second_section + DT_STEP * time_rates(second_section))
```

```python
import jax
import jax.numpy as jnp
import numpy as np
from jax import lax
from jax.experimental import pallas as pl
from jax.experimental.pallas import tpu as pltpu
from jax.sharding import PartitionSpec as P

P_SIZE = 6
SUB = 16
IFD = 64
RIM = 32
NODES = 216
ELEMS = 256
FACES = 2 * IFD
SLOTS = 512
DEVICES = 128
TR = 40
FEAT = 128
DT_STEP = 0.01
F32 = jnp.float32
BF16 = jnp.bfloat16
VMEM_BYTES = 40 * 1024 * 1024


def legendre_columns(points, npts):
    legendre = np.zeros((npts, npts))
    legendre[:, 0] = 1.0
    legendre[:, 1] = points
    for k in range(2, npts):
        legendre[:, k] = (
            (2 * k - 1) * points * legendre[:, k - 1] - (k - 1) * legendre[:, k - 2]
        ) / k
    return legendre


def basis_tables(npts):
    order = npts - 1
    points = -np.cos(np.pi * np.arange(npts) / order)
    for iteration in range(60):
        legendre = legendre_columns(points, npts)
        points = points - (points * legendre[:, order] - legendre[:, order - 1]) / (
            npts * legendre[:, order]
        )
    legendre = legendre_columns(points, npts)
    weights = 2.0 / (order * npts * legendre[:, order] ** 2)
    separation = points[:, None] - points[None, :] + np.eye(npts)
    derivative = legendre[:, order][:, None] / legendre[:, order][None, :] / separation
    derivative = derivative * (1.0 - np.eye(npts))
    derivative[0, 0] = -order * npts / 4.0
    derivative[order, order] = order * npts / 4.0
    return (points, weights, derivative)


POINTS, WEIGHTS, DERIVATIVE = basis_tables(P_SIZE)
LIFT = float(1.0 / WEIGHTS[0])
SECTIONS = (
    (0.0, 1.0, DT_STEP),
    (0.75, 0.25, 0.25 * DT_STEP),
    (1.0 / 3.0, 2.0 / 3.0, 2.0 / 3.0 * DT_STEP),
)


def face_rows():
    picks = np.zeros((6 * TR, NODES))
    for face in range(6):
        fixed = 0 if face % 2 == 0 else P_SIZE - 1
        for a in range(P_SIZE):
            for b in range(P_SIZE):
                place = [a, b]
                place.insert(face // 2, fixed)
                node = (place[0] * P_SIZE + place[1]) * P_SIZE + place[2]
                picks[face * TR + a * P_SIZE + b, node] = 1.0
    return picks


def derivative_pieces():
    one = np.eye(P_SIZE)
    square = np.eye(P_SIZE * P_SIZE)
    whole = [
        np.kron(DERIVATIVE, square),
        np.kron(one, np.kron(DERIVATIVE, one)),
        np.kron(square, DERIVATIVE),
    ]
    pieces = []
    for matrix in whole:
        matrix = matrix.astype(np.float32)
        high = matrix.astype(jnp.bfloat16)
        pieces.append(high)
        pieces.append((matrix - high.astype(np.float32)).astype(jnp.bfloat16))
    return np.stack(pieces)


def nn(a, b):
    return lax.dot_general(a, b, (((1,), (0,)), ((), ())), preferred_element_type=F32)


def nt(a, b):
    return lax.dot_general(a, b, (((1,), (1,)), ((), ())), preferred_element_type=F32)


def tn(a, b):
    return lax.dot_general(a, b, (((0,), (0,)), ((), ())), preferred_element_type=F32)


def halves(x):
    high = x.astype(BF16)
    return high, (x - high.astype(F32)).astype(BF16)


def nn2(exact, x):
    high, low = halves(x)
    return nn(exact, high) + nn(exact, low)


def mark(cond):
    return jnp.where(cond, 1.0, 0.0)


def iota(shape, dim):
    return lax.broadcasted_iota(jnp.int32, shape, dim)


def my_device():
    return lax.axis_index("blk") * 8 + lax.axis_index("sub")


def call(body, outs, args, scratch=(), flops=1e8, moved=2e6):
    return pl.pallas_call(
        body,
        out_shape=[jax.ShapeDtypeStruct(s, d) for s, d in outs],
        in_specs=[pl.BlockSpec(memory_space=pltpu.VMEM)] * len(args),
        out_specs=[pl.BlockSpec(memory_space=pltpu.VMEM)] * len(outs),
        scratch_shapes=list(scratch),
        compiler_params=pltpu.CompilerParams(vmem_limit_bytes=VMEM_BYTES),
        cost_estimate=pl.CostEstimate(
            flops=int(flops), bytes_accessed=int(moved), transcendentals=0
        ),
    )(*args)


def spread(values, pad, width):
    for group in range(3 * P_SIZE):
        c, i = divmod(group, P_SIZE)
        start = c * TR + i * P_SIZE
        pad[group, 0:P_SIZE, 0:width] = values[start : start + P_SIZE, :]


def to_mortars(basis, pad, out, comps, add):
    for half in range(2):
        lanes = slice(half * FACES, (half + 1) * FACES)
        for c in comps:
            for m in range(P_SIZE):
                total = basis[0, m : m + 1, lanes] * pad[c * P_SIZE, :, 0:FACES]
                for i in range(1, P_SIZE):
                    total += basis[i, m : m + 1, lanes] * pad[c * P_SIZE + i, :, 0:FACES]
                start = c * TR + m * P_SIZE
                rows = slice(start, start + P_SIZE)
                if add:
                    out[rows, lanes] += total[0:P_SIZE, :]
                else:
                    out[rows, lanes] = total[0:P_SIZE, :]


def outgoing(traces4, traces5):
    blank = jnp.zeros((FEAT - 3 * TR, ELEMS), F32)
    out4 = jnp.concatenate([traces4[0] - traces4[3], traces4[1], traces4[2], blank], axis=0)
    out5 = jnp.concatenate([traces5[0] + traces5[3], traces5[1], traces5[2], blank], axis=0)
    return out4, out5


def at_faces(rows4, rows5, members):
    high5, low5 = halves(rows5)
    high4, low4 = halves(rows4)
    rotor = nt(high5, members) + nt(low5, members)
    stator = nt(high4, members) + nt(low4, members)
    return jnp.where(iota((FEAT, FACES), 1) < IFD, rotor, stator)


def at_elements(values, members):
    rotor_side = iota((FEAT, FACES), 1) < IFD
    to5 = nn2b(jnp.where(rotor_side, values, 0.0), members)
    to4 = nn2b(jnp.where(rotor_side, 0.0, values), members)
    return to4, to5


def nn2b(x, exact):
    high, low = halves(x)
    return nn(high, exact) + nn(low, exact)


def comp(rows, c):
    return rows[c * TR : (c + 1) * TR, :]


def partner_body(pairs, out):
    row = iota((DEVICES, ELEMS), 0)
    total = None
    for mine, other in ((0, 1), (1, 0)):
        entry = pairs[mine : mine + 1, :]
        partner = pairs[other : other + 1, :]
        owner_row = mark(row == (entry >> 2)).astype(BF16)
        spot = entry & 3
        facts = jnp.where(row == spot, (partner >> 2) + 1, 0) + jnp.where(
            row == spot + 4, partner & 3, 0
        )
        term = nt(owner_row, facts.astype(F32).astype(BF16))
        total = term if total is None else total + term
    out[...] = total


def tables_body(
    neighbours, sends, metric, fields, sel45,
    local, rim_out, rim_in, members, basis, project, own, info, face_metric, mortars,
    rows, pad,
):
    me = my_device()
    nb = neighbours[...]
    face_id = iota(nb.shape, 0)
    remote = (nb >= 0) & ((nb >> 8) != me)
    here = (nb >= 0) & ((nb >> 8) == me)
    spot = nb & 255
    flags = jnp.where(face_id < 4, mark(remote), mark(nb == -2))
    rows[...] = jnp.zeros(rows.shape, F32)
    rows[0, 0:6, :] = flags
    rows[1, 0:6, :] = spot.astype(F32)
    flag_rows = rows[0].astype(BF16)
    spot_rows = rows[1].astype(BF16)
    down = iota((ELEMS, ELEMS), 0)
    across = iota((ELEMS, ELEMS), 1)
    before = mark(down < across).astype(BF16)
    same = mark(down == across).astype(BF16)
    rank = nn(flag_rows, before)
    spot_down = jnp.where(nt(same, flag_rows) > 0.5, nt(same, spot_rows), 1e4)
    key = jnp.where(here, spot, -1)
    for face in range(6):
        local[face] = mark(down == key[face : face + 1, :]).astype(BF16)
    slot = iota((RIM, ELEMS), 0).astype(F32)
    for face in range(4):
        live = flags[face : face + 1, :] > 0.5
        order = jnp.sum(
            mark(spot_down[:, face : face + 1] < rows[1, face : face + 1, :]),
            axis=0,
            keepdims=True,
        )
        lines = slice(face * RIM, (face + 1) * RIM)
        rim_out[lines, :] = mark((slot == rank[face : face + 1, :]) & live).astype(BF16)
        rim_in[lines, :] = mark((slot == order) & live).astype(BF16)
    number = iota((FACES, ELEMS), 0)
    wanted = number.astype(F32)
    rotor = (wanted == rank[5:6, :]) & (flags[5:6, :] > 0.5)
    stator = (wanted - IFD == rank[4:5, :]) & (flags[4:5, :] > 0.5)
    member = jnp.where(number < IFD, mark(rotor), mark(stator)).astype(BF16)
    members[...] = member
    face_of = sends[0:1, :]
    lo_of = sends[1:2, :]
    lane_of = jnp.where(face_of >= 0, face_of + jnp.where(lo_of > 0, FACES, 0), -1)
    slot_lane = mark(iota((2 * FACES, SLOTS), 0) == lane_of).astype(BF16)
    kind = iota((16, SLOTS), 0)
    number = iota((16, SLOTS), 1)
    facts = jnp.where(kind == 0, number >> 2, 0) + jnp.where(kind == 1, number & 3, 0)
    facts += jnp.where(kind == 2, lo_of, 0) + jnp.where(kind == 3, sends[2:3, :], 0)
    found = nt(facts.astype(F32).astype(BF16), slot_lane)
    info[...] = found
    lo = found[2:3, :]
    width = found[3:4, :] - lo
    point = iota((8, 2 * FACES), 0)
    unit = jnp.zeros((8, 2 * FACES), F32)
    weight = jnp.zeros((8, 2 * FACES), F32)
    for m in range(P_SIZE):
        unit = jnp.where(point == m, float((POINTS[m] + 1.0) * 0.5), unit)
        weight = jnp.where(point == m, float(0.5 * WEIGHTS[m] / SUB), weight)
    spots = (lo + width * unit) * (2.0 / SUB) - 1.0
    for i in range(P_SIZE):
        product = None
        for j in range(P_SIZE):
            if j != i:
                term = (spots - float(POINTS[j])) * float(1.0 / (POINTS[i] - POINTS[j]))
                product = term if product is None else product * term
        basis[i] = product
        project[i] = product * weight * width * float(1.0 / WEIGHTS[i])
    for i in range(P_SIZE):
        for k in range(P_SIZE):
            term = jnp.sum(project[i] * basis[k], axis=0, keepdims=True)
            own[i, k : k + 1, :] = term[:, 0:FACES] + term[:, FACES:]
    scale = jnp.broadcast_to(metric[...], (16, ELEMS))
    high, rest = scale.astype(BF16), scale - scale.astype(BF16).astype(F32)
    middle, low = halves(rest)
    face_metric[...] = nt(high, member) + nt(middle, member) + nt(low, member)
    traces = [nn2(sel45[...], fields[c]) for c in range(4)]
    out4, out5 = outgoing([t[:TR] for t in traces], [t[TR:] for t in traces])
    spread(at_faces(out4, out5, member), pad, FACES)
    mortars[...] = jnp.zeros(mortars.shape, F32)
    to_mortars(basis, pad, mortars, (0, 1, 2), False)


def send_rows(exact, values):
    high, low = halves(values)
    return nt(exact, high) + nt(exact, low)


def route_body(facts, info, mortars, send, receive, payload):
    owner = info[0:1, :]
    turn = info[1:2, :]
    owner_pick = mark(iota((DEVICES, 2 * FACES), 0).astype(F32) == owner).astype(BF16)
    found = tn(facts[...].astype(BF16), owner_pick)
    partner = jnp.zeros((1, 2 * FACES), F32)
    other = jnp.zeros((1, 2 * FACES), F32)
    for t in range(4):
        partner = jnp.where(turn == t, found[t : t + 1, :], partner)
        other = jnp.where(turn == t, found[4 + t : 5 + t, :], other)
    partner = partner - 1.0
    kind = iota((16, 2 * FACES), 0)
    lines = jnp.where(kind == 0, partner, 0.0) + jnp.where(kind == 1, owner, 0.0)
    lines += jnp.where(kind == 2, turn, 0.0) + jnp.where(kind == 3, other, 0.0)
    same = mark(iota((2 * FACES, 2 * FACES), 0) == iota((2 * FACES, 2 * FACES), 1)).astype(BF16)
    down = nt(same, lines.astype(BF16))
    partner_down = down[:, 0:1]
    together = partner_down == partner
    mine_down = down[:, 1:2] * 4.0 + down[:, 2:3]
    theirs_down = down[:, 1:2] * 4.0 + down[:, 3:4]
    mine = owner * 4.0 + turn
    theirs = owner * 4.0 + other
    ahead = jnp.sum(mark(together & (mine_down < mine)), axis=0, keepdims=True)
    behind = jnp.sum(mark(together & (theirs_down < theirs)), axis=0, keepdims=True)
    place = iota((SLOTS, 2 * FACES), 0).astype(F32)
    sending = mark(place == partner * 4.0 + ahead).astype(BF16)
    send[...] = sending
    receive[...] = mark(place == partner * 4.0 + behind).astype(BF16)
    payload[...] = send_rows(sending, mortars[...])


def place_interface(part, arrived, members, place45):
    to4, to5 = at_elements(arrived[...], members[...])
    result = []
    for c in range(4):
        source = (0, 1, 2, 0)[c]
        sign5 = -1.0 if c == 3 else 1.0
        stack = jnp.concatenate([comp(to4, source), sign5 * comp(to5, source)], axis=0)
        result.append(part[c] + nn2(place45[...], stack))
    return result


def inner_body(section, *refs):
    if section == 0:
        part, refs = refs[0], refs[1:]
        first = part
        arrived = None
    else:
        part, first, arrived, place45 = refs[:4]
        refs = refs[4:]
    (members, local, rim_out, own, metric, neighbours, derive, select, place) = refs[:9]
    rims = refs[9:13]
    after, pad, mixed = refs[13:]
    keep, stay, rate = SECTIONS[section]
    if section == 0:
        fields = [part[c] for c in range(4)]
    else:
        fields = place_interface(part, arrived, members, place45)
    high, low = zip(*[halves(x) for x in fields])
    sel = select[...]
    traces = [nn(sel, high[c]) + nn(sel, low[c]) for c in range(4)]
    blank = jnp.zeros((FEAT - 3 * TR, ELEMS), F32)
    leaving, inside = [], []
    for face in range(6):
        sign = 1.0 if face % 2 else -1.0
        cut = [t[face * TR : (face + 1) * TR, :] for t in traces]
        along = face // 2
        tangent = [cut[1 + c] for c in range(3) if c != along]
        normal = sign * cut[1 + along]
        leaving.append(jnp.concatenate([cut[0] + normal] + tangent + [blank], axis=0))
        inside.append(jnp.concatenate([cut[0] - normal] + tangent + [blank], axis=0))
    leaving = [halves(x) for x in leaving]
    for face in range(4):
        pick = rim_out[face * RIM : (face + 1) * RIM, :]
        rims[face][...] = nt(pick, leaving[face][0]) + nt(pick, leaving[face][1])
    spread(at_faces(inside[4], inside[5], members[...]), pad, FACES)
    mixed[...] = jnp.zeros(mixed.shape, F32)
    for c in range(3):
        for i in range(P_SIZE):
            total = own[i, 0:1, :] * pad[c * P_SIZE]
            for k in range(1, P_SIZE):
                total += own[i, k : k + 1, :] * pad[c * P_SIZE + k]
            start = c * TR + i * P_SIZE
            mixed[start : start + P_SIZE, :] = -total[0:P_SIZE, :]
    to4, to5 = at_elements(mixed[...], members[...])
    terms = []
    for face in range(6):
        pick = local[face]
        arriving = nn(leaving[face ^ 1][0], pick) + nn(leaving[face ^ 1][1], pick)
        term = 0.5 * (arriving - inside[face])
        if face >= 4:
            term = jnp.where(neighbours[face : face + 1, :] == -2, 0.0, term)
            term = term + (to4, to5)[face - 4]
        terms.append(term)
    scale = metric[...] * rate
    for c in range(4):
        pieces = []
        for face in range(6):
            along = face // 2
            if c == 0:
                pieces.append(comp(terms[face], 0))
            elif c == 1 + along:
                pieces.append((-1.0 if face % 2 else 1.0) * comp(terms[face], 0))
            else:
                tangents = [k for k in range(3) if k != along]
                pieces.append(comp(terms[face], 1 + tangents.index(c - 1)))
        surface = nn2(place[...], jnp.concatenate(pieces, axis=0))
        if c == 0:
            pairs = ((0, 1), (1, 2), (2, 3))
        else:
            pairs = ((c - 1, 0),)
        volume = None
        for direction, source in pairs:
            big, small = derive[2 * direction], derive[2 * direction + 1]
            term = nn(big, high[source]) + nn(big, low[source]) + nn(small, high[source])
            volume = term if volume is None else volume + term
        base = stay * fields[c]
        if keep:
            base = base + keep * first[c]
        after[c] = base + scale * (LIFT * surface - volume)


def rim_body(section, *refs):
    before, r0, r1, r2, r3, rim_in, metric, place03 = refs[:8]
    last = section == 2
    if last:
        (after,) = refs[8:]
    else:
        members, basis, sel45, after, mortars, pad = refs[8:]
    scale = metric[...] * (SECTIONS[section][2] * LIFT)
    terms = []
    for face, ref in enumerate((r0, r1, r2, r3)):
        high, low = halves(ref[...])
        pick = rim_in[face * RIM : (face + 1) * RIM, :]
        terms.append(0.5 * (tn(high, pick) + tn(low, pick)))
    fields = []
    for c in range(4):
        pieces = []
        for face in range(4):
            along = face // 2
            if c == 0:
                pieces.append(comp(terms[face], 0))
            elif c == 1 + along:
                pieces.append((-1.0 if face % 2 else 1.0) * comp(terms[face], 0))
            else:
                tangents = [k for k in range(3) if k != along]
                pieces.append(comp(terms[face], 1 + tangents.index(c - 1)))
        value = before[c] + scale * nn2(place03[...], jnp.concatenate(pieces, axis=0))
        after[c] = value
        fields.append(value)
    if not last:
        traces = [nn2(sel45[...], x) for x in fields]
        out4, out5 = outgoing([t[:TR] for t in traces], [t[TR:] for t in traces])
        spread(at_faces(out4, out5, members[...]), pad, FACES)
        mortars[...] = jnp.zeros(mortars.shape, F32)
        to_mortars(basis, pad, mortars, (0, 1, 2), False)


def arrive(section, arrivals, receive, project, face_metric, pad, wide, out):
    high, low = halves(arrivals[...])
    pick = receive[...]
    spread(tn(high, pick) + tn(low, pick), wide, 2 * FACES)
    scale = face_metric[0:1, :] * (SECTIONS[section][2] * LIFT)
    out[...] = jnp.zeros(out.shape, F32)
    for c in range(3):
        for i in range(P_SIZE):
            total = None
            for half in range(2):
                lanes = slice(half * FACES, (half + 1) * FACES)
                for m in range(P_SIZE):
                    term = project[i, m : m + 1, lanes] * wide[c * P_SIZE + m, :, lanes]
                    total = term if total is None else total + term
            total = total * scale
            pad[c * P_SIZE + i] = total
            start = c * TR + i * P_SIZE
            out[start : start + P_SIZE, :] = total[0:P_SIZE, :]


def flux_body(
    section, arrivals, receive, send, project, basis, face_metric, mortars,
    arrived, payload, pad, wide, mixed,
):
    arrive(section, arrivals, receive, project, face_metric, pad, wide, arrived)
    mixed[...] = mortars[...]
    to_mortars(basis, pad, mixed, (1, 2), True)
    payload[...] = send_rows(send[...], mixed[...])


def last_body(
    arrivals, receive, project, face_metric, part, members, place45, after, pad, wide, arrived
):
    arrive(2, arrivals, receive, project, face_metric, pad, wide, arrived)
    result = place_interface(part, arrived, members, place45)
    for c in range(4):
        after[c] = result[c]


def exchange(rows, width):
    whole = rows.reshape(DEVICES, width, FEAT)
    moved = lax.all_to_all(whole, ("blk", "sub"), split_axis=0, concat_axis=0, tiled=True)
    return moved.reshape(DEVICES * width, FEAT)


def pass_rims(rims):
    arrived = []
    for face in range(4):
        axis = ("sub", "blk")[face // 2]
        count = lax.axis_size(axis)
        step = -1 if face % 2 else 1
        pairs = [(i, i + step) for i in range(count) if 0 <= i + step < count]
        arrived.append(lax.ppermute(rims[face ^ 1], axis, pairs))
    return arrived


def bind(body, section):
    def bound(*refs):
        body(section, *refs)

    return bound


def per_device(fields, metric, neighbours, mortar_sends, mortar_pairs):
    picks = face_rows()
    select = jnp.asarray(picks, BF16)
    sel45 = jnp.asarray(picks[4 * TR :], BF16)
    place = jnp.asarray(picks.T, BF16)
    place03 = jnp.asarray(picks[: 4 * TR].T, BF16)
    place45 = jnp.asarray(picks[4 * TR :].T, BF16)
    derive = jnp.asarray(derivative_pieces())
    metric = metric.reshape(1, ELEMS)
    whole = ((4, NODES, ELEMS), F32)
    rim = ((RIM, FEAT), F32)
    pad = pltpu.VMEM((3 * P_SIZE, 8, FACES), F32)
    wide = pltpu.VMEM((3 * P_SIZE, 8, 2 * FACES), F32)
    narrow = pltpu.VMEM((FEAT, FACES), F32)
    broad = pltpu.VMEM((FEAT, 2 * FACES), F32)

    (facts,) = call(partner_body, [((DEVICES, FEAT), F32)], (mortar_pairs,))
    facts = exchange(facts, 1)
    local, rim_out, rim_in, members, basis, project, own, info, face_metric, mortars = call(
        tables_body,
        [
            ((6, ELEMS, ELEMS), BF16),
            ((4 * RIM, ELEMS), BF16),
            ((4 * RIM, ELEMS), BF16),
            ((FACES, ELEMS), BF16),
            ((P_SIZE, 8, 2 * FACES), F32),
            ((P_SIZE, 8, 2 * FACES), F32),
            ((P_SIZE, 8, FACES), F32),
            ((16, 2 * FACES), F32),
            ((16, FACES), F32),
            ((FEAT, 2 * FACES), F32),
        ],
        (neighbours, mortar_sends, metric, fields, sel45),
        scratch=[pltpu.VMEM((2, 16, ELEMS), F32), pad],
    )
    send, receive, payload = call(
        route_body,
        [((SLOTS, 2 * FACES), BF16), ((SLOTS, 2 * FACES), BF16), ((SLOTS, FEAT), F32)],
        (facts, info, mortars),
    )
    part, arrived = fields, None
    for section in range(3):
        arrivals = exchange(payload, 4)
        lead = (part,) if section == 0 else (part, fields, arrived, place45)
        fixed = (members, local, rim_out, own, metric, neighbours, derive, select, place)
        *rims, after = call(
            bind(inner_body, section), [rim] * 4 + [whole], lead + fixed, scratch=[pad, narrow]
        )
        rims = pass_rims(rims)
        held = (after, *rims, rim_in, metric, place03)
        if section == 2:
            (part,) = call(bind(rim_body, section), [whole], held)
        else:
            part, mortars = call(
                bind(rim_body, section),
                [whole, ((FEAT, 2 * FACES), F32)],
                held + (members, basis, sel45),
                scratch=[pad],
            )
            arrived, payload = call(
                bind(flux_body, section),
                [((FEAT, FACES), F32), ((SLOTS, FEAT), F32)],
                (arrivals, receive, send, project, basis, face_metric, mortars),
                scratch=[pad, wide, broad],
            )
    (result,) = call(
        last_body,
        [whole],
        (arrivals, receive, project, face_metric, part, members, place45),
        scratch=[pad, wide, narrow],
    )
    return result


def solution(mesh):
    placed = (
        P(None, None, ("blk", "sub")),
        P(("blk", "sub")),
        P(None, ("blk", "sub")),
        P(None, ("blk", "sub")),
        P(None, ("blk", "sub")),
    )
    return jax.shard_map(
        per_device,
        mesh=mesh,
        in_specs=placed,
        out_specs=P(None, None, ("blk", "sub")),
        check_vma=False,
    )
```

```python
import jax
import jax.numpy as jnp
import numpy as np
from jax import lax
from jax.experimental import pallas as pl
from jax.experimental.pallas import tpu as pltpu
from jax.sharding import PartitionSpec as P

P_SIZE = 6
SUB = 16
IFD = 64
RIM = 32
NODES = 216
ELEMS = 256
FACES = 2 * IFD
SLOTS = 512
DEVICES = 128
TR = 40
FEAT = 128
DT_STEP = 0.01
F32 = jnp.float32
BF16 = jnp.bfloat16
VMEM_BYTES = 40 * 1024 * 1024


def legendre_columns(points, npts):
    legendre = np.zeros((npts, npts))
    legendre[:, 0] = 1.0
    legendre[:, 1] = points
    for k in range(2, npts):
        legendre[:, k] = (
            (2 * k - 1) * points * legendre[:, k - 1] - (k - 1) * legendre[:, k - 2]
        ) / k
    return legendre


def basis_tables(npts):
    order = npts - 1
    points = -np.cos(np.pi * np.arange(npts) / order)
    for iteration in range(60):
        legendre = legendre_columns(points, npts)
        points = points - (points * legendre[:, order] - legendre[:, order - 1]) / (
            npts * legendre[:, order]
        )
    legendre = legendre_columns(points, npts)
    weights = 2.0 / (order * npts * legendre[:, order] ** 2)
    separation = points[:, None] - points[None, :] + np.eye(npts)
    derivative = legendre[:, order][:, None] / legendre[:, order][None, :] / separation
    derivative = derivative * (1.0 - np.eye(npts))
    derivative[0, 0] = -order * npts / 4.0
    derivative[order, order] = order * npts / 4.0
    return (points, weights, derivative)


POINTS, WEIGHTS, DERIVATIVE = basis_tables(P_SIZE)
LIFT = float(1.0 / WEIGHTS[0])
SECTIONS = (
    (0.0, 1.0, DT_STEP),
    (0.75, 0.25, 0.25 * DT_STEP),
    (1.0 / 3.0, 2.0 / 3.0, 2.0 / 3.0 * DT_STEP),
)


def face_rows():
    picks = np.zeros((6 * TR, NODES))
    for face in range(6):
        fixed = 0 if face % 2 == 0 else P_SIZE - 1
        for a in range(P_SIZE):
            for b in range(P_SIZE):
                place = [a, b]
                place.insert(face // 2, fixed)
                node = (place[0] * P_SIZE + place[1]) * P_SIZE + place[2]
                picks[face * TR + a * P_SIZE + b, node] = 1.0
    return picks


def derivative_pieces():
    one = np.eye(P_SIZE)
    square = np.eye(P_SIZE * P_SIZE)
    whole = [
        np.kron(DERIVATIVE, square),
        np.kron(one, np.kron(DERIVATIVE, one)),
        np.kron(square, DERIVATIVE),
    ]
    pieces = []
    for matrix in whole:
        matrix = matrix.astype(np.float32)
        high = matrix.astype(jnp.bfloat16)
        pieces.append(high)
        pieces.append((matrix - high.astype(np.float32)).astype(jnp.bfloat16))
    return np.stack(pieces)


def nn(a, b):
    return lax.dot_general(a, b, (((1,), (0,)), ((), ())), preferred_element_type=F32)


def nt(a, b):
    return lax.dot_general(a, b, (((1,), (1,)), ((), ())), preferred_element_type=F32)


def tn(a, b):
    return lax.dot_general(a, b, (((0,), (0,)), ((), ())), preferred_element_type=F32)


def halves(x):
    high = x.astype(BF16)
    return high, (x - high.astype(F32)).astype(BF16)


def nn2(exact, x):
    high, low = halves(x)
    return nn(exact, high) + nn(exact, low)


def mark(cond):
    return jnp.where(cond, 1.0, 0.0)


def iota(shape, dim):
    return lax.broadcasted_iota(jnp.int32, shape, dim)


def my_device():
    return lax.axis_index("blk") * 8 + lax.axis_index("sub")


def even_place(turn):
    return (lax.axis_index(("sub", "blk")[turn]) & 1) == 0


def call(body, outs, args, scratch=(), flops=1e8, moved=2e6):
    return pl.pallas_call(
        body,
        out_shape=[jax.ShapeDtypeStruct(s, d) for s, d in outs],
        in_specs=[pl.BlockSpec(memory_space=pltpu.VMEM)] * len(args),
        out_specs=[pl.BlockSpec(memory_space=pltpu.VMEM)] * len(outs),
        scratch_shapes=list(scratch),
        compiler_params=pltpu.CompilerParams(vmem_limit_bytes=VMEM_BYTES),
        cost_estimate=pl.CostEstimate(
            flops=int(flops), bytes_accessed=int(moved), transcendentals=0
        ),
    )(*args)


def spread(values, pad, width):
    for group in range(3 * P_SIZE):
        c, i = divmod(group, P_SIZE)
        start = c * TR + i * P_SIZE
        pad[group, 0:P_SIZE, 0:width] = values[start : start + P_SIZE, :]


def to_mortars(basis, pad, out, comps, add):
    for half in range(2):
        lanes = slice(half * FACES, (half + 1) * FACES)
        for c in comps:
            for m in range(P_SIZE):
                total = basis[0, m : m + 1, lanes] * pad[c * P_SIZE, :, 0:FACES]
                for i in range(1, P_SIZE):
                    total += basis[i, m : m + 1, lanes] * pad[c * P_SIZE + i, :, 0:FACES]
                start = c * TR + m * P_SIZE
                rows = slice(start, start + P_SIZE)
                if add:
                    out[rows, lanes] += total[0:P_SIZE, :]
                else:
                    out[rows, lanes] = total[0:P_SIZE, :]


def outgoing(traces4, traces5):
    blank = jnp.zeros((FEAT - 3 * TR, ELEMS), F32)
    out4 = jnp.concatenate([traces4[0] - traces4[3], traces4[1], traces4[2], blank], axis=0)
    out5 = jnp.concatenate([traces5[0] + traces5[3], traces5[1], traces5[2], blank], axis=0)
    return out4, out5


def at_faces(rows4, rows5, members):
    high5, low5 = halves(rows5)
    high4, low4 = halves(rows4)
    rotor = nt(high5, members) + nt(low5, members)
    stator = nt(high4, members) + nt(low4, members)
    return jnp.where(iota((FEAT, FACES), 1) < IFD, rotor, stator)


def at_elements(values, members):
    rotor_side = iota((FEAT, FACES), 1) < IFD
    to5 = nn2b(jnp.where(rotor_side, values, 0.0), members)
    to4 = nn2b(jnp.where(rotor_side, 0.0, values), members)
    return to4, to5


def nn2b(x, exact):
    high, low = halves(x)
    return nn(high, exact) + nn(low, exact)


def comp(rows, c):
    return rows[c * TR : (c + 1) * TR, :]


def partner_body(pairs, out):
    row = iota((DEVICES, ELEMS), 0)
    total = None
    for mine, other in ((0, 1), (1, 0)):
        entry = pairs[mine : mine + 1, :]
        partner = pairs[other : other + 1, :]
        owner_row = mark(row == (entry >> 2)).astype(BF16)
        spot = entry & 3
        facts = jnp.where(row == spot, (partner >> 2) + 1, 0) + jnp.where(
            row == spot + 4, partner & 3, 0
        )
        term = nt(owner_row, facts.astype(F32).astype(BF16))
        total = term if total is None else total + term
    out[...] = total


def tables_body(
    neighbours, sends, metric, fields, sel45,
    local, rim_out, rim_in, members, basis, project, own, info, face_metric, mortars,
    rows, pad,
):
    me = my_device()
    nb = neighbours[...]
    face_id = iota(nb.shape, 0)
    remote = (nb >= 0) & ((nb >> 8) != me)
    here = (nb >= 0) & ((nb >> 8) == me)
    spot = nb & 255
    flags = jnp.where(face_id < 4, mark(remote), mark(nb == -2))
    rows[...] = jnp.zeros(rows.shape, F32)
    rows[0, 0:6, :] = flags
    rows[1, 0:6, :] = spot.astype(F32)
    flag_rows = rows[0].astype(BF16)
    spot_rows = rows[1].astype(BF16)
    down = iota((ELEMS, ELEMS), 0)
    across = iota((ELEMS, ELEMS), 1)
    before = mark(down < across).astype(BF16)
    same = mark(down == across).astype(BF16)
    rank = nn(flag_rows, before)
    spot_down = jnp.where(nt(same, flag_rows) > 0.5, nt(same, spot_rows), 1e4)
    key = jnp.where(here, spot, -1)
    for face in range(6):
        local[face] = mark(down == key[face : face + 1, :]).astype(BF16)
    slot = iota((RIM, ELEMS), 0).astype(F32)
    for face in range(4):
        live = flags[face : face + 1, :] > 0.5
        order = jnp.sum(
            mark(spot_down[:, face : face + 1] < rows[1, face : face + 1, :]),
            axis=0,
            keepdims=True,
        )
        lines = slice(face * RIM, (face + 1) * RIM)
        rim_out[lines, :] = mark((slot == rank[face : face + 1, :]) & live).astype(BF16)
        rim_in[lines, :] = mark((slot == order) & live).astype(BF16)
    number = iota((FACES, ELEMS), 0)
    wanted = number.astype(F32)
    rotor = (wanted == rank[5:6, :]) & (flags[5:6, :] > 0.5)
    stator = (wanted - IFD == rank[4:5, :]) & (flags[4:5, :] > 0.5)
    member = jnp.where(number < IFD, mark(rotor), mark(stator)).astype(BF16)
    members[...] = member
    face_of = sends[0:1, :]
    lo_of = sends[1:2, :]
    lane_of = jnp.where(face_of >= 0, face_of + jnp.where(lo_of > 0, FACES, 0), -1)
    slot_lane = mark(iota((2 * FACES, SLOTS), 0) == lane_of).astype(BF16)
    kind = iota((16, SLOTS), 0)
    number = iota((16, SLOTS), 1)
    facts = jnp.where(kind == 0, number >> 2, 0) + jnp.where(kind == 1, number & 3, 0)
    facts += jnp.where(kind == 2, lo_of, 0) + jnp.where(kind == 3, sends[2:3, :], 0)
    found = nt(facts.astype(F32).astype(BF16), slot_lane)
    info[...] = found
    lo = found[2:3, :]
    width = found[3:4, :] - lo
    point = iota((8, 2 * FACES), 0)
    unit = jnp.zeros((8, 2 * FACES), F32)
    weight = jnp.zeros((8, 2 * FACES), F32)
    for m in range(P_SIZE):
        unit = jnp.where(point == m, float((POINTS[m] + 1.0) * 0.5), unit)
        weight = jnp.where(point == m, float(0.5 * WEIGHTS[m] / SUB), weight)
    spots = (lo + width * unit) * (2.0 / SUB) - 1.0
    for i in range(P_SIZE):
        product = None
        for j in range(P_SIZE):
            if j != i:
                term = (spots - float(POINTS[j])) * float(1.0 / (POINTS[i] - POINTS[j]))
                product = term if product is None else product * term
        basis[i] = product
        project[i] = product * weight * width * float(1.0 / WEIGHTS[i])
    for i in range(P_SIZE):
        for k in range(P_SIZE):
            term = jnp.sum(project[i] * basis[k], axis=0, keepdims=True)
            own[i, k : k + 1, :] = term[:, 0:FACES] + term[:, FACES:]
    scale = jnp.broadcast_to(metric[...], (16, ELEMS))
    high, rest = scale.astype(BF16), scale - scale.astype(BF16).astype(F32)
    middle, low = halves(rest)
    face_metric[...] = nt(high, member) + nt(middle, member) + nt(low, member)
    traces = [nn2(sel45[...], fields[c]) for c in range(4)]
    out4, out5 = outgoing([t[:TR] for t in traces], [t[TR:] for t in traces])
    spread(at_faces(out4, out5, member), pad, FACES)
    mortars[...] = jnp.zeros(mortars.shape, F32)
    to_mortars(basis, pad, mortars, (0, 1, 2), False)


def send_rows(exact, values):
    high, low = halves(values)
    return nt(exact, high) + nt(exact, low)


def route_body(facts, info, mortars, send, receive, payload):
    owner = info[0:1, :]
    turn = info[1:2, :]
    owner_pick = mark(iota((DEVICES, 2 * FACES), 0).astype(F32) == owner).astype(BF16)
    found = tn(facts[...].astype(BF16), owner_pick)
    partner = jnp.zeros((1, 2 * FACES), F32)
    other = jnp.zeros((1, 2 * FACES), F32)
    for t in range(4):
        partner = jnp.where(turn == t, found[t : t + 1, :], partner)
        other = jnp.where(turn == t, found[4 + t : 5 + t, :], other)
    partner = partner - 1.0
    kind = iota((16, 2 * FACES), 0)
    lines = jnp.where(kind == 0, partner, 0.0) + jnp.where(kind == 1, owner, 0.0)
    lines += jnp.where(kind == 2, turn, 0.0) + jnp.where(kind == 3, other, 0.0)
    same = mark(iota((2 * FACES, 2 * FACES), 0) == iota((2 * FACES, 2 * FACES), 1)).astype(BF16)
    down = nt(same, lines.astype(BF16))
    partner_down = down[:, 0:1]
    together = partner_down == partner
    mine_down = down[:, 1:2] * 4.0 + down[:, 2:3]
    theirs_down = down[:, 1:2] * 4.0 + down[:, 3:4]
    mine = owner * 4.0 + turn
    theirs = owner * 4.0 + other
    ahead = jnp.sum(mark(together & (mine_down < mine)), axis=0, keepdims=True)
    behind = jnp.sum(mark(together & (theirs_down < theirs)), axis=0, keepdims=True)
    place = iota((SLOTS, 2 * FACES), 0).astype(F32)
    sending = mark(place == partner * 4.0 + ahead).astype(BF16)
    send[...] = sending
    receive[...] = mark(place == partner * 4.0 + behind).astype(BF16)
    payload[...] = send_rows(sending, mortars[...])


def place_interface(part, arrived, members, place45):
    to4, to5 = at_elements(arrived[...], members[...])
    result = []
    for c in range(4):
        source = (0, 1, 2, 0)[c]
        sign5 = -1.0 if c == 3 else 1.0
        stack = jnp.concatenate([comp(to4, source), sign5 * comp(to5, source)], axis=0)
        result.append(part[c] + nn2(place45[...], stack))
    return result


def inner_body(section, *refs):
    if section == 0:
        part, refs = refs[0], refs[1:]
        first = part
        arrived = None
    else:
        part, first, arrived, place45 = refs[:4]
        refs = refs[4:]
    (members, local, rim_out, own, metric, neighbours, derive, select, place) = refs[:9]
    rims = refs[9:13]
    after, pad, mixed = refs[13:]
    keep, stay, rate = SECTIONS[section]
    if section == 0:
        fields = [part[c] for c in range(4)]
    else:
        fields = place_interface(part, arrived, members, place45)
    high, low = zip(*[halves(x) for x in fields])
    sel = select[...]
    traces = [nn(sel, high[c]) + nn(sel, low[c]) for c in range(4)]
    blank = jnp.zeros((FEAT - 3 * TR, ELEMS), F32)
    leaving, inside = [], []
    for face in range(6):
        sign = 1.0 if face % 2 else -1.0
        cut = [t[face * TR : (face + 1) * TR, :] for t in traces]
        along = face // 2
        tangent = [cut[1 + c] for c in range(3) if c != along]
        normal = sign * cut[1 + along]
        leaving.append(jnp.concatenate([cut[0] + normal] + tangent + [blank], axis=0))
        inside.append(jnp.concatenate([cut[0] - normal] + tangent + [blank], axis=0))
    leaving = [halves(x) for x in leaving]
    parts = []
    for face in range(4):
        pick = rim_out[face * RIM : (face + 1) * RIM, :]
        parts.append(nt(pick, leaving[face][0]) + nt(pick, leaving[face][1]))
    for turn, (down, up) in enumerate((parts[:2], parts[2:])):
        even = even_place(turn)
        rims[2 * turn][...] = jnp.where(even, up, down)
        rims[2 * turn + 1][...] = jnp.where(even, down, up)
    spread(at_faces(inside[4], inside[5], members[...]), pad, FACES)
    mixed[...] = jnp.zeros(mixed.shape, F32)
    for c in range(3):
        for i in range(P_SIZE):
            total = own[i, 0:1, :] * pad[c * P_SIZE]
            for k in range(1, P_SIZE):
                total += own[i, k : k + 1, :] * pad[c * P_SIZE + k]
            start = c * TR + i * P_SIZE
            mixed[start : start + P_SIZE, :] = -total[0:P_SIZE, :]
    to4, to5 = at_elements(mixed[...], members[...])
    terms = []
    for face in range(6):
        pick = local[face]
        arriving = nn(leaving[face ^ 1][0], pick) + nn(leaving[face ^ 1][1], pick)
        term = 0.5 * (arriving - inside[face])
        if face >= 4:
            term = jnp.where(neighbours[face : face + 1, :] == -2, 0.0, term)
            term = term + (to4, to5)[face - 4]
        terms.append(term)
    scale = metric[...] * rate
    for c in range(4):
        pieces = []
        for face in range(6):
            along = face // 2
            if c == 0:
                pieces.append(comp(terms[face], 0))
            elif c == 1 + along:
                pieces.append((-1.0 if face % 2 else 1.0) * comp(terms[face], 0))
            else:
                tangents = [k for k in range(3) if k != along]
                pieces.append(comp(terms[face], 1 + tangents.index(c - 1)))
        surface = nn2(place[...], jnp.concatenate(pieces, axis=0))
        if c == 0:
            pairs = ((0, 1), (1, 2), (2, 3))
        else:
            pairs = ((c - 1, 0),)
        volume = None
        for direction, source in pairs:
            big, small = derive[2 * direction], derive[2 * direction + 1]
            term = nn(big, high[source]) + nn(big, low[source]) + nn(small, high[source])
            volume = term if volume is None else volume + term
        base = stay * fields[c]
        if keep:
            base = base + keep * first[c]
        after[c] = base + scale * (LIFT * surface - volume)


def rim_body(section, *refs):
    before, r0, r1, r2, r3, rim_in, metric, place03 = refs[:8]
    last = section == 2
    if last:
        (after,) = refs[8:]
    else:
        members, basis, sel45, after, mortars, pad = refs[8:]
    scale = metric[...] * (SECTIONS[section][2] * LIFT)
    terms = []
    got = []
    for turn, (one, two) in enumerate(((r0, r1), (r2, r3))):
        even = even_place(turn)
        got.append(jnp.where(even, two[...], one[...]))
        got.append(jnp.where(even, one[...], two[...]))
    for face, value in enumerate(got):
        high, low = halves(value)
        pick = rim_in[face * RIM : (face + 1) * RIM, :]
        terms.append(0.5 * (tn(high, pick) + tn(low, pick)))
    fields = []
    for c in range(4):
        pieces = []
        for face in range(4):
            along = face // 2
            if c == 0:
                pieces.append(comp(terms[face], 0))
            elif c == 1 + along:
                pieces.append((-1.0 if face % 2 else 1.0) * comp(terms[face], 0))
            else:
                tangents = [k for k in range(3) if k != along]
                pieces.append(comp(terms[face], 1 + tangents.index(c - 1)))
        value = before[c] + scale * nn2(place03[...], jnp.concatenate(pieces, axis=0))
        after[c] = value
        fields.append(value)
    if not last:
        traces = [nn2(sel45[...], x) for x in fields]
        out4, out5 = outgoing([t[:TR] for t in traces], [t[TR:] for t in traces])
        spread(at_faces(out4, out5, members[...]), pad, FACES)
        mortars[...] = jnp.zeros(mortars.shape, F32)
        to_mortars(basis, pad, mortars, (0, 1, 2), False)


def arrive(section, arrivals, receive, project, face_metric, pad, wide, out):
    high, low = halves(arrivals[...])
    pick = receive[...]
    spread(tn(high, pick) + tn(low, pick), wide, 2 * FACES)
    scale = face_metric[0:1, :] * (SECTIONS[section][2] * LIFT)
    out[...] = jnp.zeros(out.shape, F32)
    for c in range(3):
        for i in range(P_SIZE):
            total = None
            for half in range(2):
                lanes = slice(half * FACES, (half + 1) * FACES)
                for m in range(P_SIZE):
                    term = project[i, m : m + 1, lanes] * wide[c * P_SIZE + m, :, lanes]
                    total = term if total is None else total + term
            total = total * scale
            pad[c * P_SIZE + i] = total
            start = c * TR + i * P_SIZE
            out[start : start + P_SIZE, :] = total[0:P_SIZE, :]


def flux_body(
    section, arrivals, receive, send, project, basis, face_metric, mortars,
    arrived, payload, pad, wide, mixed,
):
    arrive(section, arrivals, receive, project, face_metric, pad, wide, arrived)
    mixed[...] = mortars[...]
    to_mortars(basis, pad, mixed, (1, 2), True)
    payload[...] = send_rows(send[...], mixed[...])


def last_body(
    arrivals, receive, project, face_metric, part, members, place45, after, pad, wide, arrived
):
    arrive(2, arrivals, receive, project, face_metric, pad, wide, arrived)
    result = place_interface(part, arrived, members, place45)
    for c in range(4):
        after[c] = result[c]


def exchange(rows, width):
    whole = rows.reshape(DEVICES, width, FEAT)
    moved = lax.all_to_all(whole, ("blk", "sub"), split_axis=0, concat_axis=0, tiled=True)
    return moved.reshape(DEVICES * width, FEAT)


def pass_rims(rims):
    arrived = []
    for turn in range(4):
        axis = ("sub", "blk")[turn // 2]
        count = lax.axis_size(axis)
        pairs = []
        for i in range(turn % 2, count, 2):
            j = (i + 1) % count
            pairs += [(i, j), (j, i)]
        arrived.append(lax.ppermute(rims[turn], axis, pairs))
    return arrived


def bind(body, section):
    def bound(*refs):
        body(section, *refs)

    return bound


def per_device(fields, metric, neighbours, mortar_sends, mortar_pairs):
    picks = face_rows()
    select = jnp.asarray(picks, BF16)
    sel45 = jnp.asarray(picks[4 * TR :], BF16)
    place = jnp.asarray(picks.T, BF16)
    place03 = jnp.asarray(picks[: 4 * TR].T, BF16)
    place45 = jnp.asarray(picks[4 * TR :].T, BF16)
    derive = jnp.asarray(derivative_pieces())
    metric = metric.reshape(1, ELEMS)
    whole = ((4, NODES, ELEMS), F32)
    rim = ((RIM, FEAT), F32)
    pad = pltpu.VMEM((3 * P_SIZE, 8, FACES), F32)
    wide = pltpu.VMEM((3 * P_SIZE, 8, 2 * FACES), F32)
    narrow = pltpu.VMEM((FEAT, FACES), F32)
    broad = pltpu.VMEM((FEAT, 2 * FACES), F32)

    (facts,) = call(partner_body, [((DEVICES, FEAT), F32)], (mortar_pairs,))
    facts = exchange(facts, 1)
    local, rim_out, rim_in, members, basis, project, own, info, face_metric, mortars = call(
        tables_body,
        [
            ((6, ELEMS, ELEMS), BF16),
            ((4 * RIM, ELEMS), BF16),
            ((4 * RIM, ELEMS), BF16),
            ((FACES, ELEMS), BF16),
            ((P_SIZE, 8, 2 * FACES), F32),
            ((P_SIZE, 8, 2 * FACES), F32),
            ((P_SIZE, 8, FACES), F32),
            ((16, 2 * FACES), F32),
            ((16, FACES), F32),
            ((FEAT, 2 * FACES), F32),
        ],
        (neighbours, mortar_sends, metric, fields, sel45),
        scratch=[pltpu.VMEM((2, 16, ELEMS), F32), pad],
    )
    send, receive, payload = call(
        route_body,
        [((SLOTS, 2 * FACES), BF16), ((SLOTS, 2 * FACES), BF16), ((SLOTS, FEAT), F32)],
        (facts, info, mortars),
    )
    part, arrived = fields, None
    for section in range(3):
        arrivals = exchange(payload, 4)
        lead = (part,) if section == 0 else (part, fields, arrived, place45)
        fixed = (members, local, rim_out, own, metric, neighbours, derive, select, place)
        *rims, after = call(
            bind(inner_body, section), [rim] * 4 + [whole], lead + fixed, scratch=[pad, narrow]
        )
        rims = pass_rims(rims)
        held = (after, *rims, rim_in, metric, place03)
        if section == 2:
            (part,) = call(bind(rim_body, section), [whole], held)
        else:
            part, mortars = call(
                bind(rim_body, section),
                [whole, ((FEAT, 2 * FACES), F32)],
                held + (members, basis, sel45),
                scratch=[pad],
            )
            arrived, payload = call(
                bind(flux_body, section),
                [((FEAT, FACES), F32), ((SLOTS, FEAT), F32)],
                (arrivals, receive, send, project, basis, face_metric, mortars),
                scratch=[pad, wide, broad],
            )
    (result,) = call(
        last_body,
        [whole],
        (arrivals, receive, project, face_metric, part, members, place45),
        scratch=[pad, wide, narrow],
    )
    return result


def solution(mesh):
    placed = (
        P(None, None, ("blk", "sub")),
        P(("blk", "sub")),
        P(None, ("blk", "sub")),
        P(None, ("blk", "sub")),
        P(None, ("blk", "sub")),
    )
    return jax.shard_map(
        per_device,
        mesh=mesh,
        in_specs=placed,
        out_specs=P(None, None, ("blk", "sub")),
        check_vma=False,
    )
```

```python
import jax
import jax.numpy as jnp
import numpy as np
from jax import lax
from jax.experimental import pallas as pl
from jax.experimental.pallas import tpu as pltpu
from jax.sharding import PartitionSpec as P

P_SIZE = 6
SUB = 16
IFD = 64
RIM = 32
NODES = 216
ELEMS = 256
FACES = 2 * IFD
SLOTS = 512
DEVICES = 128
TR = 40
PROJECT = 48
METRIC = 96
FACT_ROWS = 104
ROUTES = FACT_ROWS + 128
NEAR, RIM_OUT, RIM_IN, ROTOR, STATOR, SCALE, KEY_ROWS = 0, 6, 10, 14, 15, 16, 24
FEAT = 128
DT_STEP = 0.01
F32 = jnp.float32
BF16 = jnp.bfloat16
VMEM_BYTES = 24 * 1024 * 1024


def legendre_columns(points, npts):
    legendre = np.zeros((npts, npts))
    legendre[:, 0] = 1.0
    legendre[:, 1] = points
    for k in range(2, npts):
        legendre[:, k] = (
            (2 * k - 1) * points * legendre[:, k - 1] - (k - 1) * legendre[:, k - 2]
        ) / k
    return legendre


def basis_tables(npts):
    order = npts - 1
    points = -np.cos(np.pi * np.arange(npts) / order)
    for iteration in range(60):
        legendre = legendre_columns(points, npts)
        points = points - (points * legendre[:, order] - legendre[:, order - 1]) / (
            npts * legendre[:, order]
        )
    legendre = legendre_columns(points, npts)
    weights = 2.0 / (order * npts * legendre[:, order] ** 2)
    separation = points[:, None] - points[None, :] + np.eye(npts)
    derivative = legendre[:, order][:, None] / legendre[:, order][None, :] / separation
    derivative = derivative * (1.0 - np.eye(npts))
    derivative[0, 0] = -order * npts / 4.0
    derivative[order, order] = order * npts / 4.0
    return (points, weights, derivative)


POINTS, WEIGHTS, DERIVATIVE = basis_tables(P_SIZE)
LIFT = float(1.0 / WEIGHTS[0])
SECTIONS = (
    (0.0, 1.0, DT_STEP),
    (0.75, 0.25, 0.25 * DT_STEP),
    (1.0 / 3.0, 2.0 / 3.0, 2.0 / 3.0 * DT_STEP),
)


def face_rows():
    picks = np.zeros((6 * TR, NODES))
    for face in range(6):
        fixed = 0 if face % 2 == 0 else P_SIZE - 1
        for a in range(P_SIZE):
            for b in range(P_SIZE):
                place = [a, b]
                place.insert(face // 2, fixed)
                node = (place[0] * P_SIZE + place[1]) * P_SIZE + place[2]
                picks[face * TR + a * P_SIZE + b, node] = 1.0
    return picks


def derivative_pieces():
    one = np.eye(P_SIZE)
    square = np.eye(P_SIZE * P_SIZE)
    whole = [
        np.kron(DERIVATIVE, square),
        np.kron(one, np.kron(DERIVATIVE, one)),
        np.kron(square, DERIVATIVE),
    ]
    pieces = []
    for matrix in whole:
        matrix = matrix.astype(np.float32)
        high = matrix.astype(jnp.bfloat16)
        pieces.append(high)
        pieces.append((matrix - high.astype(np.float32)).astype(jnp.bfloat16))
    return np.stack(pieces)


def nn(a, b):
    return lax.dot_general(a, b, (((1,), (0,)), ((), ())), preferred_element_type=F32)


def nt(a, b):
    return lax.dot_general(a, b, (((1,), (1,)), ((), ())), preferred_element_type=F32)


def tn(a, b):
    return lax.dot_general(a, b, (((0,), (0,)), ((), ())), preferred_element_type=F32)


def halves(x):
    high = x.astype(BF16)
    return high, (x - high.astype(F32)).astype(BF16)


def nn2(exact, x):
    high, low = halves(x)
    return nn(exact, high) + nn(exact, low)


def mark(cond):
    return jnp.where(cond, 1.0, 0.0)


def iota(shape, dim):
    return lax.broadcasted_iota(jnp.int32, shape, dim)


def my_device():
    return lax.axis_index("blk") * 8 + lax.axis_index("sub")


def even_place(turn):
    return (lax.axis_index(("sub", "blk")[turn]) & 1) == 0


class Fetched:
    def __init__(self, copy, buffer):
        self.copy, self.buffer, self.here = copy, buffer, False

    def __getitem__(self, key):
        if not self.here:
            self.copy.wait()
            self.here = True
        return self.buffer[key]


def call(body, outs, args, scratch=(), flops=1e8, moved=2e6):
    far_in = [i for i, (_, space) in enumerate(args) if space == "h"]
    far_out = [i for i, (_, _, space) in enumerate(outs) if space == "h"]
    own = [pltpu.VMEM(args[i][0].shape, args[i][0].dtype) for i in far_in]
    own += [pltpu.VMEM(outs[i][0], outs[i][1]) for i in far_out]
    count = len(far_in) + len(far_out)

    def kernel(*refs):
        refs = list(refs)
        ins, refs = refs[: len(args)], refs[len(args) :]
        results, refs = refs[: len(outs)], refs[len(outs) :]
        extra, refs = refs[: len(scratch)], refs[len(scratch) :]
        sems = refs[-1] if count else None
        for n, i in enumerate(far_in):
            copy = pltpu.make_async_copy(ins[i], refs[n], sems.at[n])
            copy.start()
            ins[i] = Fetched(copy, refs[n])
        shown = list(results)
        for n, i in enumerate(far_out):
            shown[i] = refs[len(far_in) + n]
        body(*ins, *shown, *extra)
        for i in far_in:
            if not ins[i].here:
                ins[i].copy.wait()
        copies = []
        for n, i in enumerate(far_out):
            spot = len(far_in) + n
            copies.append(pltpu.make_async_copy(refs[spot], results[i], sems.at[spot]))
            copies[-1].start()
        for copy in copies:
            copy.wait()

    spaces = {"h": pltpu.HBM, "v": pltpu.VMEM}
    return pl.pallas_call(
        kernel,
        out_shape=[jax.ShapeDtypeStruct(o[0], o[1]) for o in outs],
        in_specs=[pl.BlockSpec(memory_space=spaces[space]) for _, space in args],
        out_specs=[pl.BlockSpec(memory_space=spaces[o[2]]) for o in outs],
        scratch_shapes=list(scratch)
        + own
        + ([pltpu.SemaphoreType.DMA((count,))] if count else []),
        compiler_params=pltpu.CompilerParams(vmem_limit_bytes=VMEM_BYTES),
        cost_estimate=pl.CostEstimate(
            flops=int(flops), bytes_accessed=int(moved), transcendentals=0
        ),
    )(*[array for array, _ in args])


def spread(values, pad, width):
    for group in range(3 * P_SIZE):
        c, i = divmod(group, P_SIZE)
        start = c * TR + i * P_SIZE
        pad[group, 0:P_SIZE, 0:width] = values[start : start + P_SIZE, :]


def to_mortars(facts, pad, out, comps, add):
    for half in range(2):
        lanes = slice(half * FACES, (half + 1) * FACES)
        for c in comps:
            for m in range(P_SIZE):
                total = facts[m : m + 1, lanes] * pad[c * P_SIZE, :, 0:FACES]
                for i in range(1, P_SIZE):
                    row = i * 8 + m
                    total += facts[row : row + 1, lanes] * pad[c * P_SIZE + i, :, 0:FACES]
                start = c * TR + m * P_SIZE
                rows = slice(start, start + P_SIZE)
                if add:
                    out[rows, lanes] += total[0:P_SIZE, :]
                else:
                    out[rows, lanes] = total[0:P_SIZE, :]


def outgoing(traces4, traces5):
    blank = jnp.zeros((FEAT - 3 * TR, ELEMS), F32)
    out4 = jnp.concatenate([traces4[0] - traces4[3], traces4[1], traces4[2], blank], axis=0)
    out5 = jnp.concatenate([traces5[0] + traces5[3], traces5[1], traces5[2], blank], axis=0)
    return out4, out5


def at_faces(rows4, rows5, members):
    high5, low5 = halves(rows5)
    high4, low4 = halves(rows4)
    rotor = nt(high5, members) + nt(low5, members)
    stator = nt(high4, members) + nt(low4, members)
    return jnp.where(iota((FEAT, FACES), 1) < IFD, rotor, stator)


def at_elements(values, members):
    rotor_side = iota((FEAT, FACES), 1) < IFD
    to5 = nn2b(jnp.where(rotor_side, values, 0.0), members)
    to4 = nn2b(jnp.where(rotor_side, 0.0, values), members)
    return to4, to5


def nn2b(x, exact):
    high, low = halves(x)
    return nn(high, exact) + nn(low, exact)


def comp(rows, c):
    return rows[c * TR : (c + 1) * TR, :]


def partner_body(pairs, out):
    row = iota((DEVICES, ELEMS), 0)
    total = None
    for mine, other in ((0, 1), (1, 0)):
        entry = pairs[mine : mine + 1, :]
        partner = pairs[other : other + 1, :]
        owner_row = mark(row == (entry >> 2)).astype(BF16)
        spot = entry & 3
        facts = jnp.where(row == spot, (partner >> 2) + 1, 0) + jnp.where(
            row == spot + 4, partner & 3, 0
        )
        term = nt(owner_row, facts.astype(F32).astype(BF16))
        total = term if total is None else total + term
    out[...] = total


def picked(keys, row, count):
    return mark(iota((count, ELEMS), 0).astype(F32) == keys[row : row + 1, :]).astype(BF16)


def member_picks(keys):
    number = iota((FACES, ELEMS), 0).astype(F32)
    rotor = number == keys[ROTOR : ROTOR + 1, :]
    stator = number == keys[STATOR : STATOR + 1, :]
    return mark(rotor | stator).astype(BF16)


def tables_body(
    neighbours, sends, metric, fields, select,
    keys, facts, own, info, mortars,
    rows, pad,
):
    me = my_device()
    nb = neighbours[...]
    face_id = iota((6, ELEMS), 0)
    remote = (nb >= 0) & ((nb >> 8) != me)
    here = (nb >= 0) & ((nb >> 8) == me)
    spot = nb & 255
    flags = jnp.where(face_id < 4, mark(remote), mark(nb == -2))
    rows[...] = jnp.zeros(rows.shape, F32)
    rows[0, 0:6, :] = flags
    rows[1, 0:6, :] = spot.astype(F32)
    flag_rows = rows[0].astype(BF16)
    spot_rows = rows[1].astype(BF16)
    down = iota((ELEMS, ELEMS), 0)
    across = iota((ELEMS, ELEMS), 1)
    before = mark(down < across).astype(BF16)
    same = mark(down == across).astype(BF16)
    rank = nn(flag_rows, before)
    spot_down = jnp.where(nt(same, flag_rows) > 0.5, nt(same, spot_rows), 1e4)
    keys[...] = jnp.zeros(keys.shape, F32)
    keys[NEAR : NEAR + 6, :] = jnp.where(here, spot, -1).astype(F32)
    for face in range(4):
        live = flags[face : face + 1, :] > 0.5
        order = jnp.sum(
            mark(spot_down[:, face : face + 1] < rows[1, face : face + 1, :]),
            axis=0,
            keepdims=True,
        )
        place = RIM_OUT + face
        keys[place : place + 1, :] = jnp.where(live, rank[face : face + 1, :], -1.0)
        place = RIM_IN + face
        keys[place : place + 1, :] = jnp.where(live, order, -1.0)
    keys[ROTOR : ROTOR + 1, :] = jnp.where(flags[5:6, :] > 0.5, rank[5:6, :], -1.0)
    keys[STATOR : STATOR + 1, :] = jnp.where(flags[4:5, :] > 0.5, rank[4:5, :] + IFD, -1.0)
    keys[SCALE : SCALE + 1, :] = metric[...]
    member = member_picks(keys)
    face_of = sends[0:1, :]
    lo_of = sends[1:2, :]
    lane_of = jnp.where(face_of >= 0, face_of + jnp.where(lo_of > 0, FACES, 0), -1)
    slot_lane = mark(iota((2 * FACES, SLOTS), 0) == lane_of).astype(BF16)
    kind = iota((16, SLOTS), 0)
    number = iota((16, SLOTS), 1)
    lines = jnp.where(kind == 0, number >> 2, 0) + jnp.where(kind == 1, number & 3, 0)
    lines += jnp.where(kind == 2, lo_of, 0) + jnp.where(kind == 3, sends[2:3, :], 0)
    found = nt(lines.astype(F32).astype(BF16), slot_lane)
    info[...] = found
    lo = found[2:3, :]
    width = found[3:4, :] - lo
    point = iota((8, 2 * FACES), 0)
    unit = jnp.zeros((8, 2 * FACES), F32)
    weight = jnp.zeros((8, 2 * FACES), F32)
    for m in range(P_SIZE):
        unit = jnp.where(point == m, float((POINTS[m] + 1.0) * 0.5), unit)
        weight = jnp.where(point == m, float(0.5 * WEIGHTS[m] / SUB), weight)
    spots = (lo + width * unit) * (2.0 / SUB) - 1.0
    for i in range(P_SIZE):
        product = None
        for j in range(P_SIZE):
            if j != i:
                term = (spots - float(POINTS[j])) * float(1.0 / (POINTS[i] - POINTS[j]))
                product = term if product is None else product * term
        facts[i * 8 : i * 8 + 8, :] = product
        start = PROJECT + i * 8
        facts[start : start + 8, :] = product * weight * width * float(1.0 / WEIGHTS[i])
    for i in range(P_SIZE):
        for k in range(P_SIZE):
            start = PROJECT + i * 8
            term = facts[start : start + 8, :] * facts[k * 8 : k * 8 + 8, :]
            term = jnp.sum(term, axis=0, keepdims=True)
            own[i * 8 + k : i * 8 + k + 1, :] = term[:, 0:FACES] + term[:, FACES:]
    scale = jnp.broadcast_to(metric[...], (16, ELEMS))
    high, rest = scale.astype(BF16), scale - scale.astype(BF16).astype(F32)
    middle, low = halves(rest)
    scale = nt(high, member) + nt(middle, member) + nt(low, member)
    facts[METRIC:FACT_ROWS, :] = jnp.concatenate([scale[0:8, :]] * 2, axis=1)
    traces = [nn2(select[4 * TR : 6 * TR, :], fields[c]) for c in range(4)]
    out4, out5 = outgoing([t[:TR] for t in traces], [t[TR:] for t in traces])
    spread(at_faces(out4, out5, member), pad, FACES)
    mortars[...] = jnp.zeros((FEAT, 2 * FACES), F32)
    to_mortars(facts, pad, mortars, (0, 1, 2), False)


def slot_picks(row):
    return mark(iota((SLOTS, 2 * FACES), 0).astype(F32) == row).astype(BF16)


def send_rows(exact, values):
    high, low = halves(values)
    return nt(exact, high) + nt(exact, low)


def route_body(facts, info, mortars, routes, payload):
    owner = info[0:1, :]
    turn = info[1:2, :]
    owner_pick = mark(iota((DEVICES, 2 * FACES), 0).astype(F32) == owner).astype(BF16)
    found = tn(facts[...].astype(BF16), owner_pick)
    partner = jnp.zeros((1, 2 * FACES), F32)
    other = jnp.zeros((1, 2 * FACES), F32)
    for t in range(4):
        partner = jnp.where(turn == t, found[t : t + 1, :], partner)
        other = jnp.where(turn == t, found[4 + t : 5 + t, :], other)
    partner = partner - 1.0
    kind = iota((16, 2 * FACES), 0)
    lines = jnp.where(kind == 0, partner, 0.0) + jnp.where(kind == 1, owner, 0.0)
    lines += jnp.where(kind == 2, turn, 0.0) + jnp.where(kind == 3, other, 0.0)
    same = mark(iota((2 * FACES, 2 * FACES), 0) == iota((2 * FACES, 2 * FACES), 1)).astype(BF16)
    down = nt(same, lines.astype(BF16))
    partner_down = down[:, 0:1]
    together = partner_down == partner
    mine_down = down[:, 1:2] * 4.0 + down[:, 2:3]
    theirs_down = down[:, 1:2] * 4.0 + down[:, 3:4]
    mine = owner * 4.0 + turn
    theirs = owner * 4.0 + other
    ahead = jnp.sum(mark(together & (mine_down < mine)), axis=0, keepdims=True)
    behind = jnp.sum(mark(together & (theirs_down < theirs)), axis=0, keepdims=True)
    kind = iota((8, 2 * FACES), 0)
    routes[...] = partner * 4.0 + jnp.where(kind == 0, ahead, behind)
    payload[...] = send_rows(slot_picks(partner * 4.0 + ahead), mortars[...])


def placed(picks, x):
    high, low = halves(x)
    return tn(picks, high) + tn(picks, low)


def place_interface(part, arrived, keys, select):
    picks = select[4 * TR : 6 * TR, :]
    to4, to5 = at_elements(arrived[...], member_picks(keys))
    result = []
    for c in range(4):
        source = (0, 1, 2, 0)[c]
        sign5 = -1.0 if c == 3 else 1.0
        stack = jnp.concatenate([comp(to4, source), sign5 * comp(to5, source)], axis=0)
        result.append(part[c] + placed(picks, stack))
    return result


def characteristics(traces, faces):
    blank = jnp.zeros((FEAT - 3 * TR, ELEMS), F32)
    leaving, inside = [], []
    for face in range(faces):
        sign = 1.0 if face % 2 else -1.0
        cut = [t[face * TR : (face + 1) * TR, :] for t in traces]
        along = face // 2
        tangent = [cut[1 + c] for c in range(3) if c != along]
        normal = sign * cut[1 + along]
        leaving.append(halves(jnp.concatenate([cut[0] + normal] + tangent + [blank], axis=0)))
        inside.append(jnp.concatenate([cut[0] - normal] + tangent + [blank], axis=0))
    return leaving, inside


def edge_body(section, *refs):
    part, keys, select = refs[:3]
    if section == 0:
        fields = [part[c] for c in range(4)]
        rims = refs[3:]
    else:
        arrived, whole = refs[3:5]
        fields = place_interface(part, arrived, keys, select)
        rims = refs[5:]
        for c in range(4):
            whole[c] = fields[c]
    leaving, _ = characteristics([nn2(select[0 : 4 * TR, :], x) for x in fields], 4)
    parts = []
    for face in range(4):
        pick = picked(keys, RIM_OUT + face, RIM)
        parts.append(nt(pick, leaving[face][0]) + nt(pick, leaving[face][1]))
    for turn, (down, up) in enumerate((parts[:2], parts[2:])):
        even = even_place(turn)
        rims[2 * turn][...] = jnp.where(even, up, down)
        rims[2 * turn + 1][...] = jnp.where(even, down, up)


def inner_body(section, *refs):
    whole, refs = refs[0], refs[1:]
    if section:
        first, refs = refs[0], refs[1:]
    select, derive, neighbours, keys, own, after, pad, mixed = refs
    keep, stay, rate = SECTIONS[section]
    fields = [whole[c] for c in range(4)]
    high, low = zip(*[halves(x) for x in fields])
    sel = select[...]
    traces = [nn(sel, high[c]) + nn(sel, low[c]) for c in range(4)]
    leaving, inside = characteristics(traces, 6)
    members = member_picks(keys)
    spread(at_faces(inside[4], inside[5], members), pad, FACES)
    mixed[...] = jnp.zeros(mixed.shape, F32)
    for c in range(3):
        for i in range(P_SIZE):
            total = own[i * 8 : i * 8 + 1, :] * pad[c * P_SIZE]
            for k in range(1, P_SIZE):
                row = i * 8 + k
                total += own[row : row + 1, :] * pad[c * P_SIZE + k]
            start = c * TR + i * P_SIZE
            mixed[start : start + P_SIZE, :] = -total[0:P_SIZE, :]
    to4, to5 = at_elements(mixed[...], members)
    terms = []
    for face in range(6):
        pick = picked(keys, NEAR + face, ELEMS)
        arriving = nn(leaving[face ^ 1][0], pick) + nn(leaving[face ^ 1][1], pick)
        term = 0.5 * (arriving - inside[face])
        if face >= 4:
            term = jnp.where(neighbours[face : face + 1, :] == -2, 0.0, term)
            term = term + (to4, to5)[face - 4]
        terms.append(term)
    scale = keys[SCALE : SCALE + 1, :] * rate
    for c in range(4):
        pieces = []
        for face in range(6):
            along = face // 2
            if c == 0:
                pieces.append(comp(terms[face], 0))
            elif c == 1 + along:
                pieces.append((-1.0 if face % 2 else 1.0) * comp(terms[face], 0))
            else:
                tangents = [k for k in range(3) if k != along]
                pieces.append(comp(terms[face], 1 + tangents.index(c - 1)))
        surface = placed(sel, jnp.concatenate(pieces, axis=0))
        if c == 0:
            pairs = ((0, 1), (1, 2), (2, 3))
        else:
            pairs = ((c - 1, 0),)
        volume = None
        for direction, source in pairs:
            big, small = derive[2 * direction], derive[2 * direction + 1]
            term = nn(big, high[source]) + nn(big, low[source]) + nn(small, high[source])
            volume = term if volume is None else volume + term
        base = stay * fields[c]
        if keep:
            base = base + keep * first[c]
        after[c] = base + scale * (LIFT * surface - volume)


def rim_body(section, *refs):
    before, r0, r1, r2, r3, select, keys, facts, routes = refs[:9]
    last = section == 2
    after, pack = refs[9:11]
    scale = keys[SCALE : SCALE + 1, :] * (SECTIONS[section][2] * LIFT)
    terms = []
    terms = []
    got = []
    for turn, (one, two) in enumerate(((r0, r1), (r2, r3))):
        even = even_place(turn)
        got.append(jnp.where(even, two[...], one[...]))
        got.append(jnp.where(even, one[...], two[...]))
    for face, value in enumerate(got):
        high, low = halves(value)
        pick = picked(keys, RIM_IN + face, RIM)
        terms.append(0.5 * (tn(high, pick) + tn(low, pick)))
    fields = []
    for c in range(4):
        pieces = []
        for face in range(4):
            along = face // 2
            if c == 0:
                pieces.append(comp(terms[face], 0))
            elif c == 1 + along:
                pieces.append((-1.0 if face % 2 else 1.0) * comp(terms[face], 0))
            else:
                tangents = [k for k in range(3) if k != along]
                pieces.append(comp(terms[face], 1 + tangents.index(c - 1)))
        value = before[c] + scale * placed(select[0 : 4 * TR, :], jnp.concatenate(pieces, axis=0))
        after[c] = value
        fields.append(value)
    pack[0:FACT_ROWS, :] = facts[...]
    pack[ROUTES : ROUTES + 8, :] = routes[...]
    if not last:
        pad = refs[11]
        traces = [nn2(select[4 * TR : 6 * TR, :], x) for x in fields]
        out4, out5 = outgoing([t[:TR] for t in traces], [t[TR:] for t in traces])
        spread(at_faces(out4, out5, member_picks(keys)), pad, FACES)
        mortars = pack.at[FACT_ROWS:ROUTES, :]
        mortars[...] = jnp.zeros((FEAT, 2 * FACES), F32)
        to_mortars(facts, pad, mortars, (0, 1, 2), False)


def arrive(section, arrivals, held, pad, wide, out):
    high, low = halves(arrivals[...])
    pick = slot_picks(held[ROUTES + 1 : ROUTES + 2, :])
    spread(tn(high, pick) + tn(low, pick), wide, 2 * FACES)
    scale = held[METRIC : METRIC + 1, 0:FACES] * (SECTIONS[section][2] * LIFT)
    out[...] = jnp.zeros(out.shape, F32)
    for c in range(3):
        for i in range(P_SIZE):
            total = None
            for half in range(2):
                lanes = slice(half * FACES, (half + 1) * FACES)
                for m in range(P_SIZE):
                    row = PROJECT + i * 8 + m
                    term = held[row : row + 1, lanes] * wide[c * P_SIZE + m, :, lanes]
                    total = term if total is None else total + term
            total = total * scale
            pad[c * P_SIZE + i] = total
            start = c * TR + i * P_SIZE
            out[start : start + P_SIZE, :] = total[0:P_SIZE, :]


def flux_body(section, arrivals, held, arrived, payload, pad, wide, mixed):
    arrive(section, arrivals, held, pad, wide, arrived)
    mixed[...] = held[FACT_ROWS:ROUTES, :]
    to_mortars(held, pad, mixed, (1, 2), True)
    payload[...] = send_rows(slot_picks(held[ROUTES : ROUTES + 1, :]), mixed[...])


def last_body(arrivals, held, part, keys, select, after, pad, wide, arrived):
    arrive(2, arrivals, held, pad, wide, arrived)
    result = place_interface(part, arrived, keys, select)
    for c in range(4):
        after[c] = result[c]


def exchange(rows, width):
    whole = rows.reshape(DEVICES, width, FEAT)
    moved = lax.all_to_all(whole, ("blk", "sub"), split_axis=0, concat_axis=0, tiled=True)
    return moved.reshape(DEVICES * width, FEAT)


def pass_rims(rims):
    arrived = []
    for turn in range(4):
        axis = ("sub", "blk")[turn // 2]
        count = lax.axis_size(axis)
        pairs = []
        for i in range(turn % 2, count, 2):
            j = (i + 1) % count
            pairs += [(i, j), (j, i)]
        arrived.append(lax.ppermute(rims[turn], axis, pairs))
    return arrived


def bind(body, section):
    def bound(*refs):
        body(section, *refs)

    return bound


def per_device(fields, metric, neighbours, mortar_sends, mortar_pairs):
    select = jnp.asarray(face_rows(), BF16)
    derive = jnp.asarray(derivative_pieces())
    metric = metric.reshape(1, ELEMS)
    whole = ((4, NODES, ELEMS), F32, "v")
    rim = ((RIM, FEAT), F32, "v")
    table = ((FACT_ROWS, 2 * FACES), F32, "h")
    pad = pltpu.VMEM((3 * P_SIZE, 8, FACES), F32)
    wide = pltpu.VMEM((3 * P_SIZE, 8, 2 * FACES), F32)
    narrow = pltpu.VMEM((FEAT, FACES), F32)
    broad = pltpu.VMEM((FEAT, 2 * FACES), F32)

    def far(*arrays):
        return tuple((array, "h") for array in arrays)

    def near(*arrays):
        return tuple((array, "v") for array in arrays)

    (owned,) = call(partner_body, [((DEVICES, FEAT), F32, "v")], near(mortar_pairs))
    owned = exchange(owned, 1)
    keys, facts, own, info, mortars = call(
        tables_body,
        [
            ((KEY_ROWS, ELEMS), F32, "h"),
            table,
            ((48, FACES), F32, "h"),
            ((16, 2 * FACES), F32, "v"),
            ((FEAT, 2 * FACES), F32, "v"),
        ],
        near(neighbours, mortar_sends, metric, fields, select),
        scratch=[pltpu.VMEM((2, 16, ELEMS), F32), pad],
    )
    routes, payload = call(
        route_body,
        [((8, 2 * FACES), F32, "h"), ((SLOTS, FEAT), F32, "v")],
        near(owned, info, mortars),
    )
    part, arrived = fields, None
    packed = ((ROUTES + 8, 2 * FACES), F32, "v")
    for section in range(3):
        arrivals = exchange(payload, 4)
        edge = near(part) + far(keys) + near(select)
        if section == 0:
            current = near(fields)
            rims = call(bind(edge_body, section), [rim] * 4, edge, flops=5e7)
        else:
            current, *rims = call(
                bind(edge_body, section), [whole] + [rim] * 4, edge + far(arrived), flops=5e7
            )
            current = near(current, fields)
        rims = pass_rims(rims)
        (after,) = call(
            bind(inner_body, section),
            [whole],
            current + near(select, derive, neighbours) + far(keys, own),
            scratch=[pad, narrow],
            flops=8e8,
        )
        part, held = call(
            bind(rim_body, section),
            [whole, packed],
            near(after, *rims, select) + far(keys, facts, routes),
            scratch=[] if section == 2 else [pad],
        )
        if section < 2:
            arrived, payload = call(
                bind(flux_body, section),
                [((FEAT, FACES), F32, "h"), ((SLOTS, FEAT), F32, "v")],
                near(arrivals, held),
                scratch=[pad, wide, broad],
            )
    (result,) = call(
        last_body,
        [whole],
        near(arrivals, held, part) + far(keys) + near(select),
        scratch=[pad, wide, narrow],
    )
    return result


def solution(mesh):
    placed = (
        P(None, None, ("blk", "sub")),
        P(("blk", "sub")),
        P(None, ("blk", "sub")),
        P(None, ("blk", "sub")),
        P(None, ("blk", "sub")),
    )
    return jax.shard_map(
        per_device,
        mesh=mesh,
        in_specs=placed,
        out_specs=P(None, None, ("blk", "sub")),
        check_vma=False,
    )
```

```python
import jax
import jax.numpy as jnp
import numpy as np
from jax import lax
from jax.experimental import pallas as pl
from jax.experimental.pallas import tpu as pltpu
from jax.sharding import PartitionSpec as P

P_SIZE = 6
SUB = 16
IFD = 64
RIM = 32
NODES = 216
ELEMS = 256
FACES = 2 * IFD
SLOTS = 512
DEVICES = 128
TR = 40
PROJECT = 48
METRIC = 96
FACT_ROWS = 104
ROUTES = FACT_ROWS + 128
NEAR, RIM_OUT, RIM_IN, ROTOR, STATOR, SCALE, KEY_ROWS = 0, 6, 10, 14, 15, 16, 24
FEAT = 128
DT_STEP = 0.01
F32 = jnp.float32
BF16 = jnp.bfloat16
VMEM_BYTES = 24 * 1024 * 1024


def legendre_columns(points, npts):
    legendre = np.zeros((npts, npts))
    legendre[:, 0] = 1.0
    legendre[:, 1] = points
    for k in range(2, npts):
        legendre[:, k] = (
            (2 * k - 1) * points * legendre[:, k - 1] - (k - 1) * legendre[:, k - 2]
        ) / k
    return legendre


def basis_tables(npts):
    order = npts - 1
    points = -np.cos(np.pi * np.arange(npts) / order)
    for iteration in range(60):
        legendre = legendre_columns(points, npts)
        points = points - (points * legendre[:, order] - legendre[:, order - 1]) / (
            npts * legendre[:, order]
        )
    legendre = legendre_columns(points, npts)
    weights = 2.0 / (order * npts * legendre[:, order] ** 2)
    separation = points[:, None] - points[None, :] + np.eye(npts)
    derivative = legendre[:, order][:, None] / legendre[:, order][None, :] / separation
    derivative = derivative * (1.0 - np.eye(npts))
    derivative[0, 0] = -order * npts / 4.0
    derivative[order, order] = order * npts / 4.0
    return (points, weights, derivative)


POINTS, WEIGHTS, DERIVATIVE = basis_tables(P_SIZE)
LIFT = float(1.0 / WEIGHTS[0])
SECTIONS = (
    (0.0, 1.0, DT_STEP),
    (0.75, 0.25, 0.25 * DT_STEP),
    (1.0 / 3.0, 2.0 / 3.0, 2.0 / 3.0 * DT_STEP),
)


def face_rows():
    picks = np.zeros((6 * TR, NODES))
    for face in range(6):
        fixed = 0 if face % 2 == 0 else P_SIZE - 1
        for a in range(P_SIZE):
            for b in range(P_SIZE):
                place = [a, b]
                place.insert(face // 2, fixed)
                node = (place[0] * P_SIZE + place[1]) * P_SIZE + place[2]
                picks[face * TR + a * P_SIZE + b, node] = 1.0
    return picks


def derivative_pieces():
    one = np.eye(P_SIZE)
    square = np.eye(P_SIZE * P_SIZE)
    whole = [
        np.kron(DERIVATIVE, square),
        np.kron(one, np.kron(DERIVATIVE, one)),
        np.kron(square, DERIVATIVE),
    ]
    pieces = []
    for matrix in whole:
        matrix = matrix.astype(np.float32)
        high = matrix.astype(jnp.bfloat16)
        pieces.append(high)
        pieces.append((matrix - high.astype(np.float32)).astype(jnp.bfloat16))
    return np.stack(pieces)


def nn(a, b):
    return lax.dot_general(a, b, (((1,), (0,)), ((), ())), preferred_element_type=F32)


def nt(a, b):
    return lax.dot_general(a, b, (((1,), (1,)), ((), ())), preferred_element_type=F32)


def tn(a, b):
    return lax.dot_general(a, b, (((0,), (0,)), ((), ())), preferred_element_type=F32)


def halves(x):
    high = x.astype(BF16)
    return high, (x - high.astype(F32)).astype(BF16)


def nn2(exact, x):
    high, low = halves(x)
    return nn(exact, high) + nn(exact, low)


def mark(cond):
    return jnp.where(cond, 1.0, 0.0)


def iota(shape, dim):
    return lax.broadcasted_iota(jnp.int32, shape, dim)


def my_device():
    return lax.axis_index("blk") * 8 + lax.axis_index("sub")


def even_place(turn):
    return (lax.axis_index(("sub", "blk")[turn]) & 1) == 0


class Fetched:
    def __init__(self, copy, buffer):
        self.copy, self.buffer, self.here = copy, buffer, False

    def __getitem__(self, key):
        if not self.here:
            self.copy.wait()
            self.here = True
        return self.buffer[key]


def call(body, outs, args, scratch=(), flops=1e8, moved=2e6):
    far_in = [i for i, (_, space) in enumerate(args) if space == "h"]
    far_out = [i for i, (_, _, space) in enumerate(outs) if space == "h"]
    own = [pltpu.VMEM(args[i][0].shape, args[i][0].dtype) for i in far_in]
    own += [pltpu.VMEM(outs[i][0], outs[i][1]) for i in far_out]
    count = len(far_in) + len(far_out)

    def kernel(*refs):
        refs = list(refs)
        ins, refs = refs[: len(args)], refs[len(args) :]
        results, refs = refs[: len(outs)], refs[len(outs) :]
        extra, refs = refs[: len(scratch)], refs[len(scratch) :]
        sems = refs[-1] if count else None
        for n, i in enumerate(far_in):
            copy = pltpu.make_async_copy(ins[i], refs[n], sems.at[n])
            copy.start()
            ins[i] = Fetched(copy, refs[n])
        shown = list(results)
        for n, i in enumerate(far_out):
            shown[i] = refs[len(far_in) + n]
        body(*ins, *shown, *extra)
        for i in far_in:
            if not ins[i].here:
                ins[i].copy.wait()
        copies = []
        for n, i in enumerate(far_out):
            spot = len(far_in) + n
            copies.append(pltpu.make_async_copy(refs[spot], results[i], sems.at[spot]))
            copies[-1].start()
        for copy in copies:
            copy.wait()

    spaces = {"h": pltpu.HBM, "v": pltpu.VMEM}
    return pl.pallas_call(
        kernel,
        out_shape=[jax.ShapeDtypeStruct(o[0], o[1]) for o in outs],
        in_specs=[pl.BlockSpec(memory_space=spaces[space]) for _, space in args],
        out_specs=[pl.BlockSpec(memory_space=spaces[o[2]]) for o in outs],
        scratch_shapes=list(scratch)
        + own
        + ([pltpu.SemaphoreType.DMA((count,))] if count else []),
        compiler_params=pltpu.CompilerParams(vmem_limit_bytes=VMEM_BYTES),
        cost_estimate=pl.CostEstimate(
            flops=int(flops), bytes_accessed=int(moved), transcendentals=0
        ),
    )(*[array for array, _ in args])


def spread(values, pad, width):
    for group in range(3 * P_SIZE):
        c, i = divmod(group, P_SIZE)
        start = c * TR + i * P_SIZE
        pad[group, 0:P_SIZE, 0:width] = values[start : start + P_SIZE, :]


def to_mortars(facts, pad, out, comps, add):
    for half in range(2):
        lanes = slice(half * FACES, (half + 1) * FACES)
        for c in comps:
            for m in range(P_SIZE):
                total = facts[m : m + 1, lanes] * pad[c * P_SIZE, :, 0:FACES]
                for i in range(1, P_SIZE):
                    row = i * 8 + m
                    total += facts[row : row + 1, lanes] * pad[c * P_SIZE + i, :, 0:FACES]
                start = c * TR + m * P_SIZE
                rows = slice(start, start + P_SIZE)
                if add:
                    out[rows, lanes] += total[0:P_SIZE, :]
                else:
                    out[rows, lanes] = total[0:P_SIZE, :]


def outgoing(traces4, traces5):
    blank = jnp.zeros((FEAT - 3 * TR, ELEMS), F32)
    out4 = jnp.concatenate([traces4[0] - traces4[3], traces4[1], traces4[2], blank], axis=0)
    out5 = jnp.concatenate([traces5[0] + traces5[3], traces5[1], traces5[2], blank], axis=0)
    return out4, out5


def at_faces(rows4, rows5, members):
    high5, low5 = halves(rows5)
    high4, low4 = halves(rows4)
    rotor = nt(high5, members) + nt(low5, members)
    stator = nt(high4, members) + nt(low4, members)
    return jnp.where(iota((FEAT, FACES), 1) < IFD, rotor, stator)


def at_elements(values, members):
    rotor_side = iota((FEAT, FACES), 1) < IFD
    to5 = nn2b(jnp.where(rotor_side, values, 0.0), members)
    to4 = nn2b(jnp.where(rotor_side, 0.0, values), members)
    return to4, to5


def nn2b(x, exact):
    high, low = halves(x)
    return nn(high, exact) + nn(low, exact)


def comp(rows, c):
    return rows[c * TR : (c + 1) * TR, :]


def partner_body(pairs, out):
    row = iota((DEVICES, ELEMS), 0)
    total = None
    for mine, other in ((0, 1), (1, 0)):
        entry = pairs[mine : mine + 1, :]
        partner = pairs[other : other + 1, :]
        owner_row = mark(row == (entry >> 2)).astype(BF16)
        spot = entry & 3
        facts = jnp.where(row == spot, (partner >> 2) + 1, 0) + jnp.where(
            row == spot + 4, partner & 3, 0
        )
        term = nt(owner_row, facts.astype(F32).astype(BF16))
        total = term if total is None else total + term
    out[...] = total


def picked(keys, row, count):
    return mark(iota((count, ELEMS), 0).astype(F32) == keys[row : row + 1, :]).astype(BF16)


def member_picks(keys):
    number = iota((FACES, ELEMS), 0).astype(F32)
    rotor = number == keys[ROTOR : ROTOR + 1, :]
    stator = number == keys[STATOR : STATOR + 1, :]
    return mark(rotor | stator).astype(BF16)


def tables_body(
    neighbours, sends, metric, fields, select,
    keys, facts, own, info, mortars,
    rows, pad,
):
    me = my_device()
    nb = neighbours[...]
    face_id = iota((6, ELEMS), 0)
    remote = (nb >= 0) & ((nb >> 8) != me)
    here = (nb >= 0) & ((nb >> 8) == me)
    spot = nb & 255
    flags = jnp.where(face_id < 4, mark(remote), mark(nb == -2))
    rows[...] = jnp.zeros(rows.shape, F32)
    rows[0, 0:6, :] = flags
    rows[1, 0:6, :] = spot.astype(F32)
    flag_rows = rows[0].astype(BF16)
    spot_rows = rows[1].astype(BF16)
    down = iota((ELEMS, ELEMS), 0)
    across = iota((ELEMS, ELEMS), 1)
    before = mark(down < across).astype(BF16)
    same = mark(down == across).astype(BF16)
    rank = nn(flag_rows, before)
    spot_down = jnp.where(nt(same, flag_rows) > 0.5, nt(same, spot_rows), 1e4)
    keys[...] = jnp.zeros(keys.shape, F32)
    keys[NEAR : NEAR + 6, :] = jnp.where(here, spot, -1).astype(F32)
    for face in range(4):
        live = flags[face : face + 1, :] > 0.5
        order = jnp.sum(
            mark(spot_down[:, face : face + 1] < rows[1, face : face + 1, :]),
            axis=0,
            keepdims=True,
        )
        place = RIM_OUT + face
        keys[place : place + 1, :] = jnp.where(live, rank[face : face + 1, :], -1.0)
        place = RIM_IN + face
        keys[place : place + 1, :] = jnp.where(live, order, -1.0)
    keys[ROTOR : ROTOR + 1, :] = jnp.where(flags[5:6, :] > 0.5, rank[5:6, :], -1.0)
    keys[STATOR : STATOR + 1, :] = jnp.where(flags[4:5, :] > 0.5, rank[4:5, :] + IFD, -1.0)
    keys[SCALE : SCALE + 1, :] = metric[...]
    member = member_picks(keys)
    face_of = sends[0:1, :]
    lo_of = sends[1:2, :]
    lane_of = jnp.where(face_of >= 0, face_of + jnp.where(lo_of > 0, FACES, 0), -1)
    slot_lane = mark(iota((2 * FACES, SLOTS), 0) == lane_of).astype(BF16)
    kind = iota((16, SLOTS), 0)
    number = iota((16, SLOTS), 1)
    lines = jnp.where(kind == 0, number >> 2, 0) + jnp.where(kind == 1, number & 3, 0)
    lines += jnp.where(kind == 2, lo_of, 0) + jnp.where(kind == 3, sends[2:3, :], 0)
    found = nt(lines.astype(F32).astype(BF16), slot_lane)
    info[...] = found
    lo = found[2:3, :]
    width = found[3:4, :] - lo
    point = iota((8, 2 * FACES), 0)
    unit = jnp.zeros((8, 2 * FACES), F32)
    weight = jnp.zeros((8, 2 * FACES), F32)
    for m in range(P_SIZE):
        unit = jnp.where(point == m, float((POINTS[m] + 1.0) * 0.5), unit)
        weight = jnp.where(point == m, float(0.5 * WEIGHTS[m] / SUB), weight)
    spots = (lo + width * unit) * (2.0 / SUB) - 1.0
    for i in range(P_SIZE):
        product = None
        for j in range(P_SIZE):
            if j != i:
                term = (spots - float(POINTS[j])) * float(1.0 / (POINTS[i] - POINTS[j]))
                product = term if product is None else product * term
        facts[i * 8 : i * 8 + 8, :] = product
        start = PROJECT + i * 8
        facts[start : start + 8, :] = product * weight * width * float(1.0 / WEIGHTS[i])
    for i in range(P_SIZE):
        for k in range(P_SIZE):
            start = PROJECT + i * 8
            term = facts[start : start + 8, :] * facts[k * 8 : k * 8 + 8, :]
            term = jnp.sum(term, axis=0, keepdims=True)
            own[i * 8 + k : i * 8 + k + 1, :] = term[:, 0:FACES] + term[:, FACES:]
    scale = jnp.broadcast_to(metric[...], (16, ELEMS))
    high, rest = scale.astype(BF16), scale - scale.astype(BF16).astype(F32)
    middle, low = halves(rest)
    scale = nt(high, member) + nt(middle, member) + nt(low, member)
    facts[METRIC:FACT_ROWS, :] = jnp.concatenate([scale[0:8, :]] * 2, axis=1)
    traces = [nn2(select[4 * TR : 6 * TR, :], fields[c]) for c in range(4)]
    out4, out5 = outgoing([t[:TR] for t in traces], [t[TR:] for t in traces])
    spread(at_faces(out4, out5, member), pad, FACES)
    mortars[...] = jnp.zeros((FEAT, 2 * FACES), F32)
    to_mortars(facts, pad, mortars, (0, 1, 2), False)


def slot_picks(row):
    return mark(iota((SLOTS, 2 * FACES), 0).astype(F32) == row).astype(BF16)


def send_rows(exact, values):
    high, low = halves(values)
    return nt(exact, high) + nt(exact, low)


def route_body(facts, info, mortars, routes, payload):
    owner = info[0:1, :]
    turn = info[1:2, :]
    owner_pick = mark(iota((DEVICES, 2 * FACES), 0).astype(F32) == owner).astype(BF16)
    found = tn(facts[...].astype(BF16), owner_pick)
    partner = jnp.zeros((1, 2 * FACES), F32)
    other = jnp.zeros((1, 2 * FACES), F32)
    for t in range(4):
        partner = jnp.where(turn == t, found[t : t + 1, :], partner)
        other = jnp.where(turn == t, found[4 + t : 5 + t, :], other)
    partner = partner - 1.0
    kind = iota((16, 2 * FACES), 0)
    lines = jnp.where(kind == 0, partner, 0.0) + jnp.where(kind == 1, owner, 0.0)
    lines += jnp.where(kind == 2, turn, 0.0) + jnp.where(kind == 3, other, 0.0)
    same = mark(iota((2 * FACES, 2 * FACES), 0) == iota((2 * FACES, 2 * FACES), 1)).astype(BF16)
    down = nt(same, lines.astype(BF16))
    partner_down = down[:, 0:1]
    together = partner_down == partner
    mine_down = down[:, 1:2] * 4.0 + down[:, 2:3]
    theirs_down = down[:, 1:2] * 4.0 + down[:, 3:4]
    mine = owner * 4.0 + turn
    theirs = owner * 4.0 + other
    ahead = jnp.sum(mark(together & (mine_down < mine)), axis=0, keepdims=True)
    behind = jnp.sum(mark(together & (theirs_down < theirs)), axis=0, keepdims=True)
    kind = iota((8, 2 * FACES), 0)
    routes[...] = partner * 4.0 + jnp.where(kind == 0, ahead, behind)
    payload[...] = send_rows(slot_picks(partner * 4.0 + ahead), mortars[...])


def placed(picks, x):
    high, low = halves(x)
    return tn(picks, high) + tn(picks, low)


def place_interface(part, arrived, keys, select):
    picks = select[4 * TR : 6 * TR, :]
    to4, to5 = at_elements(arrived[...], member_picks(keys))
    result = []
    for c in range(4):
        source = (0, 1, 2, 0)[c]
        sign5 = -1.0 if c == 3 else 1.0
        stack = jnp.concatenate([comp(to4, source), sign5 * comp(to5, source)], axis=0)
        result.append(part[c] + placed(picks, stack))
    return result


def characteristics(traces, faces):
    blank = jnp.zeros((FEAT - 3 * TR, ELEMS), F32)
    leaving, inside = [], []
    for face in range(faces):
        sign = 1.0 if face % 2 else -1.0
        cut = [t[face * TR : (face + 1) * TR, :] for t in traces]
        along = face // 2
        tangent = [cut[1 + c] for c in range(3) if c != along]
        normal = sign * cut[1 + along]
        leaving.append(halves(jnp.concatenate([cut[0] + normal] + tangent + [blank], axis=0)))
        inside.append(jnp.concatenate([cut[0] - normal] + tangent + [blank], axis=0))
    return leaving, inside


def edge_body(section, *refs):
    part, keys, select = refs[:3]
    if section == 0:
        fields = [part[c] for c in range(4)]
        rims = refs[3:]
    else:
        arrived, whole = refs[3:5]
        fields = place_interface(part, arrived, keys, select)
        rims = refs[5:]
        for c in range(4):
            whole[c] = fields[c]
    leaving, _ = characteristics([nn2(select[0 : 4 * TR, :], x) for x in fields], 4)
    parts = []
    for face in range(4):
        pick = picked(keys, RIM_OUT + face, RIM)
        parts.append(nt(pick, leaving[face][0]) + nt(pick, leaving[face][1]))
    for turn, (down, up) in enumerate((parts[:2], parts[2:])):
        even = even_place(turn)
        rims[2 * turn][...] = jnp.where(even, up, down)
        rims[2 * turn + 1][...] = jnp.where(even, down, up)


def inner_body(section, *refs):
    whole, refs = refs[0], refs[1:]
    if section:
        first, refs = refs[0], refs[1:]
    select, derive, neighbours, keys, own, after, pad, mixed = refs
    keep, stay, rate = SECTIONS[section]
    fields = [whole[c] for c in range(4)]
    high, low = zip(*[halves(x) for x in fields])
    sel = select[...]
    traces = [nn(sel, high[c]) + nn(sel, low[c]) for c in range(4)]
    leaving, inside = characteristics(traces, 6)
    members = member_picks(keys)
    spread(at_faces(inside[4], inside[5], members), pad, FACES)
    mixed[...] = jnp.zeros(mixed.shape, F32)
    for c in range(3):
        for i in range(P_SIZE):
            total = own[i * 8 : i * 8 + 1, :] * pad[c * P_SIZE]
            for k in range(1, P_SIZE):
                row = i * 8 + k
                total += own[row : row + 1, :] * pad[c * P_SIZE + k]
            start = c * TR + i * P_SIZE
            mixed[start : start + P_SIZE, :] = -total[0:P_SIZE, :]
    to4, to5 = at_elements(mixed[...], members)
    terms = []
    for face in range(6):
        pick = picked(keys, NEAR + face, ELEMS)
        arriving = nn(leaving[face ^ 1][0], pick) + nn(leaving[face ^ 1][1], pick)
        term = 0.5 * (arriving - inside[face])
        if face >= 4:
            term = jnp.where(neighbours[face : face + 1, :] == -2, 0.0, term)
            term = term + (to4, to5)[face - 4]
        terms.append(term)
    scale = keys[SCALE : SCALE + 1, :] * rate
    for c in range(4):
        pieces = []
        for face in range(6):
            along = face // 2
            if c == 0:
                pieces.append(comp(terms[face], 0))
            elif c == 1 + along:
                pieces.append((-1.0 if face % 2 else 1.0) * comp(terms[face], 0))
            else:
                tangents = [k for k in range(3) if k != along]
                pieces.append(comp(terms[face], 1 + tangents.index(c - 1)))
        surface = placed(sel, jnp.concatenate(pieces, axis=0))
        if c == 0:
            pairs = ((0, 1), (1, 2), (2, 3))
        else:
            pairs = ((c - 1, 0),)
        volume = None
        for direction, source in pairs:
            big, small = derive[2 * direction], derive[2 * direction + 1]
            term = nn(big, high[source]) + nn(big, low[source]) + nn(small, high[source])
            volume = term if volume is None else volume + term
        base = stay * fields[c]
        if keep:
            base = base + keep * first[c]
        after[c] = base + scale * (LIFT * surface - volume)


def rim_body(section, *refs):
    before, r0, r1, r2, r3, select, keys, facts, routes = refs[:9]
    last = section == 2
    after, pack = refs[9:11]
    scale = keys[SCALE : SCALE + 1, :] * (SECTIONS[section][2] * LIFT)
    terms = []
    terms = []
    got = []
    for turn, (one, two) in enumerate(((r0, r1), (r2, r3))):
        even = even_place(turn)
        got.append(jnp.where(even, two[...], one[...]))
        got.append(jnp.where(even, one[...], two[...]))
    for face, value in enumerate(got):
        high, low = halves(value)
        pick = picked(keys, RIM_IN + face, RIM)
        terms.append(0.5 * (tn(high, pick) + tn(low, pick)))
    fields = []
    for c in range(4):
        pieces = []
        for face in range(4):
            along = face // 2
            if c == 0:
                pieces.append(comp(terms[face], 0))
            elif c == 1 + along:
                pieces.append((-1.0 if face % 2 else 1.0) * comp(terms[face], 0))
            else:
                tangents = [k for k in range(3) if k != along]
                pieces.append(comp(terms[face], 1 + tangents.index(c - 1)))
        value = before[c] + scale * placed(select[0 : 4 * TR, :], jnp.concatenate(pieces, axis=0))
        after[c] = value
        fields.append(value)
    pack[0:FACT_ROWS, :] = facts[...]
    pack[ROUTES : ROUTES + 8, :] = routes[...]
    if not last:
        pad = refs[11]
        traces = [nn2(select[4 * TR : 6 * TR, :], x) for x in fields]
        out4, out5 = outgoing([t[:TR] for t in traces], [t[TR:] for t in traces])
        spread(at_faces(out4, out5, member_picks(keys)), pad, FACES)
        mortars = pack.at[FACT_ROWS:ROUTES, :]
        mortars[...] = jnp.zeros((FEAT, 2 * FACES), F32)
        to_mortars(facts, pad, mortars, (0, 1, 2), False)


def arrive(section, arrivals, held, pad, wide, out):
    high, low = halves(arrivals[...])
    pick = slot_picks(held[ROUTES + 1 : ROUTES + 2, :])
    spread(tn(high, pick) + tn(low, pick), wide, 2 * FACES)
    scale = held[METRIC : METRIC + 1, 0:FACES] * (SECTIONS[section][2] * LIFT)
    out[...] = jnp.zeros(out.shape, F32)
    for c in range(3):
        for i in range(P_SIZE):
            total = None
            for half in range(2):
                lanes = slice(half * FACES, (half + 1) * FACES)
                for m in range(P_SIZE):
                    row = PROJECT + i * 8 + m
                    term = held[row : row + 1, lanes] * wide[c * P_SIZE + m, :, lanes]
                    total = term if total is None else total + term
            total = total * scale
            pad[c * P_SIZE + i] = total
            start = c * TR + i * P_SIZE
            out[start : start + P_SIZE, :] = total[0:P_SIZE, :]


def flux_body(section, arrivals, held, arrived, payload, pad, wide, mixed):
    arrive(section, arrivals, held, pad, wide, arrived)
    mixed[...] = held[FACT_ROWS:ROUTES, :]
    to_mortars(held, pad, mixed, (1, 2), True)
    payload[...] = send_rows(slot_picks(held[ROUTES : ROUTES + 1, :]), mixed[...])


def last_body(arrivals, held, part, keys, select, after, pad, wide, arrived):
    arrive(2, arrivals, held, pad, wide, arrived)
    result = place_interface(part, arrived, keys, select)
    for c in range(4):
        after[c] = result[c]


def exchange(rows, width):
    whole = rows.reshape(DEVICES, width, FEAT)
    moved = lax.all_to_all(whole, ("blk", "sub"), split_axis=0, concat_axis=0, tiled=True)
    return moved.reshape(DEVICES * width, FEAT)


def pass_rims(rims):
    arrived = []
    blks, subs = lax.axis_size("blk"), lax.axis_size("sub")
    for turn in range(4):
        pairs = []
        for blk in range(blks):
            for sub in range(subs):
                at, count = ((sub, subs), (blk, blks))[turn // 2]
                other = at + 1 if at % 2 == turn % 2 else at - 1
                there = [blk, sub]
                if 0 <= other < count:
                    there[1 - turn // 2] = other
                else:
                    there[turn // 2] ^= 1
                pairs.append((blk * subs + sub, there[0] * subs + there[1]))
        arrived.append(lax.ppermute(rims[turn], ("blk", "sub"), pairs))
    return arrived


def bind(body, section):
    def bound(*refs):
        body(section, *refs)

    return bound


def per_device(fields, metric, neighbours, mortar_sends, mortar_pairs):
    select = jnp.asarray(face_rows(), BF16)
    derive = jnp.asarray(derivative_pieces())
    metric = metric.reshape(1, ELEMS)
    whole = ((4, NODES, ELEMS), F32, "v")
    rim = ((RIM, FEAT), F32, "v")
    table = ((FACT_ROWS, 2 * FACES), F32, "h")
    pad = pltpu.VMEM((3 * P_SIZE, 8, FACES), F32)
    wide = pltpu.VMEM((3 * P_SIZE, 8, 2 * FACES), F32)
    narrow = pltpu.VMEM((FEAT, FACES), F32)
    broad = pltpu.VMEM((FEAT, 2 * FACES), F32)

    def far(*arrays):
        return tuple((array, "h") for array in arrays)

    def near(*arrays):
        return tuple((array, "v") for array in arrays)

    (owned,) = call(partner_body, [((DEVICES, FEAT), F32, "v")], near(mortar_pairs))
    owned = exchange(owned, 1)
    keys, facts, own, info, mortars = call(
        tables_body,
        [
            ((KEY_ROWS, ELEMS), F32, "h"),
            table,
            ((48, FACES), F32, "h"),
            ((16, 2 * FACES), F32, "v"),
            ((FEAT, 2 * FACES), F32, "v"),
        ],
        near(neighbours, mortar_sends, metric, fields, select),
        scratch=[pltpu.VMEM((2, 16, ELEMS), F32), pad],
    )
    routes, payload = call(
        route_body,
        [((8, 2 * FACES), F32, "h"), ((SLOTS, FEAT), F32, "v")],
        near(owned, info, mortars),
    )
    part, arrived = fields, None
    packed = ((ROUTES + 8, 2 * FACES), F32, "v")
    for section in range(3):
        arrivals = exchange(payload, 4)
        edge = near(part) + far(keys) + near(select)
        if section == 0:
            current = near(fields)
            rims = call(bind(edge_body, section), [rim] * 4, edge, flops=5e7)
        else:
            current, *rims = call(
                bind(edge_body, section), [whole] + [rim] * 4, edge + far(arrived), flops=5e7
            )
            current = near(current, fields)
        rims = pass_rims(rims)
        (after,) = call(
            bind(inner_body, section),
            [whole],
            current + near(select, derive, neighbours) + far(keys, own),
            scratch=[pad, narrow],
            flops=8e8,
        )
        part, held = call(
            bind(rim_body, section),
            [whole, packed],
            near(after, *rims, select) + far(keys, facts, routes),
            scratch=[] if section == 2 else [pad],
        )
        if section < 2:
            arrived, payload = call(
                bind(flux_body, section),
                [((FEAT, FACES), F32, "h"), ((SLOTS, FEAT), F32, "v")],
                near(arrivals, held),
                scratch=[pad, wide, broad],
            )
    (result,) = call(
        last_body,
        [whole],
        near(arrivals, held, part) + far(keys) + near(select),
        scratch=[pad, wide, narrow],
    )
    return result


def solution(mesh):
    placed = (
        P(None, None, ("blk", "sub")),
        P(("blk", "sub")),
        P(None, ("blk", "sub")),
        P(None, ("blk", "sub")),
        P(None, ("blk", "sub")),
    )
    return jax.shard_map(
        per_device,
        mesh=mesh,
        in_specs=placed,
        out_specs=P(None, None, ("blk", "sub")),
        check_vma=False,
    )
```

```python
import jax
import jax.numpy as jnp
import numpy as np
from jax import lax
from jax.experimental import pallas as pl
from jax.experimental.pallas import tpu as pltpu
from jax.sharding import PartitionSpec as P

P_SIZE = 6
SUB = 16
IFD = 64
RIM = 32
NODES = 216
ELEMS = 256
FACES = 2 * IFD
SLOTS = 512
DEVICES = 128
TR = 40
PROJECT = 48
METRIC = 96
FACT_ROWS = 104
ROUTES = FACT_ROWS + 128
NEAR, RIM_OUT, RIM_IN, ROTOR, STATOR, SCALE, KEY_ROWS = 0, 6, 10, 14, 15, 16, 24
FEAT = 128
DT_STEP = 0.01
F32 = jnp.float32
BF16 = jnp.bfloat16
VMEM_BYTES = 24 * 1024 * 1024


def legendre_columns(points, npts):
    legendre = np.zeros((npts, npts))
    legendre[:, 0] = 1.0
    legendre[:, 1] = points
    for k in range(2, npts):
        legendre[:, k] = (
            (2 * k - 1) * points * legendre[:, k - 1] - (k - 1) * legendre[:, k - 2]
        ) / k
    return legendre


def basis_tables(npts):
    order = npts - 1
    points = -np.cos(np.pi * np.arange(npts) / order)
    for iteration in range(60):
        legendre = legendre_columns(points, npts)
        points = points - (points * legendre[:, order] - legendre[:, order - 1]) / (
            npts * legendre[:, order]
        )
    legendre = legendre_columns(points, npts)
    weights = 2.0 / (order * npts * legendre[:, order] ** 2)
    separation = points[:, None] - points[None, :] + np.eye(npts)
    derivative = legendre[:, order][:, None] / legendre[:, order][None, :] / separation
    derivative = derivative * (1.0 - np.eye(npts))
    derivative[0, 0] = -order * npts / 4.0
    derivative[order, order] = order * npts / 4.0
    return (points, weights, derivative)


POINTS, WEIGHTS, DERIVATIVE = basis_tables(P_SIZE)
LIFT = float(1.0 / WEIGHTS[0])
SECTIONS = (
    (0.0, 1.0, DT_STEP),
    (0.75, 0.25, 0.25 * DT_STEP),
    (1.0 / 3.0, 2.0 / 3.0, 2.0 / 3.0 * DT_STEP),
)


def face_rows():
    picks = np.zeros((6 * TR, NODES))
    for face in range(6):
        fixed = 0 if face % 2 == 0 else P_SIZE - 1
        for a in range(P_SIZE):
            for b in range(P_SIZE):
                place = [a, b]
                place.insert(face // 2, fixed)
                node = (place[0] * P_SIZE + place[1]) * P_SIZE + place[2]
                picks[face * TR + a * P_SIZE + b, node] = 1.0
    return picks


def derivative_pieces():
    one = np.eye(P_SIZE)
    square = np.eye(P_SIZE * P_SIZE)
    whole = [
        np.kron(DERIVATIVE, square),
        np.kron(one, np.kron(DERIVATIVE, one)),
        np.kron(square, DERIVATIVE),
    ]
    pieces = []
    for matrix in whole:
        matrix = matrix.astype(np.float32)
        high = matrix.astype(jnp.bfloat16)
        pieces.append(high)
        pieces.append((matrix - high.astype(np.float32)).astype(jnp.bfloat16))
    return np.stack(pieces)


def nn(a, b):
    return lax.dot_general(a, b, (((1,), (0,)), ((), ())), preferred_element_type=F32)


def nt(a, b):
    return lax.dot_general(a, b, (((1,), (1,)), ((), ())), preferred_element_type=F32)


def tn(a, b):
    return lax.dot_general(a, b, (((0,), (0,)), ((), ())), preferred_element_type=F32)


def halves(x):
    high = x.astype(BF16)
    return high, (x - high.astype(F32)).astype(BF16)


def nn2(exact, x):
    high, low = halves(x)
    return nn(exact, high) + nn(exact, low)


def mark(cond):
    return jnp.where(cond, 1.0, 0.0)


def iota(shape, dim):
    return lax.broadcasted_iota(jnp.int32, shape, dim)


def my_device():
    return lax.axis_index("blk") * 8 + lax.axis_index("sub")


def even_place(turn):
    return (lax.axis_index(("sub", "blk")[turn]) & 1) == 0


class Fetched:
    def __init__(self, copy, buffer):
        self.copy, self.buffer, self.here = copy, buffer, False

    def __getitem__(self, key):
        if not self.here:
            self.copy.wait()
            self.here = True
        return self.buffer[key]


def call(body, outs, args, scratch=(), flops=1e8, moved=2e6):
    far_in = [i for i, (_, space) in enumerate(args) if space == "h"]
    far_out = [i for i, (_, _, space) in enumerate(outs) if space == "h"]
    own = [pltpu.VMEM(args[i][0].shape, args[i][0].dtype) for i in far_in]
    own += [pltpu.VMEM(outs[i][0], outs[i][1]) for i in far_out]
    count = len(far_in) + len(far_out)

    def kernel(*refs):
        refs = list(refs)
        ins, refs = refs[: len(args)], refs[len(args) :]
        results, refs = refs[: len(outs)], refs[len(outs) :]
        extra, refs = refs[: len(scratch)], refs[len(scratch) :]
        sems = refs[-1] if count else None
        for n, i in enumerate(far_in):
            copy = pltpu.make_async_copy(ins[i], refs[n], sems.at[n])
            copy.start()
            ins[i] = Fetched(copy, refs[n])
        shown = list(results)
        for n, i in enumerate(far_out):
            shown[i] = refs[len(far_in) + n]
        body(*ins, *shown, *extra)
        for i in far_in:
            if not ins[i].here:
                ins[i].copy.wait()
        copies = []
        for n, i in enumerate(far_out):
            spot = len(far_in) + n
            copies.append(pltpu.make_async_copy(refs[spot], results[i], sems.at[spot]))
            copies[-1].start()
        for copy in copies:
            copy.wait()

    spaces = {"h": pltpu.HBM, "v": pltpu.VMEM}
    return pl.pallas_call(
        kernel,
        out_shape=[jax.ShapeDtypeStruct(o[0], o[1]) for o in outs],
        in_specs=[pl.BlockSpec(memory_space=spaces[space]) for _, space in args],
        out_specs=[pl.BlockSpec(memory_space=spaces[o[2]]) for o in outs],
        scratch_shapes=list(scratch)
        + own
        + ([pltpu.SemaphoreType.DMA((count,))] if count else []),
        compiler_params=pltpu.CompilerParams(vmem_limit_bytes=VMEM_BYTES),
        cost_estimate=pl.CostEstimate(
            flops=int(flops), bytes_accessed=int(moved), transcendentals=0
        ),
    )(*[array for array, _ in args])


def spread(values, pad, width):
    for group in range(3 * P_SIZE):
        c, i = divmod(group, P_SIZE)
        start = c * TR + i * P_SIZE
        pad[group, 0:P_SIZE, 0:width] = values[start : start + P_SIZE, :]


def to_mortars(facts, pad, out, comps, add):
    for half in range(2):
        lanes = slice(half * FACES, (half + 1) * FACES)
        for c in comps:
            for m in range(P_SIZE):
                total = facts[m : m + 1, lanes] * pad[c * P_SIZE, :, 0:FACES]
                for i in range(1, P_SIZE):
                    row = i * 8 + m
                    total += facts[row : row + 1, lanes] * pad[c * P_SIZE + i, :, 0:FACES]
                start = c * TR + m * P_SIZE
                rows = slice(start, start + P_SIZE)
                if add:
                    out[rows, lanes] += total[0:P_SIZE, :]
                else:
                    out[rows, lanes] = total[0:P_SIZE, :]


def outgoing(traces4, traces5):
    blank = jnp.zeros((FEAT - 3 * TR, ELEMS), F32)
    out4 = jnp.concatenate([traces4[0] - traces4[3], traces4[1], traces4[2], blank], axis=0)
    out5 = jnp.concatenate([traces5[0] + traces5[3], traces5[1], traces5[2], blank], axis=0)
    return out4, out5


def at_faces(rows4, rows5, members):
    high5, low5 = halves(rows5)
    high4, low4 = halves(rows4)
    rotor = nt(high5, members) + nt(low5, members)
    stator = nt(high4, members) + nt(low4, members)
    return jnp.where(iota((FEAT, FACES), 1) < IFD, rotor, stator)


def at_elements(values, members):
    rotor_side = iota((FEAT, FACES), 1) < IFD
    to5 = nn2b(jnp.where(rotor_side, values, 0.0), members)
    to4 = nn2b(jnp.where(rotor_side, 0.0, values), members)
    return to4, to5


def nn2b(x, exact):
    high, low = halves(x)
    return nn(high, exact) + nn(low, exact)


def comp(rows, c):
    return rows[c * TR : (c + 1) * TR, :]


def partner_body(pairs, out):
    row = iota((DEVICES, ELEMS), 0)
    total = None
    for mine, other in ((0, 1), (1, 0)):
        entry = pairs[mine : mine + 1, :]
        partner = pairs[other : other + 1, :]
        owner_row = mark(row == (entry >> 2)).astype(BF16)
        spot = entry & 3
        facts = jnp.where(row == spot, (partner >> 2) + 1, 0) + jnp.where(
            row == spot + 4, partner & 3, 0
        )
        term = nt(owner_row, facts.astype(F32).astype(BF16))
        total = term if total is None else total + term
    out[...] = total


def picked(keys, row, count):
    return mark(iota((count, ELEMS), 0).astype(F32) == keys[row : row + 1, :]).astype(BF16)


def member_picks(keys):
    number = iota((FACES, ELEMS), 0).astype(F32)
    rotor = number == keys[ROTOR : ROTOR + 1, :]
    stator = number == keys[STATOR : STATOR + 1, :]
    return mark(rotor | stator).astype(BF16)


def tables_body(
    neighbours, sends, metric, fields, select,
    keys, facts, own, info, mortars,
    rows, pad,
):
    me = my_device()
    nb = neighbours[...]
    face_id = iota((6, ELEMS), 0)
    remote = (nb >= 0) & ((nb >> 8) != me)
    here = (nb >= 0) & ((nb >> 8) == me)
    spot = nb & 255
    flags = jnp.where(face_id < 4, mark(remote), mark(nb == -2))
    rows[...] = jnp.zeros(rows.shape, F32)
    rows[0, 0:6, :] = flags
    rows[1, 0:6, :] = spot.astype(F32)
    flag_rows = rows[0].astype(BF16)
    spot_rows = rows[1].astype(BF16)
    down = iota((ELEMS, ELEMS), 0)
    across = iota((ELEMS, ELEMS), 1)
    before = mark(down < across).astype(BF16)
    same = mark(down == across).astype(BF16)
    rank = nn(flag_rows, before)
    spot_down = jnp.where(nt(same, flag_rows) > 0.5, nt(same, spot_rows), 1e4)
    keys[...] = jnp.zeros(keys.shape, F32)
    keys[NEAR : NEAR + 6, :] = jnp.where(here, spot, -1).astype(F32)
    for face in range(4):
        live = flags[face : face + 1, :] > 0.5
        order = jnp.sum(
            mark(spot_down[:, face : face + 1] < rows[1, face : face + 1, :]),
            axis=0,
            keepdims=True,
        )
        place = RIM_OUT + face
        keys[place : place + 1, :] = jnp.where(live, rank[face : face + 1, :], -1.0)
        place = RIM_IN + face
        keys[place : place + 1, :] = jnp.where(live, order, -1.0)
    keys[ROTOR : ROTOR + 1, :] = jnp.where(flags[5:6, :] > 0.5, rank[5:6, :], -1.0)
    keys[STATOR : STATOR + 1, :] = jnp.where(flags[4:5, :] > 0.5, rank[4:5, :] + IFD, -1.0)
    keys[SCALE : SCALE + 1, :] = metric[...]
    member = member_picks(keys)
    face_of = sends[0:1, :]
    lo_of = sends[1:2, :]
    lane_of = jnp.where(face_of >= 0, face_of + jnp.where(lo_of > 0, FACES, 0), -1)
    slot_lane = mark(iota((2 * FACES, SLOTS), 0) == lane_of).astype(BF16)
    kind = iota((16, SLOTS), 0)
    number = iota((16, SLOTS), 1)
    lines = jnp.where(kind == 0, number >> 2, 0) + jnp.where(kind == 1, number & 3, 0)
    lines += jnp.where(kind == 2, lo_of, 0) + jnp.where(kind == 3, sends[2:3, :], 0)
    found = nt(lines.astype(F32).astype(BF16), slot_lane)
    info[...] = found
    lo = found[2:3, :]
    width = found[3:4, :] - lo
    point = iota((8, 2 * FACES), 0)
    unit = jnp.zeros((8, 2 * FACES), F32)
    weight = jnp.zeros((8, 2 * FACES), F32)
    for m in range(P_SIZE):
        unit = jnp.where(point == m, float((POINTS[m] + 1.0) * 0.5), unit)
        weight = jnp.where(point == m, float(0.5 * WEIGHTS[m] / SUB), weight)
    spots = (lo + width * unit) * (2.0 / SUB) - 1.0
    for i in range(P_SIZE):
        product = None
        for j in range(P_SIZE):
            if j != i:
                term = (spots - float(POINTS[j])) * float(1.0 / (POINTS[i] - POINTS[j]))
                product = term if product is None else product * term
        facts[i * 8 : i * 8 + 8, :] = product
        start = PROJECT + i * 8
        facts[start : start + 8, :] = product * weight * width * float(1.0 / WEIGHTS[i])
    for i in range(P_SIZE):
        for k in range(P_SIZE):
            start = PROJECT + i * 8
            term = facts[start : start + 8, :] * facts[k * 8 : k * 8 + 8, :]
            term = jnp.sum(term, axis=0, keepdims=True)
            own[i * 8 + k : i * 8 + k + 1, :] = term[:, 0:FACES] + term[:, FACES:]
    scale = jnp.broadcast_to(metric[...], (16, ELEMS))
    high, rest = scale.astype(BF16), scale - scale.astype(BF16).astype(F32)
    middle, low = halves(rest)
    scale = nt(high, member) + nt(middle, member) + nt(low, member)
    facts[METRIC:FACT_ROWS, :] = jnp.concatenate([scale[0:8, :]] * 2, axis=1)
    traces = [nn2(select[4 * TR : 6 * TR, :], fields[c]) for c in range(4)]
    out4, out5 = outgoing([t[:TR] for t in traces], [t[TR:] for t in traces])
    spread(at_faces(out4, out5, member), pad, FACES)
    mortars[...] = jnp.zeros((FEAT, 2 * FACES), F32)
    to_mortars(facts, pad, mortars, (0, 1, 2), False)


def slot_picks(row):
    return mark(iota((SLOTS, 2 * FACES), 0).astype(F32) == row).astype(BF16)


def send_rows(exact, values):
    high, low = halves(values)
    return nt(exact, high) + nt(exact, low)


def route_body(facts, info, mortars, routes, payload):
    owner = info[0:1, :]
    turn = info[1:2, :]
    owner_pick = mark(iota((DEVICES, 2 * FACES), 0).astype(F32) == owner).astype(BF16)
    found = tn(facts[...].astype(BF16), owner_pick)
    partner = jnp.zeros((1, 2 * FACES), F32)
    other = jnp.zeros((1, 2 * FACES), F32)
    for t in range(4):
        partner = jnp.where(turn == t, found[t : t + 1, :], partner)
        other = jnp.where(turn == t, found[4 + t : 5 + t, :], other)
    partner = partner - 1.0
    kind = iota((16, 2 * FACES), 0)
    lines = jnp.where(kind == 0, partner, 0.0) + jnp.where(kind == 1, owner, 0.0)
    lines += jnp.where(kind == 2, turn, 0.0) + jnp.where(kind == 3, other, 0.0)
    same = mark(iota((2 * FACES, 2 * FACES), 0) == iota((2 * FACES, 2 * FACES), 1)).astype(BF16)
    down = nt(same, lines.astype(BF16))
    partner_down = down[:, 0:1]
    together = partner_down == partner
    mine_down = down[:, 1:2] * 4.0 + down[:, 2:3]
    theirs_down = down[:, 1:2] * 4.0 + down[:, 3:4]
    mine = owner * 4.0 + turn
    theirs = owner * 4.0 + other
    ahead = jnp.sum(mark(together & (mine_down < mine)), axis=0, keepdims=True)
    behind = jnp.sum(mark(together & (theirs_down < theirs)), axis=0, keepdims=True)
    kind = iota((8, 2 * FACES), 0)
    routes[...] = partner * 4.0 + jnp.where(kind == 0, ahead, behind)
    payload[...] = send_rows(slot_picks(partner * 4.0 + ahead), mortars[...])


def placed(picks, x):
    high, low = halves(x)
    return tn(picks, high) + tn(picks, low)


def place_interface(part, arrived, keys, select):
    picks = select[4 * TR : 6 * TR, :]
    to4, to5 = at_elements(arrived[...], member_picks(keys))
    result = []
    for c in range(4):
        source = (0, 1, 2, 0)[c]
        sign5 = -1.0 if c == 3 else 1.0
        stack = jnp.concatenate([comp(to4, source), sign5 * comp(to5, source)], axis=0)
        result.append(part[c] + placed(picks, stack))
    return result


def characteristics(traces, faces):
    blank = jnp.zeros((FEAT - 3 * TR, ELEMS), F32)
    leaving, inside = [], []
    for face in range(faces):
        sign = 1.0 if face % 2 else -1.0
        cut = [t[face * TR : (face + 1) * TR, :] for t in traces]
        along = face // 2
        tangent = [cut[1 + c] for c in range(3) if c != along]
        normal = sign * cut[1 + along]
        leaving.append(halves(jnp.concatenate([cut[0] + normal] + tangent + [blank], axis=0)))
        inside.append(jnp.concatenate([cut[0] - normal] + tangent + [blank], axis=0))
    return leaving, inside


def edge_body(section, *refs):
    part, keys, select = refs[:3]
    if section == 0:
        fields = [part[c] for c in range(4)]
        rims = refs[3:]
    else:
        arrived, whole = refs[3:5]
        fields = place_interface(part, arrived, keys, select)
        rims = refs[5:]
        for c in range(4):
            whole[c] = fields[c]
    leaving, _ = characteristics([nn2(select[0 : 4 * TR, :], x) for x in fields], 4)
    parts = []
    for face in range(4):
        pick = picked(keys, RIM_OUT + face, RIM)
        parts.append(nt(pick, leaving[face][0]) + nt(pick, leaving[face][1]))
    for turn, (down, up) in enumerate((parts[:2], parts[2:])):
        even = even_place(turn)
        rims[2 * turn][...] = jnp.where(even, up, down)
        rims[2 * turn + 1][...] = jnp.where(even, down, up)


def inner_body(section, *refs):
    whole, refs = refs[0], refs[1:]
    if section:
        first, refs = refs[0], refs[1:]
    select, derive, neighbours, keys, own, after, pad, mixed = refs
    keep, stay, rate = SECTIONS[section]
    fields = [whole[c] for c in range(4)]
    high, low = zip(*[halves(x) for x in fields])
    sel = select[...]
    traces = [nn(sel, high[c]) + nn(sel, low[c]) for c in range(4)]
    leaving, inside = characteristics(traces, 6)
    members = member_picks(keys)
    spread(at_faces(inside[4], inside[5], members), pad, FACES)
    mixed[...] = jnp.zeros(mixed.shape, F32)
    for c in range(3):
        for i in range(P_SIZE):
            total = own[i * 8 : i * 8 + 1, :] * pad[c * P_SIZE]
            for k in range(1, P_SIZE):
                row = i * 8 + k
                total += own[row : row + 1, :] * pad[c * P_SIZE + k]
            start = c * TR + i * P_SIZE
            mixed[start : start + P_SIZE, :] = -total[0:P_SIZE, :]
    to4, to5 = at_elements(mixed[...], members)
    terms = []
    for face in range(6):
        pick = picked(keys, NEAR + face, ELEMS)
        arriving = nn(leaving[face ^ 1][0], pick) + nn(leaving[face ^ 1][1], pick)
        term = 0.5 * (arriving - inside[face])
        if face >= 4:
            term = jnp.where(neighbours[face : face + 1, :] == -2, 0.0, term)
            term = term + (to4, to5)[face - 4]
        terms.append(term)
    scale = keys[SCALE : SCALE + 1, :] * rate
    for c in range(4):
        pieces = []
        for face in range(6):
            along = face // 2
            if c == 0:
                pieces.append(comp(terms[face], 0))
            elif c == 1 + along:
                pieces.append((-1.0 if face % 2 else 1.0) * comp(terms[face], 0))
            else:
                tangents = [k for k in range(3) if k != along]
                pieces.append(comp(terms[face], 1 + tangents.index(c - 1)))
        surface = placed(sel, jnp.concatenate(pieces, axis=0))
        if c == 0:
            pairs = ((0, 1), (1, 2), (2, 3))
        else:
            pairs = ((c - 1, 0),)
        volume = None
        for direction, source in pairs:
            big, small = derive[2 * direction], derive[2 * direction + 1]
            term = nn(big, high[source]) + nn(big, low[source]) + nn(small, high[source])
            volume = term if volume is None else volume + term
        base = stay * fields[c]
        if keep:
            base = base + keep * first[c]
        after[c] = base + scale * (LIFT * surface - volume)


def rim_body(section, *refs):
    before, r0, r1, r2, r3, select, keys, facts, routes = refs[:9]
    last = section == 2
    after, pack = refs[9:11]
    scale = keys[SCALE : SCALE + 1, :] * (SECTIONS[section][2] * LIFT)
    terms = []
    terms = []
    got = []
    for turn, (one, two) in enumerate(((r0, r1), (r2, r3))):
        even = even_place(turn)
        got.append(jnp.where(even, two[...], one[...]))
        got.append(jnp.where(even, one[...], two[...]))
    for face, value in enumerate(got):
        high, low = halves(value)
        pick = picked(keys, RIM_IN + face, RIM)
        terms.append(0.5 * (tn(high, pick) + tn(low, pick)))
    fields = []
    for c in range(4):
        pieces = []
        for face in range(4):
            along = face // 2
            if c == 0:
                pieces.append(comp(terms[face], 0))
            elif c == 1 + along:
                pieces.append((-1.0 if face % 2 else 1.0) * comp(terms[face], 0))
            else:
                tangents = [k for k in range(3) if k != along]
                pieces.append(comp(terms[face], 1 + tangents.index(c - 1)))
        value = before[c] + scale * placed(select[0 : 4 * TR, :], jnp.concatenate(pieces, axis=0))
        after[c] = value
        fields.append(value)
    pack[0:FACT_ROWS, :] = facts[...]
    pack[ROUTES : ROUTES + 8, :] = routes[...]
    if not last:
        pad = refs[11]
        traces = [nn2(select[4 * TR : 6 * TR, :], x) for x in fields]
        out4, out5 = outgoing([t[:TR] for t in traces], [t[TR:] for t in traces])
        spread(at_faces(out4, out5, member_picks(keys)), pad, FACES)
        mortars = pack.at[FACT_ROWS:ROUTES, :]
        mortars[...] = jnp.zeros((FEAT, 2 * FACES), F32)
        to_mortars(facts, pad, mortars, (0, 1, 2), False)


def arrive(section, arrivals, held, pad, wide, out):
    high, low = halves(arrivals[...])
    pick = slot_picks(held[ROUTES + 1 : ROUTES + 2, :])
    spread(tn(high, pick) + tn(low, pick), wide, 2 * FACES)
    scale = held[METRIC : METRIC + 1, 0:FACES] * (SECTIONS[section][2] * LIFT)
    out[...] = jnp.zeros(out.shape, F32)
    for c in range(3):
        for i in range(P_SIZE):
            total = None
            for half in range(2):
                lanes = slice(half * FACES, (half + 1) * FACES)
                for m in range(P_SIZE):
                    row = PROJECT + i * 8 + m
                    term = held[row : row + 1, lanes] * wide[c * P_SIZE + m, :, lanes]
                    total = term if total is None else total + term
            total = total * scale
            pad[c * P_SIZE + i] = total
            start = c * TR + i * P_SIZE
            out[start : start + P_SIZE, :] = total[0:P_SIZE, :]


def flux_body(section, arrivals, held, arrived, payload, pad, wide, mixed):
    arrive(section, arrivals, held, pad, wide, arrived)
    mixed[...] = held[FACT_ROWS:ROUTES, :]
    to_mortars(held, pad, mixed, (1, 2), True)
    payload[...] = send_rows(slot_picks(held[ROUTES : ROUTES + 1, :]), mixed[...])


def last_body(arrivals, held, part, keys, select, after, pad, wide, arrived):
    arrive(2, arrivals, held, pad, wide, arrived)
    result = place_interface(part, arrived, keys, select)
    for c in range(4):
        after[c] = result[c]


def exchange(rows, width):
    whole = rows.reshape(DEVICES, width, FEAT)
    moved = lax.all_to_all(whole, ("blk", "sub"), split_axis=0, concat_axis=0, tiled=True)
    return moved.reshape(DEVICES * width, FEAT)


def pass_rims(rims):
    arrived = []
    blks, subs = lax.axis_size("blk"), lax.axis_size("sub")
    for turn in range(4):
        pairs = []
        for blk in range(blks):
            for sub in range(subs):
                at, count = ((sub, subs), (blk, blks))[turn // 2]
                other = at + 1 if at % 2 == turn % 2 else at - 1
                there = [blk, sub]
                if 0 <= other < count:
                    there[1 - turn // 2] = other
                else:
                    there[turn // 2] ^= 1
                pairs.append((blk * subs + sub, there[0] * subs + there[1]))
        arrived.append(lax.ppermute(rims[turn], ("blk", "sub"), pairs))
    return arrived


def bind(body, section):
    def bound(*refs):
        body(section, *refs)

    return bound


def per_device(fields, metric, neighbours, mortar_sends, mortar_pairs):
    select = jnp.asarray(face_rows(), BF16)
    derive = jnp.asarray(derivative_pieces())
    metric = metric.reshape(1, ELEMS)
    whole = ((4, NODES, ELEMS), F32, "v")
    rim = ((RIM, FEAT), F32, "v")
    table = ((FACT_ROWS, 2 * FACES), F32, "v")
    pad = pltpu.VMEM((3 * P_SIZE, 8, FACES), F32)
    wide = pltpu.VMEM((3 * P_SIZE, 8, 2 * FACES), F32)
    narrow = pltpu.VMEM((FEAT, FACES), F32)
    broad = pltpu.VMEM((FEAT, 2 * FACES), F32)

    def far(*arrays):
        return tuple((array, "v") for array in arrays)

    def near(*arrays):
        return tuple((array, "v") for array in arrays)

    (owned,) = call(partner_body, [((DEVICES, FEAT), F32, "v")], near(mortar_pairs))
    owned = exchange(owned, 1)
    keys, facts, own, info, mortars = call(
        tables_body,
        [
            ((KEY_ROWS, ELEMS), F32, "v"),
            table,
            ((48, FACES), F32, "v"),
            ((16, 2 * FACES), F32, "v"),
            ((FEAT, 2 * FACES), F32, "v"),
        ],
        near(neighbours, mortar_sends, metric, fields, select),
        scratch=[pltpu.VMEM((2, 16, ELEMS), F32), pad],
    )
    routes, payload = call(
        route_body,
        [((8, 2 * FACES), F32, "v"), ((SLOTS, FEAT), F32, "v")],
        near(owned, info, mortars),
    )
    part, arrived = fields, None
    packed = ((ROUTES + 8, 2 * FACES), F32, "v")
    for section in range(3):
        arrivals = exchange(payload, 4)
        edge = near(part) + far(keys) + near(select)
        if section == 0:
            current = near(fields)
            rims = call(bind(edge_body, section), [rim] * 4, edge, flops=5e7)
        else:
            current, *rims = call(
                bind(edge_body, section), [whole] + [rim] * 4, edge + far(arrived), flops=5e7
            )
            current = near(current, fields)
        rims = pass_rims(rims)
        (after,) = call(
            bind(inner_body, section),
            [whole],
            current + near(select, derive, neighbours) + far(keys, own),
            scratch=[pad, narrow],
            flops=8e8,
        )
        part, held = call(
            bind(rim_body, section),
            [whole, packed],
            near(after, *rims, select) + far(keys, facts, routes),
            scratch=[] if section == 2 else [pad],
        )
        if section < 2:
            arrived, payload = call(
                bind(flux_body, section),
                [((FEAT, FACES), F32, "v"), ((SLOTS, FEAT), F32, "v")],
                near(arrivals, held),
                scratch=[pad, wide, broad],
            )
    (result,) = call(
        last_body,
        [whole],
        near(arrivals, held, part) + far(keys) + near(select),
        scratch=[pad, wide, narrow],
    )
    return result


def solution(mesh):
    placed = (
        P(None, None, ("blk", "sub")),
        P(("blk", "sub")),
        P(None, ("blk", "sub")),
        P(None, ("blk", "sub")),
        P(None, ("blk", "sub")),
    )
    return jax.shard_map(
        per_device,
        mesh=mesh,
        in_specs=placed,
        out_specs=P(None, None, ("blk", "sub")),
        check_vma=False,
    )
```

```python
import jax
import jax.numpy as jnp
import numpy as np
from jax import lax
from jax.experimental import pallas as pl
from jax.experimental.pallas import tpu as pltpu
from jax.sharding import PartitionSpec as P

P_SIZE = 6
SUB = 16
IFD = 64
RIM = 32
NODES = 216
ELEMS = 256
FACES = 2 * IFD
SLOTS = 512
DEVICES = 128
TR = 40
PROJECT = 48
METRIC = 96
FACT_ROWS = 104
ROUTES = FACT_ROWS + 128
NEAR, RIM_OUT, RIM_IN, ROTOR, STATOR, SCALE, KEY_ROWS = 0, 6, 10, 14, 15, 16, 24
FEAT = 128
DT_STEP = 0.01
F32 = jnp.float32
BF16 = jnp.bfloat16
VMEM_BYTES = 24 * 1024 * 1024


def legendre_columns(points, npts):
    legendre = np.zeros((npts, npts))
    legendre[:, 0] = 1.0
    legendre[:, 1] = points
    for k in range(2, npts):
        legendre[:, k] = (
            (2 * k - 1) * points * legendre[:, k - 1] - (k - 1) * legendre[:, k - 2]
        ) / k
    return legendre


def basis_tables(npts):
    order = npts - 1
    points = -np.cos(np.pi * np.arange(npts) / order)
    for iteration in range(60):
        legendre = legendre_columns(points, npts)
        points = points - (points * legendre[:, order] - legendre[:, order - 1]) / (
            npts * legendre[:, order]
        )
    legendre = legendre_columns(points, npts)
    weights = 2.0 / (order * npts * legendre[:, order] ** 2)
    separation = points[:, None] - points[None, :] + np.eye(npts)
    derivative = legendre[:, order][:, None] / legendre[:, order][None, :] / separation
    derivative = derivative * (1.0 - np.eye(npts))
    derivative[0, 0] = -order * npts / 4.0
    derivative[order, order] = order * npts / 4.0
    return (points, weights, derivative)


POINTS, WEIGHTS, DERIVATIVE = basis_tables(P_SIZE)
LIFT = float(1.0 / WEIGHTS[0])
SECTIONS = (
    (0.0, 1.0, DT_STEP),
    (0.75, 0.25, 0.25 * DT_STEP),
    (1.0 / 3.0, 2.0 / 3.0, 2.0 / 3.0 * DT_STEP),
)


def face_rows():
    picks = np.zeros((6 * TR, NODES))
    for face in range(6):
        fixed = 0 if face % 2 == 0 else P_SIZE - 1
        for a in range(P_SIZE):
            for b in range(P_SIZE):
                place = [a, b]
                place.insert(face // 2, fixed)
                node = (place[0] * P_SIZE + place[1]) * P_SIZE + place[2]
                picks[face * TR + a * P_SIZE + b, node] = 1.0
    return picks


def derivative_pieces():
    one = np.eye(P_SIZE)
    square = np.eye(P_SIZE * P_SIZE)
    whole = [
        np.kron(DERIVATIVE, square),
        np.kron(one, np.kron(DERIVATIVE, one)),
        np.kron(square, DERIVATIVE),
    ]
    pieces = []
    for matrix in whole:
        matrix = matrix.astype(np.float32)
        high = matrix.astype(jnp.bfloat16)
        pieces.append(high)
        pieces.append((matrix - high.astype(np.float32)).astype(jnp.bfloat16))
    return np.stack(pieces)


def nn(a, b):
    return lax.dot_general(a, b, (((1,), (0,)), ((), ())), preferred_element_type=F32)


def nt(a, b):
    return lax.dot_general(a, b, (((1,), (1,)), ((), ())), preferred_element_type=F32)


def tn(a, b):
    return lax.dot_general(a, b, (((0,), (0,)), ((), ())), preferred_element_type=F32)


def halves(x):
    high = x.astype(BF16)
    return high, (x - high.astype(F32)).astype(BF16)


def nn2(exact, x):
    high, low = halves(x)
    return nn(exact, high) + nn(exact, low)


def mark(cond):
    return jnp.where(cond, 1.0, 0.0)


def iota(shape, dim):
    return lax.broadcasted_iota(jnp.int32, shape, dim)


def my_device():
    return lax.axis_index("blk") * 8 + lax.axis_index("sub")


def even_place(turn):
    return (lax.axis_index(("sub", "blk")[turn]) & 1) == 0


class Fetched:
    def __init__(self, copy, buffer):
        self.copy, self.buffer, self.here = copy, buffer, False

    def __getitem__(self, key):
        if not self.here:
            self.copy.wait()
            self.here = True
        return self.buffer[key]


def call(body, outs, args, scratch=(), flops=1e8, moved=2e6):
    far_in = [i for i, (_, space) in enumerate(args) if space == "h"]
    far_out = [i for i, (_, _, space) in enumerate(outs) if space == "h"]
    own = [pltpu.VMEM(args[i][0].shape, args[i][0].dtype) for i in far_in]
    own += [pltpu.VMEM(outs[i][0], outs[i][1]) for i in far_out]
    count = len(far_in) + len(far_out)

    def kernel(*refs):
        refs = list(refs)
        ins, refs = refs[: len(args)], refs[len(args) :]
        results, refs = refs[: len(outs)], refs[len(outs) :]
        extra, refs = refs[: len(scratch)], refs[len(scratch) :]
        sems = refs[-1] if count else None
        for n, i in enumerate(far_in):
            copy = pltpu.make_async_copy(ins[i], refs[n], sems.at[n])
            copy.start()
            ins[i] = Fetched(copy, refs[n])
        shown = list(results)
        for n, i in enumerate(far_out):
            shown[i] = refs[len(far_in) + n]
        body(*ins, *shown, *extra)
        for i in far_in:
            if not ins[i].here:
                ins[i].copy.wait()
        copies = []
        for n, i in enumerate(far_out):
            spot = len(far_in) + n
            copies.append(pltpu.make_async_copy(refs[spot], results[i], sems.at[spot]))
            copies[-1].start()
        for copy in copies:
            copy.wait()

    spaces = {"h": pltpu.HBM, "v": pltpu.VMEM}
    return pl.pallas_call(
        kernel,
        out_shape=[jax.ShapeDtypeStruct(o[0], o[1]) for o in outs],
        in_specs=[pl.BlockSpec(memory_space=spaces[space]) for _, space in args],
        out_specs=[pl.BlockSpec(memory_space=spaces[o[2]]) for o in outs],
        scratch_shapes=list(scratch)
        + own
        + ([pltpu.SemaphoreType.DMA((count,))] if count else []),
        compiler_params=pltpu.CompilerParams(vmem_limit_bytes=VMEM_BYTES),
        cost_estimate=pl.CostEstimate(
            flops=int(flops), bytes_accessed=int(moved), transcendentals=0
        ),
    )(*[array for array, _ in args])


def spread(values, pad, width):
    for group in range(3 * P_SIZE):
        c, i = divmod(group, P_SIZE)
        start = c * TR + i * P_SIZE
        pad[group, 0:P_SIZE, 0:width] = values[start : start + P_SIZE, :]


def to_mortars(facts, pad, out, comps, add):
    for half in range(2):
        lanes = slice(half * FACES, (half + 1) * FACES)
        for c in comps:
            for m in range(P_SIZE):
                total = facts[m : m + 1, lanes] * pad[c * P_SIZE, :, 0:FACES]
                for i in range(1, P_SIZE):
                    row = i * 8 + m
                    total += facts[row : row + 1, lanes] * pad[c * P_SIZE + i, :, 0:FACES]
                start = c * TR + m * P_SIZE
                rows = slice(start, start + P_SIZE)
                if add:
                    out[rows, lanes] += total[0:P_SIZE, :]
                else:
                    out[rows, lanes] = total[0:P_SIZE, :]


def outgoing(traces4, traces5):
    blank = jnp.zeros((FEAT - 3 * TR, ELEMS), F32)
    out4 = jnp.concatenate([traces4[0] - traces4[3], traces4[1], traces4[2], blank], axis=0)
    out5 = jnp.concatenate([traces5[0] + traces5[3], traces5[1], traces5[2], blank], axis=0)
    return out4, out5


def at_faces(rows4, rows5, members):
    high5, low5 = halves(rows5)
    high4, low4 = halves(rows4)
    rotor = nt(high5, members) + nt(low5, members)
    stator = nt(high4, members) + nt(low4, members)
    return jnp.where(iota((FEAT, FACES), 1) < IFD, rotor, stator)


def at_elements(values, members):
    rotor_side = iota((FEAT, FACES), 1) < IFD
    to5 = nn2b(jnp.where(rotor_side, values, 0.0), members)
    to4 = nn2b(jnp.where(rotor_side, 0.0, values), members)
    return to4, to5


def nn2b(x, exact):
    high, low = halves(x)
    return nn(high, exact) + nn(low, exact)


def comp(rows, c):
    return rows[c * TR : (c + 1) * TR, :]


def partner_body(pairs, out):
    row = iota((DEVICES, ELEMS), 0)
    total = None
    for mine, other in ((0, 1), (1, 0)):
        entry = pairs[mine : mine + 1, :]
        partner = pairs[other : other + 1, :]
        owner_row = mark(row == (entry >> 2)).astype(BF16)
        spot = entry & 3
        facts = jnp.where(row == spot, (partner >> 2) + 1, 0) + jnp.where(
            row == spot + 4, partner & 3, 0
        )
        term = nt(owner_row, facts.astype(F32).astype(BF16))
        total = term if total is None else total + term
    out[...] = total


def picked(keys, row, count):
    return mark(iota((count, ELEMS), 0).astype(F32) == keys[row : row + 1, :]).astype(BF16)


def member_picks(keys):
    number = iota((FACES, ELEMS), 0).astype(F32)
    rotor = number == keys[ROTOR : ROTOR + 1, :]
    stator = number == keys[STATOR : STATOR + 1, :]
    return mark(rotor | stator).astype(BF16)


def tables_body(
    neighbours, sends, metric, fields, select,
    keys, facts, own, info, mortars,
    rows, pad,
):
    me = my_device()
    nb = neighbours[...]
    face_id = iota((6, ELEMS), 0)
    remote = (nb >= 0) & ((nb >> 8) != me)
    here = (nb >= 0) & ((nb >> 8) == me)
    spot = nb & 255
    flags = jnp.where(face_id < 4, mark(remote), mark(nb == -2))
    rows[...] = jnp.zeros(rows.shape, F32)
    rows[0, 0:6, :] = flags
    rows[1, 0:6, :] = spot.astype(F32)
    flag_rows = rows[0].astype(BF16)
    spot_rows = rows[1].astype(BF16)
    down = iota((ELEMS, ELEMS), 0)
    across = iota((ELEMS, ELEMS), 1)
    before = mark(down < across).astype(BF16)
    same = mark(down == across).astype(BF16)
    rank = nn(flag_rows, before)
    spot_down = jnp.where(nt(same, flag_rows) > 0.5, nt(same, spot_rows), 1e4)
    keys[...] = jnp.zeros(keys.shape, F32)
    keys[NEAR : NEAR + 6, :] = jnp.where(here, spot, -1).astype(F32)
    for face in range(4):
        live = flags[face : face + 1, :] > 0.5
        order = jnp.sum(
            mark(spot_down[:, face : face + 1] < rows[1, face : face + 1, :]),
            axis=0,
            keepdims=True,
        )
        place = RIM_OUT + face
        keys[place : place + 1, :] = jnp.where(live, rank[face : face + 1, :], -1.0)
        place = RIM_IN + face
        keys[place : place + 1, :] = jnp.where(live, order, -1.0)
    keys[ROTOR : ROTOR + 1, :] = jnp.where(flags[5:6, :] > 0.5, rank[5:6, :], -1.0)
    keys[STATOR : STATOR + 1, :] = jnp.where(flags[4:5, :] > 0.5, rank[4:5, :] + IFD, -1.0)
    keys[SCALE : SCALE + 1, :] = metric[...]
    member = member_picks(keys)
    face_of = sends[0:1, :]
    lo_of = sends[1:2, :]
    lane_of = jnp.where(face_of >= 0, face_of + jnp.where(lo_of > 0, FACES, 0), -1)
    slot_lane = mark(iota((2 * FACES, SLOTS), 0) == lane_of).astype(BF16)
    kind = iota((16, SLOTS), 0)
    number = iota((16, SLOTS), 1)
    lines = jnp.where(kind == 0, number >> 2, 0) + jnp.where(kind == 1, number & 3, 0)
    lines += jnp.where(kind == 2, lo_of, 0) + jnp.where(kind == 3, sends[2:3, :], 0)
    found = nt(lines.astype(F32).astype(BF16), slot_lane)
    info[...] = found
    lo = found[2:3, :]
    width = found[3:4, :] - lo
    point = iota((8, 2 * FACES), 0)
    unit = jnp.zeros((8, 2 * FACES), F32)
    weight = jnp.zeros((8, 2 * FACES), F32)
    for m in range(P_SIZE):
        unit = jnp.where(point == m, float((POINTS[m] + 1.0) * 0.5), unit)
        weight = jnp.where(point == m, float(0.5 * WEIGHTS[m] / SUB), weight)
    spots = (lo + width * unit) * (2.0 / SUB) - 1.0
    for i in range(P_SIZE):
        product = None
        for j in range(P_SIZE):
            if j != i:
                term = (spots - float(POINTS[j])) * float(1.0 / (POINTS[i] - POINTS[j]))
                product = term if product is None else product * term
        facts[i * 8 : i * 8 + 8, :] = product
        start = PROJECT + i * 8
        facts[start : start + 8, :] = product * weight * width * float(1.0 / WEIGHTS[i])
    for i in range(P_SIZE):
        for k in range(P_SIZE):
            start = PROJECT + i * 8
            term = facts[start : start + 8, :] * facts[k * 8 : k * 8 + 8, :]
            term = jnp.sum(term, axis=0, keepdims=True)
            own[i * 8 + k : i * 8 + k + 1, :] = term[:, 0:FACES] + term[:, FACES:]
    scale = jnp.broadcast_to(metric[...], (16, ELEMS))
    high, rest = scale.astype(BF16), scale - scale.astype(BF16).astype(F32)
    middle, low = halves(rest)
    scale = nt(high, member) + nt(middle, member) + nt(low, member)
    facts[METRIC:FACT_ROWS, :] = jnp.concatenate([scale[0:8, :]] * 2, axis=1)
    traces = [nn2(select[4 * TR : 6 * TR, :], fields[c]) for c in range(4)]
    out4, out5 = outgoing([t[:TR] for t in traces], [t[TR:] for t in traces])
    spread(at_faces(out4, out5, member), pad, FACES)
    mortars[...] = jnp.zeros((FEAT, 2 * FACES), F32)
    to_mortars(facts, pad, mortars, (0, 1, 2), False)


def slot_picks(row):
    return mark(iota((SLOTS, 2 * FACES), 0).astype(F32) == row).astype(BF16)


def send_rows(exact, values):
    high, low = halves(values)
    return nt(exact, high) + nt(exact, low)


def route_body(facts, info, mortars, routes, payload):
    owner = info[0:1, :]
    turn = info[1:2, :]
    owner_pick = mark(iota((DEVICES, 2 * FACES), 0).astype(F32) == owner).astype(BF16)
    found = tn(facts[...].astype(BF16), owner_pick)
    partner = jnp.zeros((1, 2 * FACES), F32)
    other = jnp.zeros((1, 2 * FACES), F32)
    for t in range(4):
        partner = jnp.where(turn == t, found[t : t + 1, :], partner)
        other = jnp.where(turn == t, found[4 + t : 5 + t, :], other)
    partner = partner - 1.0
    kind = iota((16, 2 * FACES), 0)
    lines = jnp.where(kind == 0, partner, 0.0) + jnp.where(kind == 1, owner, 0.0)
    lines += jnp.where(kind == 2, turn, 0.0) + jnp.where(kind == 3, other, 0.0)
    same = mark(iota((2 * FACES, 2 * FACES), 0) == iota((2 * FACES, 2 * FACES), 1)).astype(BF16)
    down = nt(same, lines.astype(BF16))
    partner_down = down[:, 0:1]
    together = partner_down == partner
    mine_down = down[:, 1:2] * 4.0 + down[:, 2:3]
    theirs_down = down[:, 1:2] * 4.0 + down[:, 3:4]
    mine = owner * 4.0 + turn
    theirs = owner * 4.0 + other
    ahead = jnp.sum(mark(together & (mine_down < mine)), axis=0, keepdims=True)
    behind = jnp.sum(mark(together & (theirs_down < theirs)), axis=0, keepdims=True)
    kind = iota((8, 2 * FACES), 0)
    routes[...] = partner * 4.0 + jnp.where(kind == 0, ahead, behind)
    payload[...] = send_rows(slot_picks(partner * 4.0 + ahead), mortars[...])


def placed(picks, x):
    high, low = halves(x)
    return tn(picks, high) + tn(picks, low)


def place_interface(part, arrived, keys, select):
    picks = select[4 * TR : 6 * TR, :]
    to4, to5 = at_elements(arrived[...], member_picks(keys))
    result = []
    for c in range(4):
        source = (0, 1, 2, 0)[c]
        sign5 = -1.0 if c == 3 else 1.0
        stack = jnp.concatenate([comp(to4, source), sign5 * comp(to5, source)], axis=0)
        result.append(part[c] + placed(picks, stack))
    return result


def characteristics(traces, faces):
    blank = jnp.zeros((FEAT - 3 * TR, ELEMS), F32)
    leaving, inside = [], []
    for face in range(faces):
        sign = 1.0 if face % 2 else -1.0
        cut = [t[face * TR : (face + 1) * TR, :] for t in traces]
        along = face // 2
        tangent = [cut[1 + c] for c in range(3) if c != along]
        normal = sign * cut[1 + along]
        leaving.append(halves(jnp.concatenate([cut[0] + normal] + tangent + [blank], axis=0)))
        inside.append(jnp.concatenate([cut[0] - normal] + tangent + [blank], axis=0))
    return leaving, inside


def edge_body(section, *refs):
    part, keys, select = refs[:3]
    if section == 0:
        fields = [part[c] for c in range(4)]
        rims = refs[3:]
    else:
        arrived, whole = refs[3:5]
        fields = place_interface(part, arrived, keys, select)
        rims = refs[5:]
        for c in range(4):
            whole[c] = fields[c]
    leaving, _ = characteristics([nn2(select[0 : 4 * TR, :], x) for x in fields], 4)
    parts = []
    for face in range(4):
        pick = picked(keys, RIM_OUT + face, RIM)
        parts.append(nt(pick, leaving[face][0]) + nt(pick, leaving[face][1]))
    for turn, (down, up) in enumerate((parts[:2], parts[2:])):
        even = even_place(turn)
        rims[2 * turn][...] = jnp.where(even, up, down)
        rims[2 * turn + 1][...] = jnp.where(even, down, up)


def inner_body(section, *refs):
    whole, refs = refs[0], refs[1:]
    if section:
        first, refs = refs[0], refs[1:]
    select, derive, neighbours, keys, own, after, pad, mixed = refs
    keep, stay, rate = SECTIONS[section]
    fields = [whole[c] for c in range(4)]
    high, low = zip(*[halves(x) for x in fields])
    sel = select[...]
    traces = [nn(sel, high[c]) + nn(sel, low[c]) for c in range(4)]
    leaving, inside = characteristics(traces, 6)
    members = member_picks(keys)
    spread(at_faces(inside[4], inside[5], members), pad, FACES)
    mixed[...] = jnp.zeros(mixed.shape, F32)
    for c in range(3):
        for i in range(P_SIZE):
            total = own[i * 8 : i * 8 + 1, :] * pad[c * P_SIZE]
            for k in range(1, P_SIZE):
                row = i * 8 + k
                total += own[row : row + 1, :] * pad[c * P_SIZE + k]
            start = c * TR + i * P_SIZE
            mixed[start : start + P_SIZE, :] = -total[0:P_SIZE, :]
    to4, to5 = at_elements(mixed[...], members)
    terms = []
    for face in range(6):
        pick = picked(keys, NEAR + face, ELEMS)
        arriving = nn(leaving[face ^ 1][0], pick) + nn(leaving[face ^ 1][1], pick)
        term = 0.5 * (arriving - inside[face])
        if face >= 4:
            term = jnp.where(neighbours[face : face + 1, :] == -2, 0.0, term)
            term = term + (to4, to5)[face - 4]
        terms.append(term)
    scale = keys[SCALE : SCALE + 1, :] * rate
    for c in range(4):
        pieces = []
        for face in range(6):
            along = face // 2
            if c == 0:
                pieces.append(comp(terms[face], 0))
            elif c == 1 + along:
                pieces.append((-1.0 if face % 2 else 1.0) * comp(terms[face], 0))
            else:
                tangents = [k for k in range(3) if k != along]
                pieces.append(comp(terms[face], 1 + tangents.index(c - 1)))
        surface = placed(sel, jnp.concatenate(pieces, axis=0))
        if c == 0:
            pairs = ((0, 1), (1, 2), (2, 3))
        else:
            pairs = ((c - 1, 0),)
        volume = None
        for direction, source in pairs:
            big, small = derive[2 * direction], derive[2 * direction + 1]
            term = nn(big, high[source]) + nn(big, low[source]) + nn(small, high[source])
            volume = term if volume is None else volume + term
        base = stay * fields[c]
        if keep:
            base = base + keep * first[c]
        after[c] = base + scale * (LIFT * surface - volume)


def rim_body(section, *refs):
    before, r3, r2, r1, r0, select, keys, facts, routes = refs[:9]
    last = section == 2
    after, pack = refs[9:11]
    scale = keys[SCALE : SCALE + 1, :] * (SECTIONS[section][2] * LIFT)
    terms = []
    terms = []
    got = []
    for turn, (one, two) in enumerate(((r0, r1), (r2, r3))):
        even = even_place(turn)
        got.append(jnp.where(even, two[...], one[...]))
        got.append(jnp.where(even, one[...], two[...]))
    for face, value in enumerate(got):
        high, low = halves(value)
        pick = picked(keys, RIM_IN + face, RIM)
        terms.append(0.5 * (tn(high, pick) + tn(low, pick)))
    fields = []
    for c in range(4):
        pieces = []
        for face in range(4):
            along = face // 2
            if c == 0:
                pieces.append(comp(terms[face], 0))
            elif c == 1 + along:
                pieces.append((-1.0 if face % 2 else 1.0) * comp(terms[face], 0))
            else:
                tangents = [k for k in range(3) if k != along]
                pieces.append(comp(terms[face], 1 + tangents.index(c - 1)))
        value = before[c] + scale * placed(select[0 : 4 * TR, :], jnp.concatenate(pieces, axis=0))
        after[c] = value
        fields.append(value)
    pack[0:FACT_ROWS, :] = facts[...]
    pack[ROUTES : ROUTES + 8, :] = routes[...]
    if not last:
        pad = refs[11]
        traces = [nn2(select[4 * TR : 6 * TR, :], x) for x in fields]
        out4, out5 = outgoing([t[:TR] for t in traces], [t[TR:] for t in traces])
        spread(at_faces(out4, out5, member_picks(keys)), pad, FACES)
        mortars = pack.at[FACT_ROWS:ROUTES, :]
        mortars[...] = jnp.zeros((FEAT, 2 * FACES), F32)
        to_mortars(facts, pad, mortars, (0, 1, 2), False)


def arrive(section, arrivals, held, pad, wide, out):
    high, low = halves(arrivals[...])
    pick = slot_picks(held[ROUTES + 1 : ROUTES + 2, :])
    spread(tn(high, pick) + tn(low, pick), wide, 2 * FACES)
    scale = held[METRIC : METRIC + 1, 0:FACES] * (SECTIONS[section][2] * LIFT)
    out[...] = jnp.zeros(out.shape, F32)
    for c in range(3):
        for i in range(P_SIZE):
            total = None
            for half in range(2):
                lanes = slice(half * FACES, (half + 1) * FACES)
                for m in range(P_SIZE):
                    row = PROJECT + i * 8 + m
                    term = held[row : row + 1, lanes] * wide[c * P_SIZE + m, :, lanes]
                    total = term if total is None else total + term
            total = total * scale
            pad[c * P_SIZE + i] = total
            start = c * TR + i * P_SIZE
            out[start : start + P_SIZE, :] = total[0:P_SIZE, :]


def flux_body(section, arrivals, held, arrived, payload, pad, wide, mixed):
    arrive(section, arrivals, held, pad, wide, arrived)
    mixed[...] = held[FACT_ROWS:ROUTES, :]
    to_mortars(held, pad, mixed, (1, 2), True)
    payload[...] = send_rows(slot_picks(held[ROUTES : ROUTES + 1, :]), mixed[...])


def last_body(arrivals, held, part, keys, select, after, pad, wide, arrived):
    arrive(2, arrivals, held, pad, wide, arrived)
    result = place_interface(part, arrived, keys, select)
    for c in range(4):
        after[c] = result[c]


def exchange(rows, width):
    whole = rows.reshape(DEVICES, width, FEAT)
    moved = lax.all_to_all(whole, ("blk", "sub"), split_axis=0, concat_axis=0, tiled=True)
    return moved.reshape(DEVICES * width, FEAT)


def pass_rims(rims):
    arrived = []
    blks, subs = lax.axis_size("blk"), lax.axis_size("sub")
    for turn in range(4):
        pairs = []
        for blk in range(blks):
            for sub in range(subs):
                at, count = ((sub, subs), (blk, blks))[turn // 2]
                other = at + 1 if at % 2 == turn % 2 else at - 1
                there = [blk, sub]
                if 0 <= other < count:
                    there[1 - turn // 2] = other
                else:
                    there[turn // 2] ^= 1
                pairs.append((blk * subs + sub, there[0] * subs + there[1]))
        arrived.append(lax.ppermute(rims[turn], ("blk", "sub"), pairs))
    return arrived


def bind(body, section):
    def bound(*refs):
        body(section, *refs)

    return bound


def per_device(fields, metric, neighbours, mortar_sends, mortar_pairs):
    select = jnp.asarray(face_rows(), BF16)
    derive = jnp.asarray(derivative_pieces())
    metric = metric.reshape(1, ELEMS)
    whole = ((4, NODES, ELEMS), F32, "v")
    rim = ((RIM, FEAT), F32, "v")
    table = ((FACT_ROWS, 2 * FACES), F32, "v")
    pad = pltpu.VMEM((3 * P_SIZE, 8, FACES), F32)
    wide = pltpu.VMEM((3 * P_SIZE, 8, 2 * FACES), F32)
    narrow = pltpu.VMEM((FEAT, FACES), F32)
    broad = pltpu.VMEM((FEAT, 2 * FACES), F32)

    def far(*arrays):
        return tuple((array, "v") for array in arrays)

    def near(*arrays):
        return tuple((array, "v") for array in arrays)

    (owned,) = call(partner_body, [((DEVICES, FEAT), F32, "v")], near(mortar_pairs))
    owned = exchange(owned, 1)
    keys, facts, own, info, mortars = call(
        tables_body,
        [
            ((KEY_ROWS, ELEMS), F32, "v"),
            table,
            ((48, FACES), F32, "v"),
            ((16, 2 * FACES), F32, "v"),
            ((FEAT, 2 * FACES), F32, "v"),
        ],
        near(neighbours, mortar_sends, metric, fields, select),
        scratch=[pltpu.VMEM((2, 16, ELEMS), F32), pad],
    )
    routes, payload = call(
        route_body,
        [((8, 2 * FACES), F32, "v"), ((SLOTS, FEAT), F32, "v")],
        near(owned, info, mortars),
    )
    part, arrived = fields, None
    packed = ((ROUTES + 8, 2 * FACES), F32, "v")
    for section in range(3):
        arrivals = exchange(payload, 4)
        edge = near(part) + far(keys) + near(select)
        if section == 0:
            current = near(fields)
            rims = call(bind(edge_body, section), [rim] * 4, edge, flops=5e7)
        else:
            current, *rims = call(
                bind(edge_body, section), [whole] + [rim] * 4, edge + far(arrived), flops=5e7
            )
            current = near(current, fields)
        rims = pass_rims(rims)
        (after,) = call(
            bind(inner_body, section),
            [whole],
            current + near(select, derive, neighbours) + far(keys, own),
            scratch=[pad, narrow],
            flops=8e8,
        )
        part, held = call(
            bind(rim_body, section),
            [whole, packed],
            near(after, *rims[::-1], select) + far(keys, facts, routes),
            scratch=[] if section == 2 else [pad],
        )
        if section < 2:
            arrived, payload = call(
                bind(flux_body, section),
                [((FEAT, FACES), F32, "v"), ((SLOTS, FEAT), F32, "v")],
                near(arrivals, held),
                scratch=[pad, wide, broad],
            )
    (result,) = call(
        last_body,
        [whole],
        near(arrivals, held, part) + far(keys) + near(select),
        scratch=[pad, wide, narrow],
    )
    return result


def solution(mesh):
    placed = (
        P(None, None, ("blk", "sub")),
        P(("blk", "sub")),
        P(None, ("blk", "sub")),
        P(None, ("blk", "sub")),
        P(None, ("blk", "sub")),
    )
    return jax.shard_map(
        per_device,
        mesh=mesh,
        in_specs=placed,
        out_specs=P(None, None, ("blk", "sub")),
        check_vma=False,
    )
```

```python
import jax
import jax.numpy as jnp
import numpy as np
from jax import lax
from jax.experimental import pallas as pl
from jax.experimental.pallas import tpu as pltpu
from jax.sharding import PartitionSpec as P

P_SIZE = 6
SUB = 16
IFD = 64
RIM = 32
NODES = 216
ELEMS = 256
FACES = 2 * IFD
SLOTS = 512
DEVICES = 128
TR = 40
PROJECT = 48
METRIC = 96
FACT_ROWS = 104
ROUTES = FACT_ROWS + 128
NEAR, RIM_OUT, RIM_IN, ROTOR, STATOR, SCALE, KEY_ROWS = 0, 6, 10, 14, 15, 16, 24
FEAT = 128
DT_STEP = 0.01
F32 = jnp.float32
BF16 = jnp.bfloat16
VMEM_BYTES = 24 * 1024 * 1024


def legendre_columns(points, npts):
    legendre = np.zeros((npts, npts))
    legendre[:, 0] = 1.0
    legendre[:, 1] = points
    for k in range(2, npts):
        legendre[:, k] = (
            (2 * k - 1) * points * legendre[:, k - 1] - (k - 1) * legendre[:, k - 2]
        ) / k
    return legendre


def basis_tables(npts):
    order = npts - 1
    points = -np.cos(np.pi * np.arange(npts) / order)
    for iteration in range(60):
        legendre = legendre_columns(points, npts)
        points = points - (points * legendre[:, order] - legendre[:, order - 1]) / (
            npts * legendre[:, order]
        )
    legendre = legendre_columns(points, npts)
    weights = 2.0 / (order * npts * legendre[:, order] ** 2)
    separation = points[:, None] - points[None, :] + np.eye(npts)
    derivative = legendre[:, order][:, None] / legendre[:, order][None, :] / separation
    derivative = derivative * (1.0 - np.eye(npts))
    derivative[0, 0] = -order * npts / 4.0
    derivative[order, order] = order * npts / 4.0
    return (points, weights, derivative)


POINTS, WEIGHTS, DERIVATIVE = basis_tables(P_SIZE)
LIFT = float(1.0 / WEIGHTS[0])
SECTIONS = (
    (0.0, 1.0, DT_STEP),
    (0.75, 0.25, 0.25 * DT_STEP),
    (1.0 / 3.0, 2.0 / 3.0, 2.0 / 3.0 * DT_STEP),
)


def face_rows():
    picks = np.zeros((6 * TR, NODES))
    for face in range(6):
        fixed = 0 if face % 2 == 0 else P_SIZE - 1
        for a in range(P_SIZE):
            for b in range(P_SIZE):
                place = [a, b]
                place.insert(face // 2, fixed)
                node = (place[0] * P_SIZE + place[1]) * P_SIZE + place[2]
                picks[face * TR + a * P_SIZE + b, node] = 1.0
    return picks


def derivative_pieces():
    one = np.eye(P_SIZE)
    square = np.eye(P_SIZE * P_SIZE)
    whole = [
        np.kron(DERIVATIVE, square),
        np.kron(one, np.kron(DERIVATIVE, one)),
        np.kron(square, DERIVATIVE),
    ]
    pieces = []
    for matrix in whole:
        matrix = matrix.astype(np.float32)
        high = matrix.astype(jnp.bfloat16)
        pieces.append(high)
        pieces.append((matrix - high.astype(np.float32)).astype(jnp.bfloat16))
    return np.stack(pieces)


def nn(a, b):
    return lax.dot_general(a, b, (((1,), (0,)), ((), ())), preferred_element_type=F32)


def nt(a, b):
    return lax.dot_general(a, b, (((1,), (1,)), ((), ())), preferred_element_type=F32)


def tn(a, b):
    return lax.dot_general(a, b, (((0,), (0,)), ((), ())), preferred_element_type=F32)


def halves(x):
    high = x.astype(BF16)
    return high, (x - high.astype(F32)).astype(BF16)


def stacked(x):
    return jnp.concatenate(halves(x), axis=0)


def fold(x):
    count = x.shape[0] // 2
    return x[:count, :] + x[count:, :]


def fold_lanes(x):
    count = x.shape[1] // 2
    return x[:, :count] + x[:, count:]


def nn2(exact, x):
    high, low = halves(x)
    return nn(exact, high) + nn(exact, low)


def mark(cond):
    return jnp.where(cond, 1.0, 0.0)


def iota(shape, dim):
    return lax.broadcasted_iota(jnp.int32, shape, dim)


def my_device():
    return lax.axis_index("blk") * 8 + lax.axis_index("sub")


def even_place(turn):
    return (lax.axis_index(("sub", "blk")[turn]) & 1) == 0


class Fetched:
    def __init__(self, copy, buffer):
        self.copy, self.buffer, self.here = copy, buffer, False

    def __getitem__(self, key):
        if not self.here:
            self.copy.wait()
            self.here = True
        return self.buffer[key]


def call(body, outs, args, scratch=(), flops=1e8, moved=2e6):
    far_in = [i for i, (_, space) in enumerate(args) if space == "h"]
    far_out = [i for i, (_, _, space) in enumerate(outs) if space == "h"]
    own = [pltpu.VMEM(args[i][0].shape, args[i][0].dtype) for i in far_in]
    own += [pltpu.VMEM(outs[i][0], outs[i][1]) for i in far_out]
    count = len(far_in) + len(far_out)

    def kernel(*refs):
        refs = list(refs)
        ins, refs = refs[: len(args)], refs[len(args) :]
        results, refs = refs[: len(outs)], refs[len(outs) :]
        extra, refs = refs[: len(scratch)], refs[len(scratch) :]
        sems = refs[-1] if count else None
        for n, i in enumerate(far_in):
            copy = pltpu.make_async_copy(ins[i], refs[n], sems.at[n])
            copy.start()
            ins[i] = Fetched(copy, refs[n])
        shown = list(results)
        for n, i in enumerate(far_out):
            shown[i] = refs[len(far_in) + n]
        body(*ins, *shown, *extra)
        for i in far_in:
            if not ins[i].here:
                ins[i].copy.wait()
        copies = []
        for n, i in enumerate(far_out):
            spot = len(far_in) + n
            copies.append(pltpu.make_async_copy(refs[spot], results[i], sems.at[spot]))
            copies[-1].start()
        for copy in copies:
            copy.wait()

    spaces = {"h": pltpu.HBM, "v": pltpu.VMEM, "r": pltpu.HBM}
    return pl.pallas_call(
        kernel,
        out_shape=[jax.ShapeDtypeStruct(o[0], o[1]) for o in outs],
        in_specs=[pl.BlockSpec(memory_space=spaces[space]) for _, space in args],
        out_specs=[pl.BlockSpec(memory_space=spaces[o[2]]) for o in outs],
        scratch_shapes=list(scratch)
        + own
        + ([pltpu.SemaphoreType.DMA((count,))] if count else []),
        compiler_params=pltpu.CompilerParams(vmem_limit_bytes=VMEM_BYTES),
        cost_estimate=pl.CostEstimate(
            flops=int(flops), bytes_accessed=int(moved), transcendentals=0
        ),
    )(*[array for array, _ in args])


def spread(values, pad, width):
    for group in range(3 * P_SIZE):
        c, i = divmod(group, P_SIZE)
        start = c * TR + i * P_SIZE
        pad[group, 0:P_SIZE, 0:width] = values[start : start + P_SIZE, :]


def to_mortars(facts, pad, out, comps, add):
    for half in range(2):
        lanes = slice(half * FACES, (half + 1) * FACES)
        for c in comps:
            for m in range(P_SIZE):
                total = facts[m : m + 1, lanes] * pad[c * P_SIZE, :, 0:FACES]
                for i in range(1, P_SIZE):
                    row = i * 8 + m
                    total += facts[row : row + 1, lanes] * pad[c * P_SIZE + i, :, 0:FACES]
                start = c * TR + m * P_SIZE
                rows = slice(start, start + P_SIZE)
                if add:
                    out[rows, lanes] += total[0:P_SIZE, :]
                else:
                    out[rows, lanes] = total[0:P_SIZE, :]


def outgoing(traces4, traces5):
    blank = jnp.zeros((FEAT - 3 * TR, ELEMS), F32)
    out4 = jnp.concatenate([traces4[0] - traces4[3], traces4[1], traces4[2], blank], axis=0)
    out5 = jnp.concatenate([traces5[0] + traces5[3], traces5[1], traces5[2], blank], axis=0)
    return out4, out5


def at_faces(rows4, rows5, members):
    rotor = fold(nt(stacked(rows5), members))
    stator = fold(nt(stacked(rows4), members))
    return jnp.where(iota((FEAT, FACES), 1) < IFD, rotor, stator)


def at_elements(values, members):
    rotor_side = iota((FEAT, FACES), 1) < IFD
    to5 = nn2b(jnp.where(rotor_side, values, 0.0), members)
    to4 = nn2b(jnp.where(rotor_side, 0.0, values), members)
    return to4, to5


def nn2b(x, exact):
    return fold(nn(stacked(x), exact))


def comp(rows, c):
    return rows[c * TR : (c + 1) * TR, :]


def partner_body(pairs, out):
    row = iota((DEVICES, ELEMS), 0)
    total = None
    for mine, other in ((0, 1), (1, 0)):
        entry = pairs[mine : mine + 1, :]
        partner = pairs[other : other + 1, :]
        owner_row = mark(row == (entry >> 2)).astype(BF16)
        spot = entry & 3
        facts = jnp.where(row == spot, (partner >> 2) + 1, 0) + jnp.where(
            row == spot + 4, partner & 3, 0
        )
        term = nt(owner_row, facts.astype(F32).astype(BF16))
        total = term if total is None else total + term
    out[...] = total


def picked(keys, row, count):
    return mark(iota((count, ELEMS), 0).astype(F32) == keys[row : row + 1, :]).astype(BF16)


def member_picks(keys):
    number = iota((FACES, ELEMS), 0).astype(F32)
    rotor = number == keys[ROTOR : ROTOR + 1, :]
    stator = number == keys[STATOR : STATOR + 1, :]
    return mark(rotor | stator).astype(BF16)


def tables_body(
    neighbours, sends, metric, fields, select,
    keys, facts, own, info, mortars,
    rows, pad,
):
    me = my_device()
    nb = neighbours[...]
    face_id = iota((6, ELEMS), 0)
    remote = (nb >= 0) & ((nb >> 8) != me)
    here = (nb >= 0) & ((nb >> 8) == me)
    spot = nb & 255
    flags = jnp.where(face_id < 4, mark(remote), mark(nb == -2))
    rows[...] = jnp.zeros(rows.shape, F32)
    rows[0, 0:6, :] = flags
    rows[1, 0:6, :] = spot.astype(F32)
    flag_rows = rows[0].astype(BF16)
    spot_rows = rows[1].astype(BF16)
    down = iota((ELEMS, ELEMS), 0)
    across = iota((ELEMS, ELEMS), 1)
    before = mark(down < across).astype(BF16)
    same = mark(down == across).astype(BF16)
    rank = nn(flag_rows, before)
    spot_down = jnp.where(nt(same, flag_rows) > 0.5, nt(same, spot_rows), 1e4)
    keys[...] = jnp.zeros(keys.shape, F32)
    keys[NEAR : NEAR + 6, :] = jnp.where(here, spot, -1).astype(F32)
    for face in range(4):
        live = flags[face : face + 1, :] > 0.5
        order = jnp.sum(
            mark(spot_down[:, face : face + 1] < rows[1, face : face + 1, :]),
            axis=0,
            keepdims=True,
        )
        place = RIM_OUT + face
        keys[place : place + 1, :] = jnp.where(live, rank[face : face + 1, :], -1.0)
        place = RIM_IN + face
        keys[place : place + 1, :] = jnp.where(live, order, -1.0)
    keys[ROTOR : ROTOR + 1, :] = jnp.where(flags[5:6, :] > 0.5, rank[5:6, :], -1.0)
    keys[STATOR : STATOR + 1, :] = jnp.where(flags[4:5, :] > 0.5, rank[4:5, :] + IFD, -1.0)
    keys[SCALE : SCALE + 1, :] = metric[...]
    member = member_picks(keys)
    face_of = sends[0:1, :]
    lo_of = sends[1:2, :]
    lane_of = jnp.where(face_of >= 0, face_of + jnp.where(lo_of > 0, FACES, 0), -1)
    slot_lane = mark(iota((2 * FACES, SLOTS), 0) == lane_of).astype(BF16)
    kind = iota((16, SLOTS), 0)
    number = iota((16, SLOTS), 1)
    lines = jnp.where(kind == 0, number >> 2, 0) + jnp.where(kind == 1, number & 3, 0)
    lines += jnp.where(kind == 2, lo_of, 0) + jnp.where(kind == 3, sends[2:3, :], 0)
    found = nt(lines.astype(F32).astype(BF16), slot_lane)
    info[...] = found
    lo = found[2:3, :]
    width = found[3:4, :] - lo
    point = iota((8, 2 * FACES), 0)
    unit = jnp.zeros((8, 2 * FACES), F32)
    weight = jnp.zeros((8, 2 * FACES), F32)
    for m in range(P_SIZE):
        unit = jnp.where(point == m, float((POINTS[m] + 1.0) * 0.5), unit)
        weight = jnp.where(point == m, float(0.5 * WEIGHTS[m] / SUB), weight)
    spots = (lo + width * unit) * (2.0 / SUB) - 1.0
    for i in range(P_SIZE):
        product = None
        for j in range(P_SIZE):
            if j != i:
                term = (spots - float(POINTS[j])) * float(1.0 / (POINTS[i] - POINTS[j]))
                product = term if product is None else product * term
        facts[i * 8 : i * 8 + 8, :] = product
        start = PROJECT + i * 8
        facts[start : start + 8, :] = product * weight * width * float(1.0 / WEIGHTS[i])
    for i in range(P_SIZE):
        for k in range(P_SIZE):
            start = PROJECT + i * 8
            term = facts[start : start + 8, :] * facts[k * 8 : k * 8 + 8, :]
            term = jnp.sum(term, axis=0, keepdims=True)
            own[i * 8 + k : i * 8 + k + 1, :] = term[:, 0:FACES] + term[:, FACES:]
    scale = jnp.broadcast_to(metric[...], (16, ELEMS))
    high, rest = scale.astype(BF16), scale - scale.astype(BF16).astype(F32)
    middle, low = halves(rest)
    scale = nt(high, member) + nt(middle, member) + nt(low, member)
    facts[METRIC:FACT_ROWS, :] = jnp.concatenate([scale[0:8, :]] * 2, axis=1)
    traces = [nn2(select[4 * TR : 6 * TR, :], fields[c]) for c in range(4)]
    out4, out5 = outgoing([t[:TR] for t in traces], [t[TR:] for t in traces])
    spread(at_faces(out4, out5, member), pad, FACES)
    mortars[...] = jnp.zeros((FEAT, 2 * FACES), F32)
    to_mortars(facts, pad, mortars, (0, 1, 2), False)


def slot_picks(row):
    return mark(iota((SLOTS, 2 * FACES), 0).astype(F32) == row).astype(BF16)


def send_rows(exact, values):
    return fold_lanes(nt(exact, stacked(values)))


def route_body(facts, info, mortars, routes, payload):
    owner = info[0:1, :]
    turn = info[1:2, :]
    owner_pick = mark(iota((DEVICES, 2 * FACES), 0).astype(F32) == owner).astype(BF16)
    found = tn(facts[...].astype(BF16), owner_pick)
    partner = jnp.zeros((1, 2 * FACES), F32)
    other = jnp.zeros((1, 2 * FACES), F32)
    for t in range(4):
        partner = jnp.where(turn == t, found[t : t + 1, :], partner)
        other = jnp.where(turn == t, found[4 + t : 5 + t, :], other)
    partner = partner - 1.0
    kind = iota((16, 2 * FACES), 0)
    lines = jnp.where(kind == 0, partner, 0.0) + jnp.where(kind == 1, owner, 0.0)
    lines += jnp.where(kind == 2, turn, 0.0) + jnp.where(kind == 3, other, 0.0)
    same = mark(iota((2 * FACES, 2 * FACES), 0) == iota((2 * FACES, 2 * FACES), 1)).astype(BF16)
    down = nt(same, lines.astype(BF16))
    partner_down = down[:, 0:1]
    together = partner_down == partner
    mine_down = down[:, 1:2] * 4.0 + down[:, 2:3]
    theirs_down = down[:, 1:2] * 4.0 + down[:, 3:4]
    mine = owner * 4.0 + turn
    theirs = owner * 4.0 + other
    ahead = jnp.sum(mark(together & (mine_down < mine)), axis=0, keepdims=True)
    behind = jnp.sum(mark(together & (theirs_down < theirs)), axis=0, keepdims=True)
    kind = iota((8, 2 * FACES), 0)
    routes[...] = partner * 4.0 + jnp.where(kind == 0, ahead, behind)
    payload[...] = send_rows(slot_picks(partner * 4.0 + ahead), mortars[...])


def placed(picks, x):
    high, low = halves(x)
    return tn(picks, high) + tn(picks, low)


def place_interface(part, arrived, keys, select):
    picks = select[4 * TR : 6 * TR, :]
    to4, to5 = at_elements(arrived[...], member_picks(keys))
    for c in range(4):
        source = (0, 1, 2, 0)[c]
        sign5 = -1.0 if c == 3 else 1.0
        stack = jnp.concatenate([comp(to4, source), sign5 * comp(to5, source)], axis=0)
        yield part[c] + placed(picks, stack)


def characteristics(traces, faces):
    blank = jnp.zeros((FEAT - 3 * TR, ELEMS), F32)
    leaving, inside = [], []
    for face in range(faces):
        sign = 1.0 if face % 2 else -1.0
        cut = [t[face * TR : (face + 1) * TR, :] for t in traces]
        along = face // 2
        tangent = [cut[1 + c] for c in range(3) if c != along]
        normal = sign * cut[1 + along]
        leaving.append(stacked(jnp.concatenate([cut[0] + normal] + tangent + [blank], axis=0)))
        inside.append(jnp.concatenate([cut[0] - normal] + tangent + [blank], axis=0))
    return leaving, inside


def edge_body(section, *refs):
    part, keys, select = refs[:3]
    if section == 0:
        fields = [part[c] for c in range(4)]
        rims = refs[3:]
    else:
        arrived, whole = refs[3:5]
        fields = list(place_interface(part, arrived, keys, select))
        rims = refs[5:]
        for c in range(4):
            whole[c] = fields[c]
    leaving, _ = characteristics([nn2(select[0 : 4 * TR, :], x) for x in fields], 4)
    parts = []
    for face in range(4):
        pick = picked(keys, RIM_OUT + face, RIM)
        parts.append(fold_lanes(nt(pick, leaving[face])))
    for turn, (down, up) in enumerate((parts[:2], parts[2:])):
        even = even_place(turn)
        rims[2 * turn][...] = jnp.where(even, up, down)
        rims[2 * turn + 1][...] = jnp.where(even, down, up)


def inner_body(section, *refs):
    whole, refs = refs[0], refs[1:]
    if section:
        first, refs = refs[0], refs[1:]
    select, derive, neighbours, keys, own, after, pad, mixed = refs
    keep, stay, rate = SECTIONS[section]
    fields = [whole[c] for c in range(4)]
    high, low = zip(*[halves(x) for x in fields])
    sel = select[...]
    traces = [nn(sel, high[c]) + nn(sel, low[c]) for c in range(4)]
    leaving, inside = characteristics(traces, 6)
    members = member_picks(keys)
    spread(at_faces(inside[4], inside[5], members), pad, FACES)
    mixed[...] = jnp.zeros(mixed.shape, F32)
    for c in range(3):
        for i in range(P_SIZE):
            total = own[i * 8 : i * 8 + 1, :] * pad[c * P_SIZE]
            for k in range(1, P_SIZE):
                row = i * 8 + k
                total += own[row : row + 1, :] * pad[c * P_SIZE + k]
            start = c * TR + i * P_SIZE
            mixed[start : start + P_SIZE, :] = -total[0:P_SIZE, :]
    to4, to5 = at_elements(mixed[...], members)
    terms = []
    for face in range(6):
        pick = picked(keys, NEAR + face, ELEMS)
        arriving = fold(nn(leaving[face ^ 1], pick))
        term = 0.5 * (arriving - inside[face])
        if face >= 4:
            term = jnp.where(neighbours[face : face + 1, :] == -2, 0.0, term)
            term = term + (to4, to5)[face - 4]
        terms.append(term)
    scale = keys[SCALE : SCALE + 1, :] * rate
    for c in range(4):
        pieces = []
        for face in range(6):
            along = face // 2
            if c == 0:
                pieces.append(comp(terms[face], 0))
            elif c == 1 + along:
                pieces.append((-1.0 if face % 2 else 1.0) * comp(terms[face], 0))
            else:
                tangents = [k for k in range(3) if k != along]
                pieces.append(comp(terms[face], 1 + tangents.index(c - 1)))
        surface = placed(sel, jnp.concatenate(pieces, axis=0))
        if c == 0:
            pairs = ((0, 1), (1, 2), (2, 3))
        else:
            pairs = ((c - 1, 0),)
        volume = None
        for direction, source in pairs:
            big, small = derive[2 * direction], derive[2 * direction + 1]
            term = nn(big, high[source]) + nn(big, low[source]) + nn(small, high[source])
            volume = term if volume is None else volume + term
        base = stay * fields[c]
        if keep:
            base = base + keep * first[c]
        after[c] = base + scale * (LIFT * surface - volume)


def rim_body(section, *refs):
    before, r3, r2, r1, r0, select, keys = refs[:7]
    last = section == 2
    if last:
        after = refs[7]
    else:
        facts, after = refs[7:9]
    scale = keys[SCALE : SCALE + 1, :] * (SECTIONS[section][2] * LIFT)
    terms = []
    terms = []
    got = []
    for turn, (one, two) in enumerate(((r0, r1), (r2, r3))):
        even = even_place(turn)
        got.append(jnp.where(even, two[...], one[...]))
        got.append(jnp.where(even, one[...], two[...]))
    for face, value in enumerate(got):
        high, low = halves(value)
        pick = picked(keys, RIM_IN + face, RIM)
        terms.append(0.5 * (tn(high, pick) + tn(low, pick)))
    fields = []
    for c in range(4):
        pieces = []
        for face in range(4):
            along = face // 2
            if c == 0:
                pieces.append(comp(terms[face], 0))
            elif c == 1 + along:
                pieces.append((-1.0 if face % 2 else 1.0) * comp(terms[face], 0))
            else:
                tangents = [k for k in range(3) if k != along]
                pieces.append(comp(terms[face], 1 + tangents.index(c - 1)))
        value = before[c] + scale * placed(select[0 : 4 * TR, :], jnp.concatenate(pieces, axis=0))
        after[c] = value
        fields.append(value)
    if not last:
        mortars, pad = refs[9:]
        traces = [nn2(select[4 * TR : 6 * TR, :], x) for x in fields]
        out4, out5 = outgoing([t[:TR] for t in traces], [t[TR:] for t in traces])
        spread(at_faces(out4, out5, member_picks(keys)), pad, FACES)
        mortars[...] = jnp.zeros((FEAT, 2 * FACES), F32)
        to_mortars(facts, pad, mortars, (0, 1, 2), False)


def arrive(section, arrivals, held, routes, pad, wide, out):
    both = jnp.concatenate(halves(arrivals[...]), axis=1)
    pick = slot_picks(routes[1:2, :])
    spread(fold(tn(both, pick)), wide, 2 * FACES)
    scale = held[METRIC : METRIC + 1, 0:FACES] * (SECTIONS[section][2] * LIFT)
    out[...] = jnp.zeros(out.shape, F32)
    for c in range(3):
        for i in range(P_SIZE):
            total = None
            for half in range(2):
                lanes = slice(half * FACES, (half + 1) * FACES)
                for m in range(P_SIZE):
                    row = PROJECT + i * 8 + m
                    term = held[row : row + 1, lanes] * wide[c * P_SIZE + m, :, lanes]
                    total = term if total is None else total + term
            total = total * scale
            pad[c * P_SIZE + i] = total
            start = c * TR + i * P_SIZE
            out[start : start + P_SIZE, :] = total[0:P_SIZE, :]


def flux_body(
    section, arrivals, facts, routes, mortars, arrived, payload, pad, wide, mixed
):
    arrive(section, arrivals, facts, routes, pad, wide, arrived)
    mixed[...] = mortars[...]
    to_mortars(facts, pad, mixed, (1, 2), True)
    payload[...] = send_rows(slot_picks(routes[0:1, :]), mixed[...])


def last_body(
    arrivals, facts, routes, part, keys, select, after, pad, wide, arrived, whole, sems
):
    arrive(2, arrivals, facts, routes, pad, wide, arrived)
    copies = []
    for c, value in enumerate(place_interface(part, arrived, keys, select)):
        whole[c] = value
        copies.append(pltpu.make_async_copy(whole.at[c], after.at[c], sems.at[c]))
        copies[-1].start()
    for copy in copies:
        copy.wait()


def exchange(rows, width):
    whole = rows.reshape(DEVICES, width, FEAT)
    moved = lax.all_to_all(whole, ("blk", "sub"), split_axis=0, concat_axis=0, tiled=True)
    return moved.reshape(DEVICES * width, FEAT)


def pass_rims(rims):
    arrived = []
    blks, subs = lax.axis_size("blk"), lax.axis_size("sub")
    for turn in range(4):
        pairs = []
        for blk in range(blks):
            for sub in range(subs):
                at, count = ((sub, subs), (blk, blks))[turn // 2]
                other = at + 1 if at % 2 == turn % 2 else at - 1
                there = [blk, sub]
                if 0 <= other < count:
                    there[1 - turn // 2] = other
                else:
                    there[turn // 2] ^= 1
                pairs.append((blk * subs + sub, there[0] * subs + there[1]))
        arrived.append(lax.ppermute(rims[turn], ("blk", "sub"), pairs))
    return arrived


def bind(body, section):
    def bound(*refs):
        body(section, *refs)

    return bound


def per_device(fields, metric, neighbours, mortar_sends, mortar_pairs):
    select = jnp.asarray(face_rows(), BF16)
    derive = jnp.asarray(derivative_pieces())
    metric = metric.reshape(1, ELEMS)
    whole = ((4, NODES, ELEMS), F32, "v")
    rim = ((RIM, FEAT), F32, "v")
    table = ((FACT_ROWS, 2 * FACES), F32, "v")
    pad = pltpu.VMEM((3 * P_SIZE, 8, FACES), F32)
    wide = pltpu.VMEM((3 * P_SIZE, 8, 2 * FACES), F32)
    narrow = pltpu.VMEM((FEAT, FACES), F32)
    broad = pltpu.VMEM((FEAT, 2 * FACES), F32)

    def far(*arrays):
        return tuple((array, "v") for array in arrays)

    def near(*arrays):
        return tuple((array, "v") for array in arrays)

    (owned,) = call(partner_body, [((DEVICES, FEAT), F32, "v")], near(mortar_pairs))
    owned = exchange(owned, 1)
    keys, facts, own, info, mortars = call(
        tables_body,
        [
            ((KEY_ROWS, ELEMS), F32, "v"),
            table,
            ((48, FACES), F32, "v"),
            ((16, 2 * FACES), F32, "v"),
            ((FEAT, 2 * FACES), F32, "v"),
        ],
        near(neighbours, mortar_sends, metric, fields, select),
        scratch=[pltpu.VMEM((2, 16, ELEMS), F32), pad],
    )
    routes, payload = call(
        route_body,
        [((8, 2 * FACES), F32, "v"), ((SLOTS, FEAT), F32, "v")],
        near(owned, info, mortars),
    )
    part, arrived = fields, None
    packed = ((ROUTES + 8, 2 * FACES), F32, "v")
    for section in range(3):
        arrivals = exchange(payload, 4)
        edge = near(part) + far(keys) + near(select)
        if section == 0:
            current = near(fields)
            rims = call(bind(edge_body, section), [rim] * 4, edge, flops=5e7)
        else:
            current, *rims = call(
                bind(edge_body, section), [whole] + [rim] * 4, edge + far(arrived), flops=5e7
            )
            current = near(current, fields)
        rims = pass_rims(rims)
        (after,) = call(
            bind(inner_body, section),
            [whole],
            current + near(select, derive, neighbours) + far(keys, own),
            scratch=[pad, narrow],
            flops=8e8,
        )
        given = near(after, *rims[::-1], select, keys)
        if section == 2:
            (part,) = call(bind(rim_body, section), [whole], given)
        else:
            part, mortars = call(
                bind(rim_body, section),
                [whole, ((FEAT, 2 * FACES), F32, "v")],
                given + near(facts),
                scratch=[pad],
            )
            arrived, payload = call(
                bind(flux_body, section),
                [((FEAT, FACES), F32, "v"), ((SLOTS, FEAT), F32, "v")],
                near(arrivals, facts, routes, mortars),
                scratch=[pad, wide, broad],
            )
    (result,) = call(
        last_body,
        [((4, NODES, ELEMS), F32, "r")],
        near(arrivals, facts, routes, part, keys, select),
        scratch=[
            pad, wide, narrow,
            pltpu.VMEM((4, NODES, ELEMS), F32), pltpu.SemaphoreType.DMA((4,)),
        ],
    )
    return result


def solution(mesh):
    placed = (
        P(None, None, ("blk", "sub")),
        P(("blk", "sub")),
        P(None, ("blk", "sub")),
        P(None, ("blk", "sub")),
        P(None, ("blk", "sub")),
    )
    return jax.shard_map(
        per_device,
        mesh=mesh,
        in_specs=placed,
        out_specs=P(None, None, ("blk", "sub")),
        check_vma=False,
    )
```
